32 devices in a mesh: ctx: 4 (over x, core), wshard: 8 (over z, y).
Axes of the slice: x: 2, y: 2, z: 4, core: 2. Of those that a mesh axis runs over, the one named last changes fastest.
Arguments:
- layer_input: float32 [8, 2048, 768], P('wshard', 'ctx'), may hold values from -6 to 6
- segments: int32 [8, 2048], P('wshard'), may hold values from 0 to 2, as said below
- global_blocks: int32 [8, 2], P('wshard'), may hold values from 0 to 31
- random_blocks: int32 [32, 12, 3], replicated, may hold values from 0 to 31
- thresholds: float32 [12], replicated, may hold values from 4 to 40
- w_query: float32 [768, 768], P(None, 'wshard'), may hold values from -0.3125 to 0.3125
- w_key: float32 [768, 768], P(None, 'wshard'), may hold values from -0.3125 to 0.3125
- w_value: float32 [768, 768], P(None, 'wshard'), may hold values from -0.21875 to 0.21875
- w_output: float32 [768, 768], P(None, 'wshard'), may hold values from -0.875 to 0.875
- w_inner: float32 [768, 3072], P(None, 'wshard'), may hold values from -0.21875 to 0.21875
- w_outer: float32 [3072, 768], P(None, 'wshard'), may hold values from -0.15625 to 0.15625
- query_bias: float32 [768], P('wshard'), may hold values from -3 to 3
- value_bias: float32 [768], P('wshard'), may hold values from -3 to 3
- output_bias: float32 [768], P('wshard'), may hold values from -3 to 3
- inner_bias: float32 [3072], P('wshard'), may hold values from -3 to 3
- outer_bias: float32 [768], P('wshard'), may hold values from -3 to 3
- gain_attn: float32 [768], P('wshard'), may hold values from 0.5 to 1.5
- shift_attn: float32 [768], P('wshard'), may hold values from -3 to 3
- gain_mlp: float32 [768], P('wshard'), may hold values from 0.5 to 1.5
- shift_mlp: float32 [768], P('wshard'), may hold values from -3 to 3
- out_grad: float32 [8, 2048, 768], P('wshard', 'ctx'), may hold values from -6 to 6
Outputs:
- layer_output: float32 [8, 2048, 768], P('wshard', 'ctx')
- input_grad: float32 [8, 2048, 768], P('wshard', 'ctx')
- grad_query: float32 [768, 768], P(None, 'wshard')
- grad_key: float32 [768, 768], P(None, 'wshard')
- grad_value: float32 [768, 768], P(None, 'wshard')
- grad_output: float32 [768, 768], P(None, 'wshard')
- grad_inner: float32 [768, 3072], P(None, 'wshard')
- grad_outer: float32 [3072, 768], P(None, 'wshard')
- grad_query_bias: float32 [768], P('wshard')
- grad_value_bias: float32 [768], P('wshard')
- grad_output_bias: float32 [768], P('wshard')
- grad_inner_bias: float32 [3072], P('wshard')
- grad_outer_bias: float32 [768], P('wshard')
- grad_attn_gain: float32 [768], P('wshard')
- grad_attn_shift: float32 [768], P('wshard')
- grad_mlp_gain: float32 [768], P('wshard')
- grad_mlp_shift: float32 [768], P('wshard')
- clipped_query: float32 [768, 768], P(None, 'wshard')
- clipped_key: float32 [768, 768], P(None, 'wshard')
- head_maxima: float32 [12], replicated
The draws below stay inside these ranges and needn't reach their ends.
Inputs may be any that keep to these rules, and one draw needn't show every extreme that they name: `segments`: each sequence holds three documents, numbered 0, 1, 2 in order: the first ends within the first 512 tokens, the last begins within the last 512 tokens; each has at least one token. `global_blocks`: two entries of a sequence may name the same block. `random_blocks`: shared by all sequences; entries may repeat or name neighbour or global blocks.
All inputs are finite; a program needn't handle non-finite values.
Results may differ from the reference program's by a relative error of at most 0.02.
The reference program's roundings to bfloat16 on the way count: a program that leaves them out, or rounds other values in their place, can miss the bound.
Values may be sent and summed in bfloat16 or wider, within the bound.
No kernel may reach another device: no remote copies, remote signals or barrier semaphores. Data moves between devices by JAX's collectives and lax.ppermute only.
A program may use at most 320 MiB of HBM per device.

```python
import math
import jax
import jax.numpy as jnp
from jax import lax

D = 768
H = 12
DH = 64
FF = 3072
BLK = 64
NG = 2
NR = 3
TOK_DEV = 512
LEN = 2048
SEQS = 8
NB = 32


def draw_segments(key, part):
    key = jax.random.fold_in(key, 7)
    first_key, last_key = jax.random.split(key)
    first_cut = jax.random.randint(first_key, (SEQS, 1), 1, TOK_DEV)
    last_cut = LEN - jax.random.randint(last_key, (SEQS, 1), 1, TOK_DEV)
    positions = jnp.arange(LEN, dtype=jnp.int32)[None, :]
    return ((positions >= first_cut).astype(jnp.int32) + (positions >= last_cut).astype(jnp.int32)).astype(jnp.int32)


def place_ends(entries, rng, least, largest):
    extent = entries.shape
    spot = [jax.random.randint(jax.random.fold_in(rng, axis), (), 0, extent[axis]) for axis in range(len(extent))]
    entries = entries.at[tuple(spot)].set(least)
    longest = extent.index(max(extent))
    spot[longest] = (spot[longest] + 1) % extent[longest]
    return entries.at[tuple(spot)].set(largest)


def levels(key, shape, shards, low, high):
    def one(position, shards_of):
        steps = jax.random.uniform(jax.random.fold_in(jax.random.fold_in(key, 6), position), (shards_of,), jnp.float32, low / len(shards), high / len(shards))
        return jnp.repeat(jnp.exp(steps), shape[position] // shards_of).reshape((-1,) + (1,) * (len(shape) - position - 1))

    level = one(*shards[0])
    for cut in shards[1:]:
        level = level * one(*cut)
    return level


def scatter_about(own_key, shape, scale, most, shards=(), kind=jnp.bfloat16):
    array = jax.random.normal(own_key, shape, jnp.float32) * scale
    if len(shards) > 0:
        array = levels(own_key, shape, shards, -0.22, 0.18) * array
    return jnp.clip(array, min=-most, max=most).astype(kind)


def setup_inputs(seed: int = 0) -> dict:
    arg_keys = jax.random.split(jax.random.key(seed), 22)
    return {
        "layer_input": scatter_about(arg_keys[0], (SEQS, LEN, D), 1.0, 6.0, ((0, 8), (1, 4)), jnp.float32),
        "segments": draw_segments(jax.random.fold_in(arg_keys[21], 71), 0),
        "global_blocks": place_ends(jax.random.randint(arg_keys[2], (SEQS, NG), 0, NB), jax.random.fold_in(arg_keys[2], 1), 0, NB - 1).astype(jnp.int32),
        "random_blocks": place_ends(jax.random.randint(arg_keys[3], (NB, H, NR), 0, NB), jax.random.fold_in(arg_keys[3], 1), 0, NB - 1).astype(jnp.int32),
        "thresholds": jnp.clip(jnp.exp(jax.random.uniform(arg_keys[4], (H,), jnp.float32, math.log(4.0), math.log(40.0))), 4.0, 40.0),
        "w_query": scatter_about(arg_keys[5], (D, D), (D // 2) ** -0.5, 0.3125, ((1, 8),), jnp.float32),
        "w_key": scatter_about(arg_keys[6], (D, D), (D // 2) ** -0.5, 0.3125, ((1, 8),), jnp.float32),
        "w_value": scatter_about(arg_keys[7], (D, D), D ** -0.5, 0.21875, ((1, 8),), jnp.float32),
        "w_output": scatter_about(arg_keys[8], (D, D), (D // 16) ** -0.5, 0.875, ((1, 8),), jnp.float32),
        "w_inner": scatter_about(arg_keys[9], (D, FF), D ** -0.5, 0.21875, ((1, 8),), jnp.float32),
        "w_outer": scatter_about(arg_keys[10], (FF, D), (FF // 2) ** -0.5, 0.15625, ((1, 8),), jnp.float32),
        "query_bias": scatter_about(arg_keys[11], (D,), 0.5, 3.0, ((0, 8),), jnp.float32),
        "value_bias": scatter_about(arg_keys[12], (D,), 0.5, 3.0, ((0, 8),), jnp.float32),
        "output_bias": scatter_about(arg_keys[13], (D,), 0.5, 3.0, ((0, 8),), jnp.float32),
        "inner_bias": scatter_about(arg_keys[14], (FF,), 0.5, 3.0, ((0, 8),), jnp.float32),
        "outer_bias": scatter_about(arg_keys[15], (D,), 0.5, 3.0, ((0, 8),), jnp.float32),
        "gain_attn": jnp.clip(1.0 + 0.1 * jax.random.normal(arg_keys[16], (D,), jnp.float32), 0.5, 1.5),
        "shift_attn": scatter_about(arg_keys[17], (D,), 0.5, 3.0, ((0, 8),), jnp.float32),
        "gain_mlp": jnp.clip(1.0 + 0.1 * jax.random.normal(arg_keys[18], (D,), jnp.float32), 0.5, 1.5),
        "shift_mlp": scatter_about(arg_keys[19], (D,), 0.5, 3.0, ((0, 8),), jnp.float32),
        "out_grad": scatter_about(arg_keys[20], (SEQS, LEN, D), 1.0, 6.0, ((0, 8), (1, 4)), jnp.float32),
    }


EPSILON = 1e-05
HIGH = lax.Precision.HIGHEST

@jax.custom_vjp
def low(v):
    return lax.optimization_barrier(v.astype(jnp.bfloat16)).astype(jnp.float32)

@jax.custom_vjp
def low_back(v):
    return v

def low_keep(v):
    return (low(v), None)

def low_pass(kept, grad):
    return (grad,)

def back_keep(v):
    return (v, None)

def back_low(kept, grad):
    return (low(grad),)
low.defvjp(low_keep, low_pass)
low_back.defvjp(back_keep, back_low)

def product(left, right):
    return jnp.einsum('td,de->te', left, right, precision=HIGH)

def layer_norm(values, gain, shift):
    centre = values - lax.optimization_barrier(jnp.mean(values, axis=-1, keepdims=True))
    inverse = lax.rsqrt(lax.optimization_barrier(jnp.mean(centre * centre, axis=-1, keepdims=True)) + EPSILON)
    return centre * inverse * gain + shift

def block_lists(first, row_blocks, nblocks, global_pos, random_rows, heads):
    blocks = first + jnp.arange(row_blocks, dtype=jnp.int32)
    offsets = jnp.arange(-1, 2, dtype=jnp.int32)
    slide = jnp.clip(blocks[:, None] + offsets[None, :], 0, nblocks - 1).astype(jnp.int32)
    slide = jnp.broadcast_to(slide[:, None, :], (row_blocks, heads, 3))
    glob = jnp.broadcast_to(global_pos[None, None, :], (row_blocks, heads, global_pos.shape[0])).astype(jnp.int32)
    lists = jnp.concatenate([slide, glob, random_rows.astype(jnp.int32)], axis=2)
    slots = lists.shape[2]
    equal = lists[..., :, None] == lists[..., None, :]
    earlier = jnp.arange(slots)[:, None] < jnp.arange(slots)[None, :]
    active = jnp.logical_not(jnp.any(equal & earlier[None, None], axis=-2))
    return (blocks, lists, active)

def attend_sequence(query, key, value, seg, global_pos, random_rows):
    nblocks = LEN // BLK
    query_heads = query.reshape(nblocks, BLK, H, DH)
    key_heads = key.reshape(nblocks, BLK, H, DH)
    value_heads = value.reshape(nblocks, BLK, H, DH)
    seg_blocks = seg.reshape(nblocks, BLK)
    blocks, lists, active = block_lists(0, nblocks, nblocks, global_pos, random_rows, H)
    head_ids = jnp.arange(H)[:, None]

    def sparse_block(items):
        rows, row_list, row_active, row_seg = items
        keys = key_heads[row_list, :, head_ids].reshape(H, -1, DH)
        values = value_heads[row_list, :, head_ids].reshape(H, -1, DH)
        key_seg = seg_blocks[row_list].reshape(H, -1)
        mask = jnp.repeat(row_active, BLK, axis=1)[:, None, :] & (row_seg[None, :, None] == key_seg[:, None, :])
        raw = low_back(jnp.einsum('ahd,hkd->hak', rows, keys, precision=HIGH) * 0.125)
        scores = jnp.where(mask, raw, -jnp.inf)
        probs = low(jax.nn.softmax(scores, axis=-1))
        return (jnp.einsum('hak,hkd->ahd', probs, values, precision=HIGH), lax.optimization_barrier(jnp.max(scores, axis=(1, 2))))
    sparse_out, sparse_peak = lax.map(jax.checkpoint(sparse_block), (query_heads, lists, active, seg_blocks))
    keys_flat = key.reshape(LEN, H, DH)
    values_flat = value.reshape(LEN, H, DH)

    def full_block(place):
        rows = query_heads[place]
        row_seg = seg_blocks[place]
        raw = low_back(jnp.einsum('ahd,khd->hak', rows, keys_flat, precision=HIGH) * 0.125)
        mask = row_seg[None, :, None] == seg[None, None, :]
        scores = jnp.where(mask, raw, -jnp.inf)
        probs = low(jax.nn.softmax(scores, axis=-1))
        return (jnp.einsum('hak,khd->ahd', probs, values_flat, precision=HIGH), lax.optimization_barrier(jnp.max(scores, axis=(1, 2))))
    out = sparse_out
    is_global = jnp.zeros((nblocks,), dtype=bool)
    peak = jnp.full((H,), -jnp.inf, dtype=jnp.float32)
    for number in range(NG - 1, -1, -1):
        rows_out, rows_peak = jax.checkpoint(full_block)(global_pos[number])
        here = blocks == global_pos[number]
        out = jnp.where(here[:, None, None, None], rows_out[None], out)
        is_global = is_global | here
        peak = jnp.maximum(peak, rows_peak)
    peak = jnp.maximum(peak, lax.optimization_barrier(jnp.max(jnp.where(is_global[:, None], -jnp.inf, sparse_peak), axis=0)))
    return (out.reshape(LEN, H * DH), peak)

def forward(layer_input, w_query, w_key, w_value, w_output, w_inner, w_outer, query_bias, value_bias, output_bias, inner_bias, outer_bias, gain_attn, shift_attn, gain_mlp, shift_mlp, segments, global_blocks, random_blocks):
    seqs, length, width = layer_input.shape
    tokens = layer_input.reshape(seqs * length, width)
    inputs_low = low(tokens)
    query = low(low_back(product(inputs_low, low(w_query)) + low(query_bias)))
    key = low(low_back(product(inputs_low, low(w_key))))
    value = low(low_back(product(inputs_low, low(w_value)) + low(value_bias)))
    attended, peaks = jax.vmap(attend_sequence, in_axes=(0, 0, 0, 0, 0, None))(query.reshape(seqs, length, width), key.reshape(seqs, length, width), value.reshape(seqs, length, width), segments, global_blocks, random_blocks)
    maxima = lax.optimization_barrier(jnp.max(peaks, axis=0))
    attn_low = low(low_back(attended.reshape(seqs * length, width)))
    mixed = low_back(product(attn_low, low(w_output)) + low(output_bias))
    hidden = layer_norm(tokens + mixed, low(gain_attn), low(shift_attn))
    inner = low_back(product(low(hidden), low(w_inner)) + low(inner_bias))
    outer = low_back(product(low(jax.nn.gelu(inner, approximate=True)), low(w_outer)) + low(outer_bias))
    result = layer_norm(hidden + outer, low(gain_mlp), low(shift_mlp))
    return (result.reshape(seqs, length, width), maxima)

def reference(layer_input, segments, global_blocks, random_blocks, thresholds, w_query, w_key, w_value, w_output, w_inner, w_outer, query_bias, value_bias, output_bias, inner_bias, outer_bias, gain_attn, shift_attn, gain_mlp, shift_mlp, out_grad):
    primals = (layer_input, w_query, w_key, w_value, w_output, w_inner, w_outer, query_bias, value_bias, output_bias, inner_bias, outer_bias, gain_attn, shift_attn, gain_mlp, shift_mlp)

    def run(*values):
        return forward(*values, segments, global_blocks, random_blocks)
    result, pull, maxima = jax.vjp(run, *primals, has_aux=True)
    grads = pull(out_grad)
    factor = thresholds / jnp.maximum(maxima, thresholds)
    scale = jnp.repeat(jnp.sqrt(factor), DH)
    return (result, grads[0], grads[1], grads[2], grads[3], grads[4], grads[5], grads[6], grads[7], grads[8], grads[9], grads[10], grads[11], grads[12], grads[13], grads[14], grads[15], w_query * scale[None, :], w_key * scale[None, :], maxima)
```

```python
import functools

import jax
import jax.numpy as jnp
from jax import lax
from jax.experimental import pallas as pl
from jax.experimental.pallas import tpu as pltpu
from jax.sharding import PartitionSpec as P

BLK = 64
EPSILON = 1e-05
NEG = -1e30
UNROLL = 4
LOW = jnp.bfloat16
F32 = jnp.float32


def dot_nn(left, right):
    return lax.dot_general(left, right, (((1,), (0,)), ((), ())), preferred_element_type=F32)


def dot_tn(left, right):
    return lax.dot_general(left, right, (((0,), (0,)), ((), ())), preferred_element_type=F32)


def dot_nt(left, right):
    return lax.dot_general(left, right, (((1,), (1,)), ((), ())), preferred_element_type=F32)


def norm_forward(values, gain, shift):
    centre = values - jnp.mean(values, axis=-1, keepdims=True)
    inverse = lax.rsqrt(jnp.mean(centre * centre, axis=-1, keepdims=True) + EPSILON)
    normed = centre * inverse
    return (normed * gain + shift, normed, inverse)


def norm_backward(upstream, normed, inverse, gain):
    scaled = upstream * gain
    mean_one = jnp.mean(scaled, axis=-1, keepdims=True)
    mean_two = jnp.mean(scaled * normed, axis=-1, keepdims=True)
    result = inverse * (scaled - mean_one - normed * mean_two)
    return (result, jnp.sum(upstream * normed, axis=0), jnp.sum(upstream, axis=0))


def gelu_and_slope(v):
    c = 0.7978845608028654
    t = jnp.tanh(c * (v + 0.044715 * v * v * v))
    half = 0.5 * (1.0 + t)
    slope = half + 0.5 * v * (1.0 - t * t) * (c * (1.0 + 3 * 0.044715 * v * v))
    return v * half, slope


def halves():
    lane = lax.broadcasted_iota(jnp.int32, (BLK, 2 * BLK), 1)
    return lane < BLK


def stack_pair(tile):
    low = jnp.where(halves(), 1.0, 0.0).astype(tile.dtype)
    high = jnp.where(halves(), 0.0, 1.0).astype(tile.dtype)
    return jnp.concatenate([tile * low, tile * high], axis=0)


def unstack_pair(rows):
    return jnp.where(halves(), rows[:BLK], rows[BLK:])


def rows_of(ref, block, count=1):
    return ref[pl.ds(pl.multiple_of(block * BLK, BLK), count * BLK), :]


def shared_rows(ref, index, base):
    return jnp.concatenate([rows_of(ref, index[base], 3), rows_of(ref, index[base + 3])], axis=0)


def own_rows(ref, index, base):
    return jnp.concatenate([rows_of(ref, index[base + j]) for j in range(4, 8)], axis=0)


def attend_kernel(index, active, flags, q_ref, k_ref, v_ref, seg_q, seg_k, seg_row, o_ref, p_ref, og_ref, pg_ref, top_ref, score, *, heads):
    pair = pl.program_id(0)
    step = pl.program_id(1)
    wide = lax.broadcasted_iota(jnp.int32, (1, 2 * BLK), 1) < BLK
    length = k_ref.shape[0]

    @pl.when(step == 0)
    def _():
        top_ref[...] = jnp.full(top_ref.shape, NEG, F32)

        @pl.when(flags[1] == 0)
        def _():
            og_ref[...] = jnp.zeros(og_ref.shape, og_ref.dtype)
            pg_ref[...] = jnp.zeros(pg_ref.shape, pg_ref.dtype)

        @pl.when(flags[1] != 0)
        def _():
            place = flags[0]
            q2 = stack_pair(rows_of(q_ref, place))
            sq = rows_of(seg_q, place)
            sq = jnp.concatenate([sq, sq], axis=0)
            top = jnp.full((2 * BLK, 1), NEG, F32)
            cut = 512
            for j in range(length // cut):
                raw = dot_nt(q2, k_ref[j * cut : (j + 1) * cut, :])
                raw = jnp.where(seg_row[:, j * cut : (j + 1) * cut] == sq, raw, NEG)
                score[:, j * cut : (j + 1) * cut] = raw
                top = jnp.maximum(top, jnp.max(raw, axis=1, keepdims=True))
            total = jnp.zeros((2 * BLK, 1), F32)
            for j in range(length // cut):
                power = jnp.exp(score[:, j * cut : (j + 1) * cut] - top)
                score[:, j * cut : (j + 1) * cut] = power
                total = total + jnp.sum(power, axis=1, keepdims=True)
            scale = 1.0 / total
            acc = jnp.zeros((2 * BLK, 2 * BLK), F32)
            for j in range(length // cut):
                prob = (score[:, j * cut : (j + 1) * cut] * scale).astype(LOW)
                pg_ref[0, :, j * cut : (j + 1) * cut] = prob
                acc = acc + dot_nn(prob, v_ref[j * cut : (j + 1) * cut, :])
            og_ref[...] = unstack_pair(acc).astype(LOW)
            top_ref[0] = jnp.maximum(top_ref[0], jnp.broadcast_to(top, top_ref.shape[1:]))

    for u in range(UNROLL):
        b = step * UNROLL + u
        place = flags[2] + b
        q2 = stack_pair(rows_of(q_ref, place))
        sq = rows_of(seg_q, place)
        sq = jnp.concatenate([sq, sq], axis=0)
        base = (b * heads + 2 * pair) * 8
        shared = dot_nt(q2, shared_rows(k_ref, index, base))
        own = jnp.concatenate(
            [dot_nt(q2[h * BLK : (h + 1) * BLK], own_rows(k_ref, index, base + 8 * h)) for h in range(2)],
            axis=0,
        )

        def seg_of(at, j):
            first = seg_k[pl.ds(active[at + j], 1), :]
            second = seg_k[pl.ds(active[at + j + 1], 1), :]
            return jnp.where(wide, first, second)

        raw_s = jnp.where(jnp.concatenate([seg_of(base, 0), seg_of(base, 2)], axis=1) == sq, shared, NEG)
        seg_own = [
            jnp.broadcast_to(
                jnp.concatenate([seg_of(base + 8 * h, 4), seg_of(base + 8 * h, 6)], axis=1), (BLK, 4 * BLK)
            )
            for h in range(2)
        ]
        raw_o = jnp.where(jnp.concatenate(seg_own, axis=0) == sq, own, NEG)
        top = jnp.maximum(jnp.max(raw_s, axis=1, keepdims=True), jnp.max(raw_o, axis=1, keepdims=True))
        power_s = jnp.exp(raw_s - top)
        power_o = jnp.exp(raw_o - top)
        scale = 1.0 / (jnp.sum(power_s, axis=1, keepdims=True) + jnp.sum(power_o, axis=1, keepdims=True))
        prob_s = (power_s * scale).astype(LOW)
        prob_o = (power_o * scale).astype(LOW)
        p_ref[0, u, :, : 4 * BLK] = prob_s
        p_ref[0, u, :, 4 * BLK :] = prob_o
        out = dot_nn(prob_s, shared_rows(v_ref, index, base))
        out = out + jnp.concatenate(
            [
                dot_nn(prob_o[h * BLK : (h + 1) * BLK], own_rows(v_ref, index, base + 8 * h))
                for h in range(2)
            ],
            axis=0,
        )
        o_ref[u * BLK : (u + 1) * BLK, :] = unstack_pair(out).astype(LOW)
        used = jnp.where(flags[3 + b] != 0, jnp.full_like(top, NEG), top)
        top_ref[0] = jnp.maximum(top_ref[0], jnp.broadcast_to(used, top_ref.shape[1:]))


def pull_kernel(index, active, flags, q_ref, k_ref, v_ref, do_ref, dog_ref, p_ref, pg_ref, dq_ref, dk_ref, dv_ref, dk, dv, score, *, heads):
    del active
    pair = pl.program_id(0)
    step = pl.program_id(1)
    steps = pl.num_programs(1)
    length = k_ref.shape[0]

    @pl.when(step == 0)
    def _():
        dk[...] = jnp.zeros(dk.shape, F32)
        dv[...] = jnp.zeros(dv.shape, F32)
        dq_ref[...] = jnp.zeros(dq_ref.shape, dq_ref.dtype)

    def add(ref, block, value):
        at = pl.ds(pl.multiple_of(block * BLK, BLK), value.shape[0])
        ref[at, :] += value

    for u in range(UNROLL):
        b = step * UNROLL + u
        place = flags[2] + b
        q2 = stack_pair(rows_of(q_ref, place))
        keep = jnp.where(flags[3 + b] != 0, 0.0, 1.0).astype(LOW)
        do2 = stack_pair(do_ref[u * BLK : (u + 1) * BLK, :] * keep)
        base = (b * heads + 2 * pair) * 8
        ks = shared_rows(k_ref, index, base)
        ko = [own_rows(k_ref, index, base + 8 * h) for h in range(2)]
        vs = shared_rows(v_ref, index, base)
        vo = [own_rows(v_ref, index, base + 8 * h) for h in range(2)]
        prob_s = p_ref[0, u, :, : 4 * BLK]
        prob_o = p_ref[0, u, :, 4 * BLK :]
        dp_s = dot_nt(do2, vs)
        dp_o = jnp.concatenate([dot_nt(do2[h * BLK : (h + 1) * BLK], vo[h]) for h in range(2)], axis=0)
        ps = prob_s.astype(F32)
        po = prob_o.astype(F32)
        ts = ps * dp_s
        to = po * dp_o
        total = jnp.sum(ts, axis=1, keepdims=True) + jnp.sum(to, axis=1, keepdims=True)
        ds_s = (ts - ps * total).astype(LOW)
        ds_o = (to - po * total).astype(LOW)
        dq = dot_nn(ds_s, ks) + jnp.concatenate(
            [dot_nn(ds_o[h * BLK : (h + 1) * BLK], ko[h]) for h in range(2)], axis=0
        )
        at = pl.ds(pl.multiple_of(place * BLK, BLK), BLK)
        dq_ref[at, :] = (unstack_pair(dq) * 0.125).astype(LOW)
        dks = dot_tn(ds_s, q2)
        dvs = dot_tn(prob_s, do2)
        add(dk, index[base], dks[: 3 * BLK])
        add(dk, index[base + 3], dks[3 * BLK :])
        add(dv, index[base], dvs[: 3 * BLK])
        add(dv, index[base + 3], dvs[3 * BLK :])
        for h in range(2):
            part = slice(h * BLK, (h + 1) * BLK)
            dko = dot_tn(ds_o[part], q2[part])
            dvo = dot_tn(prob_o[part], do2[part])
            for j in range(4):
                add(dk, index[base + 8 * h + 4 + j], dko[j * BLK : (j + 1) * BLK])
                add(dv, index[base + 8 * h + 4 + j], dvo[j * BLK : (j + 1) * BLK])

    @pl.when((step == steps - 1) & (flags[1] != 0))
    def _():
        place = flags[0]
        q2 = stack_pair(rows_of(q_ref, place))
        do2 = stack_pair(dog_ref[...])
        cut = 512
        total = jnp.zeros((2 * BLK, 1), F32)
        for j in range(length // cut):
            part = slice(j * cut, (j + 1) * cut)
            dp = dot_nt(do2, v_ref[part, :])
            score[:, part] = dp
            total = total + jnp.sum(pg_ref[0, :, part].astype(F32) * dp, axis=1, keepdims=True)
        acc = jnp.zeros((2 * BLK, 2 * BLK), F32)
        for j in range(length // cut):
            part = slice(j * cut, (j + 1) * cut)
            prob = pg_ref[0, :, part]
            ds = (prob.astype(F32) * (score[:, part] - total)).astype(LOW)
            acc = acc + dot_nn(ds, k_ref[part, :])
            dk[part, :] += dot_tn(ds, q2)
            dv[part, :] += dot_tn(prob, do2)
        at = pl.ds(pl.multiple_of(place * BLK, BLK), BLK)
        dq_ref[at, :] = (unstack_pair(acc) * 0.125).astype(LOW)

    @pl.when(step == steps - 1)
    def _():
        dk_ref[...] = dk[...].astype(LOW)
        dv_ref[...] = dv[...].astype(LOW)


def attend(index, active, flags, query, key, value, seg_col, seg_rep, seg_row, blocks, heads):
    length, width = key.shape
    pairs = width // (2 * BLK)
    steps = blocks // UNROLL
    column = pl.BlockSpec((length, 2 * BLK), lambda p, s, *_: (0, p))
    whole = lambda shape: pl.BlockSpec(shape, lambda p, s, *_: (0,) * len(shape))
    grid = pltpu.PrefetchScalarGridSpec(
        num_scalar_prefetch=3,
        grid=(pairs, steps),
        in_specs=[column, column, column, whole(seg_col.shape), whole(seg_rep.shape), whole(seg_row.shape)],
        out_specs=[
            pl.BlockSpec((UNROLL * BLK, 2 * BLK), lambda p, s, *_: (s, p)),
            pl.BlockSpec((1, UNROLL, 2 * BLK, 8 * BLK), lambda p, s, *_: (p, s, 0, 0)),
            pl.BlockSpec((BLK, 2 * BLK), lambda p, s, *_: (0, p)),
            pl.BlockSpec((1, 2 * BLK, length), lambda p, s, *_: (p, 0, 0)),
            pl.BlockSpec((1, 2 * BLK, 2 * BLK), lambda p, s, *_: (p, 0, 0)),
        ],
        scratch_shapes=[pltpu.VMEM((2 * BLK, length), F32)],
    )
    work = pairs * (blocks * 8 + length // BLK) * 2 * BLK * BLK
    return pl.pallas_call(
        functools.partial(attend_kernel, heads=heads),
        grid_spec=grid,
        out_shape=[
            jax.ShapeDtypeStruct((blocks * BLK, width), LOW),
            jax.ShapeDtypeStruct((pairs, blocks, 2 * BLK, 8 * BLK), LOW),
            jax.ShapeDtypeStruct((BLK, width), LOW),
            jax.ShapeDtypeStruct((pairs, 2 * BLK, length), LOW),
            jax.ShapeDtypeStruct((pairs, 2 * BLK, 2 * BLK), F32),
        ],
        compiler_params=pltpu.CompilerParams(vmem_limit_bytes=48 << 20),
        cost_estimate=pl.CostEstimate(flops=work * 512 * 4, bytes_accessed=20 << 20, transcendentals=work),
        name="attend",
    )(index, active, flags, query, key, value, seg_col, seg_rep, seg_row)


def pull(index, active, flags, query, key, value, grad, grad_glob, probs, probs_glob, heads):
    length, width = key.shape
    blocks = grad.shape[0] // BLK
    pairs = width // (2 * BLK)
    steps = blocks // UNROLL
    column = pl.BlockSpec((length, 2 * BLK), lambda p, s, *_: (0, p))
    grid = pltpu.PrefetchScalarGridSpec(
        num_scalar_prefetch=3,
        grid=(pairs, steps),
        in_specs=[
            column,
            column,
            column,
            pl.BlockSpec((UNROLL * BLK, 2 * BLK), lambda p, s, *_: (s, p)),
            pl.BlockSpec((BLK, 2 * BLK), lambda p, s, *_: (0, p)),
            pl.BlockSpec((1, UNROLL, 2 * BLK, 8 * BLK), lambda p, s, *_: (p, s, 0, 0)),
            pl.BlockSpec((1, 2 * BLK, length), lambda p, s, *_: (p, 0, 0)),
        ],
        out_specs=[column, column, column],
        scratch_shapes=[
            pltpu.VMEM((length, 2 * BLK), F32),
            pltpu.VMEM((length, 2 * BLK), F32),
            pltpu.VMEM((2 * BLK, length), F32),
        ],
    )
    work = pairs * (blocks * 8 + length // BLK) * 2 * BLK * BLK
    return pl.pallas_call(
        functools.partial(pull_kernel, heads=heads),
        grid_spec=grid,
        out_shape=[jax.ShapeDtypeStruct((length, width), LOW)] * 3,
        compiler_params=pltpu.CompilerParams(vmem_limit_bytes=48 << 20),
        cost_estimate=pl.CostEstimate(flops=work * 512 * 8, bytes_accessed=24 << 20, transcendentals=0),
        name="pull",
    )(index, active, flags, query, key, value, grad, grad_glob, probs, probs_glob)


class Moves:
    def __init__(self, ctx, wshard):
        self.ctx, self.wshard, self.chips = ctx, wshard, ctx // 2
        self.order = list(range(0, wshard, 2)) + list(range(wshard - 1, 0, -2))
        places = [self.order.index(i) for i in range(wshard)]
        self.up_perm = [(self.order[i], self.order[(i + 1) % wshard]) for i in range(wshard)]
        self.down_perm = [(b, a) for a, b in self.up_perm]
        self.shard = lax.axis_index("wshard")
        self.place = jnp.asarray(places, jnp.int32)[self.shard]
        self.table = jnp.asarray(self.order, jnp.int32)
        here = lax.axis_index("ctx")
        self.core, self.chip = here % 2, here // 2

    def up(self, value):
        return lax.ppermute(value, "wshard", self.up_perm)

    def down(self, value):
        return lax.ppermute(value, "wshard", self.down_perm)

    def swap(self, value):
        return lax.ppermute(value, "ctx", [(c, c ^ 1) for c in range(self.ctx)])

    def chip_shift(self, value, j):
        return lax.ppermute(value, "ctx", [(c, (c + 2 * j) % self.ctx) for c in range(self.ctx)])

    def chip_flip(self, value, bit):
        return lax.ppermute(value, "ctx", [(c, c ^ (2 * bit)) for c in range(self.ctx)])

    def shard_at(self, delta):
        return self.table[(self.place + delta) % self.wshard]

    def gather(self, piece):
        rows = piece.shape[0]
        half = self.wshard // 2
        whole = jnp.zeros((self.wshard * rows,) + piece.shape[1:], piece.dtype)

        def put(whole, part, delta, offset=0):
            return lax.dynamic_update_slice_in_dim(whole, part, self.shard_at(delta) * rows + offset, 0)

        whole = put(whole, piece, 0)
        above = below = piece
        for step in range(1, half):
            above, below = self.up(above), self.down(below)
            whole = put(put(whole, above, -step), below, step)
        cut = (rows // 2) // 8 * 8
        above, below = self.up(above[:cut]), self.down(below[cut:])
        return put(put(whole, above, -half), below, half, cut)

    def scatter(self, parts):
        half = self.wshard // 2
        rows = parts.shape[1]
        cut = (rows // 2) // 8 * 8

        def own(delta, begin, end):
            part = lax.dynamic_index_in_dim(parts, self.shard_at(delta), 0, keepdims=False)
            return part[begin:end]

        above = self.up(own(half, 0, cut).astype(LOW))
        below = self.down(own(-half, cut, rows).astype(LOW))
        for step in range(half - 1, 0, -1):
            up_part, down_part = own(step, 0, rows), own(-step, 0, rows)
            if step == half - 1:
                up_part = jnp.concatenate([up_part[:cut] + above.astype(F32), up_part[cut:].astype(F32)], axis=0)
                down_part = jnp.concatenate([down_part[:cut].astype(F32), down_part[cut:] + below.astype(F32)], axis=0)
            else:
                up_part = up_part + above.astype(F32)
                down_part = down_part + below.astype(F32)
            above, below = self.up(up_part.astype(LOW)), self.down(down_part.astype(LOW))
        return own(0, 0, rows).astype(F32) + above.astype(F32) + below.astype(F32)

    def chip_sum(self, value):
        bit = 1
        while bit < self.chips:
            low = value.astype(LOW)
            value = low.astype(F32) + self.chip_flip(low, bit).astype(F32)
            bit *= 2
        return value.astype(LOW)

    def both(self, value, axis):
        other = self.swap(value)
        return jnp.where(
            self.core == 0,
            jnp.concatenate([value, other], axis=axis),
            jnp.concatenate([other, value], axis=axis),
        )

    def mine(self, value, axis, which=0):
        size = value.shape[axis] // 2
        core = self.core if which == 0 else 1 - self.core
        return lax.dynamic_slice_in_dim(value, core * size, size, axis)


def slot_lists(first, count, nblocks, glob, random_rows, heads):
    blocks = first + jnp.arange(count, dtype=jnp.int32)
    offsets = jnp.arange(-1, 2, dtype=jnp.int32)
    start = jnp.clip(blocks - 1, 0, nblocks - 3)
    window = start[:, None] + jnp.arange(3, dtype=jnp.int32)[None, :]
    near = jnp.abs(window - blocks[:, None]) <= 1
    slide = jnp.clip(blocks[:, None] + offsets[None, :], 0, nblocks - 1)
    spread = lambda a: jnp.broadcast_to(a[:, None, :], (count, heads, a.shape[-1]))
    rest = jnp.concatenate(
        [jnp.broadcast_to(glob[None, None, :], (count, heads, glob.shape[0])), random_rows], axis=2
    )
    lists = jnp.concatenate([spread(slide), rest], axis=2)
    slots = lists.shape[2]
    equal = lists[..., :, None] == lists[..., None, :]
    earlier = jnp.arange(slots)[:, None] < jnp.arange(slots)[None, :]
    fresh = jnp.logical_not(jnp.any(equal & earlier[None, None], axis=-2))
    on = jnp.concatenate([spread(near), fresh[..., 3:]], axis=2)
    index = jnp.concatenate([spread(window), rest], axis=2)
    return blocks, index, jnp.where(on, index, nblocks)


def per_device(ctx, wshard, layer_input, segments, global_blocks, random_blocks, thresholds, w_query, w_key, w_value, w_output, w_inner, w_outer, query_bias, value_bias, output_bias, inner_bias, outer_bias, gain_attn, shift_attn, gain_mlp, shift_mlp, out_grad):
    m = Moves(ctx, wshard)
    chips = m.chips
    tokens = layer_input[0]
    rows_here, width = tokens.shape
    seg_all = segments[0]
    length = seg_all.shape[0]
    glob = global_blocks[0]
    nglob = glob.shape[0]
    heads = thresholds.shape[0]
    head_dim = width // heads
    nblocks = length // BLK
    chip_rows = 2 * rows_here
    count = chip_rows // BLK
    first = m.chip * count
    half = width // 2
    own_heads = heads // 2
    hidden_width = w_inner.shape[1] * wshard
    cols = w_query.shape[1]

    inputs_low = tokens.astype(LOW)
    from_chips = [inputs_low] + [m.chip_shift(inputs_low, j) for j in range(1, chips)]
    mine = jnp.concatenate(from_chips, axis=0)
    theirs = m.swap(mine)
    inputs_all = jnp.zeros((length, width), LOW)
    for j in range(chips):
        source = (m.chip - j) % chips
        cut = slice(j * rows_here, (j + 1) * rows_here)
        inputs_all = lax.dynamic_update_slice_in_dim(
            inputs_all, mine[cut], (2 * source + m.core) * rows_here, 0
        )
        inputs_all = lax.dynamic_update_slice_in_dim(
            inputs_all, theirs[cut], (2 * source + 1 - m.core) * rows_here, 0
        )

    small = jnp.concatenate(
        [query_bias, value_bias, output_bias, outer_bias, gain_attn, shift_attn, gain_mlp, shift_mlp, inner_bias]
    ).astype(LOW)
    small_rows = -(-small.shape[0] // (8 * half)) * 8
    small_piece = jnp.pad(small, (0, small_rows * half - small.shape[0])).reshape(small_rows, half)
    projections = [m.mine(w.astype(LOW).T, 1) for w in (w_query, w_key, w_value)]
    first_rows = 3 * cols + small_rows
    got = m.gather(jnp.concatenate(projections + [small_piece], axis=0)).reshape(wshard, first_rows, half)
    small_all = got[:, 3 * cols :].reshape(wshard, small_rows * half)
    vectors = [small_all[:, i * cols : (i + 1) * cols].reshape(width).astype(F32) for i in range(8)]
    bias_query, bias_value, bias_output, bias_outer, attn_gain, attn_shift, mlp_gain, mlp_shift = vectors
    inner_cols = w_inner.shape[1]
    bias_inner = small_all[:, 8 * cols : 8 * cols + inner_cols].reshape(hidden_width).astype(F32)
    halves_all = jnp.stack([got[:, i * cols : (i + 1) * cols].reshape(width, half) for i in range(3)])
    received = m.swap(m.mine(halves_all, 1, 1))
    kept = m.mine(halves_all, 1)
    head_weights = jnp.where(
        m.core == 0,
        jnp.concatenate([kept, received], axis=2),
        jnp.concatenate([received, kept], axis=2),
    )
    wq, wk, wv = head_weights[0], head_weights[1], head_weights[2]

    full_output = m.both(m.gather(m.mine(w_output.astype(LOW).T, 1)), 1)
    full_inner = m.both(m.gather(m.mine(w_inner.astype(LOW).T, 1)), 1)
    full_outer = m.both(m.gather(m.mine(w_outer.astype(LOW).T, 1)), 1)

    query = ((dot_nt(inputs_all, wq) + m.mine(bias_query, 0)).astype(LOW) * 0.125).astype(LOW)
    key = dot_nt(inputs_all, wk).astype(LOW)
    value = (dot_nt(inputs_all, wv) + m.mine(bias_value, 0)).astype(LOW)

    random_own = lax.dynamic_slice(
        random_blocks, (first, m.core * own_heads, 0), (count, own_heads, random_blocks.shape[2])
    )
    blocks, index, active = slot_lists(first, count, nblocks, glob, random_own, own_heads)
    is_global = jnp.any(blocks[:, None] == glob[None, :], axis=1)
    distinct = jnp.array([True] + [False] * (nglob - 1))
    for n in range(1, nglob):
        distinct = distinct.at[n].set(jnp.all(glob[:n] != glob[n]))
    glob_ext = jnp.concatenate([glob, jnp.zeros((max(0, chips - nglob),), jnp.int32)])
    on_ext = jnp.concatenate([distinct, jnp.zeros((max(0, chips - nglob),), bool)])
    my_glob = glob_ext[m.chip]
    my_on = on_ext[m.chip]
    flags = jnp.concatenate(
        [jnp.stack([my_glob, my_on.astype(jnp.int32), first.astype(jnp.int32)]), is_global.astype(jnp.int32)]
    )
    seg_rep = seg_all.reshape(nblocks, BLK)
    seg_rep = jnp.concatenate([seg_rep, seg_rep], axis=1)
    seg_rep = jnp.concatenate([seg_rep, jnp.full((8, 2 * BLK), -1, jnp.int32)], axis=0)
    index, active = index.reshape(-1), active.reshape(-1)
    attended, probs, attended_glob, probs_glob, top = attend(
        index, active, flags, query, key, value, seg_all[:, None], seg_rep, seg_all[None, :], count, own_heads
    )
    pairs = own_heads // 2
    local_top = jnp.max(top.reshape(pairs, 2, BLK, 2 * BLK), axis=(2, 3)).reshape(own_heads)
    glob_rows = [attended_glob] + [m.chip_shift(attended_glob, j) for j in range(1, chips)]
    attended = attended.reshape(count, BLK, half)
    for j in range(chips):
        number = (m.chip - j) % chips
        here = (blocks == glob_ext[number]) & on_ext[number]
        attended = jnp.where(here[:, None, None], glob_rows[j][None], attended)
    attended = attended.reshape(chip_rows, half)
    attn_low = m.mine(attended, 0)
    attn_other = m.swap(m.mine(attended, 0, 1))
    attn_low = jnp.where(
        m.core == 0,
        jnp.concatenate([attn_low, attn_other], axis=1),
        jnp.concatenate([attn_other, attn_low], axis=1),
    )
    spot = jnp.arange(heads, dtype=jnp.int32) // own_heads == m.core
    maxima = jnp.where(spot, jnp.concatenate([local_top, local_top]), NEG)
    maxima = jnp.pad(maxima, (0, 128 - heads))[None]
    maxima = jnp.maximum(maxima, m.swap(maxima))
    bit = 1
    while bit < chips:
        maxima = jnp.maximum(maxima, m.chip_flip(maxima, bit))
        bit *= 2
    bit = 1
    while bit < wshard:
        flipped = lax.ppermute(maxima, "wshard", [(i, i ^ bit) for i in range(wshard)])
        maxima = jnp.maximum(maxima, flipped)
        bit *= 2
    maxima = maxima[0, :heads]

    mixed = dot_nt(attn_low, full_output) + bias_output
    hidden, normed_one, inverse_one = norm_forward(tokens + mixed, attn_gain, attn_shift)
    hidden_low = hidden.astype(LOW)
    inner = dot_nt(hidden_low, full_inner) + bias_inner
    activation, slope = gelu_and_slope(inner)
    activation_low = activation.astype(LOW)
    outer = dot_nt(activation_low, full_outer) + bias_outer
    layer_output, normed_two, inverse_two = norm_forward(hidden + outer, mlp_gain, mlp_shift)
    resid_two, mlp_gain_grad, mlp_shift_grad = norm_backward(out_grad[0], normed_two, inverse_two, mlp_gain)
    outer_grad = resid_two.astype(LOW)
    outer_bias_grad = jnp.sum(outer_grad.astype(F32), axis=0)
    inner_grad = (dot_nn(outer_grad, full_outer) * slope).astype(LOW)
    inner_bias_grad = jnp.sum(inner_grad.astype(F32), axis=0)
    hidden_grad = resid_two + dot_nn(inner_grad, full_inner)
    resid_one, attn_gain_grad, attn_shift_grad = norm_backward(hidden_grad, normed_one, inverse_one, attn_gain)
    mixed_grad = resid_one.astype(LOW)
    output_bias_grad = jnp.sum(mixed_grad.astype(F32), axis=0)

    def finish(left, right):
        keep = dot_tn(left, m.mine(right, 1))
        give = dot_tn(left, m.mine(right, 1, 1)).astype(LOW)
        total = (keep + m.swap(give).astype(F32)).astype(LOW)
        total = m.scatter(total.reshape(wshard, total.shape[0] // wshard, total.shape[1]))
        return m.both(m.chip_sum(total), 1).astype(F32).T

    grad_outer = finish(outer_grad, activation_low)
    grad_inner = finish(inner_grad, hidden_low)
    grad_output = finish(mixed_grad, attn_low)

    attn_grad = dot_nn(mixed_grad, full_output).astype(LOW)
    grad_other = m.swap(m.mine(attn_grad, 1, 1))
    grad_mine = m.mine(attn_grad, 1)
    heads_grad = jnp.where(
        m.core == 0,
        jnp.concatenate([grad_mine, grad_other], axis=0),
        jnp.concatenate([grad_other, grad_mine], axis=0),
    )
    blocks_grad = heads_grad.reshape(count, BLK, half)
    glob_grad = None
    for j in range(chips):
        number = (m.chip + j) % chips
        offset = glob_ext[number] - first
        owned = (offset >= 0) & (offset < count)
        rows = lax.dynamic_index_in_dim(blocks_grad, jnp.clip(offset, 0, count - 1), 0, keepdims=False)
        rows = jnp.where(owned, rows, jnp.zeros_like(rows))
        rows = rows if j == 0 else m.chip_shift(rows, j)
        glob_grad = rows if j == 0 else glob_grad + rows
    dquery, dkey, dvalue = pull(
        index, active, flags, query, key, value, heads_grad, glob_grad, probs, probs_glob, own_heads
    )
    weight_grads = jnp.stack([dot_tn(d, inputs_all).astype(LOW) for d in (dquery, dkey, dvalue)])
    give = m.swap(m.mine(weight_grads, 2, 1))
    keep = m.mine(weight_grads, 2)
    weight_grads = jnp.where(
        m.core == 0, jnp.concatenate([keep, give], axis=1), jnp.concatenate([give, keep], axis=1)
    )
    zeros = jnp.zeros((half,), F32)

    def spread(vector):
        return jnp.where(
            m.core == 0, jnp.concatenate([vector, zeros]), jnp.concatenate([zeros, vector])
        )

    vector_grads = [
        spread(jnp.sum(dquery.astype(F32), axis=0)),
        spread(jnp.sum(dvalue.astype(F32), axis=0)),
        output_bias_grad,
        outer_bias_grad,
        attn_gain_grad,
        attn_shift_grad,
        mlp_gain_grad,
        mlp_shift_grad,
        inner_bias_grad,
    ]
    packed = jnp.concatenate([v.reshape(wshard, -1) for v in vector_grads], axis=1)
    packed = jnp.pad(packed, ((0, 0), (0, small_rows * half - packed.shape[1])))
    packed = packed.reshape(wshard, small_rows, half).astype(LOW)
    pieces = [weight_grads[i].reshape(wshard, cols, half) for i in range(3)]
    tail = m.chip_sum(m.scatter(jnp.concatenate(pieces + [packed], axis=1)))
    weight_tail = m.both(tail[: 3 * cols], 1).astype(F32)
    grad_query, grad_key, grad_value = [weight_tail[i * cols : (i + 1) * cols].T for i in range(3)]
    vector_tail = tail[3 * cols :]
    vector_tail = (vector_tail.astype(F32) + m.swap(vector_tail).astype(F32)).reshape(-1)
    vector_out = [vector_tail[i * cols : (i + 1) * cols] for i in range(8)]
    inner_out = vector_tail[8 * cols : 8 * cols + inner_cols]

    partial = dot_nn(dquery, wq) + dot_nn(dkey, wk) + dot_nn(dvalue, wv)
    partial = partial.astype(LOW).reshape(chips, 2, rows_here, width)
    passed = m.swap(m.mine(partial, 1, 1))
    summed = m.mine(partial, 1).astype(F32) + passed.astype(F32)
    summed = summed.reshape(chips, rows_here, width)
    input_grad = resid_one + lax.dynamic_index_in_dim(summed, m.chip, 0, keepdims=False)
    summed_low = summed.astype(LOW)
    for j in range(1, chips):
        send = lax.dynamic_index_in_dim(summed_low, (m.chip + j) % chips, 0, keepdims=False)
        input_grad = input_grad + m.chip_shift(send, j).astype(F32)

    root = jnp.sqrt(thresholds / jnp.maximum(maxima, thresholds))
    column_ids = m.shard * cols + jnp.arange(cols, dtype=jnp.int32)
    onehot = column_ids[:, None] // head_dim == jnp.arange(heads, dtype=jnp.int32)[None, :]
    column_scale = jnp.sum(jnp.where(onehot, root[None, :], 0.0), axis=1)
    return (
        layer_output[None],
        input_grad[None],
        grad_query,
        grad_key,
        grad_value,
        grad_output,
        grad_inner,
        grad_outer,
        vector_out[0],
        vector_out[1],
        vector_out[2],
        inner_out,
        vector_out[3],
        vector_out[4],
        vector_out[5],
        vector_out[6],
        vector_out[7],
        w_query * column_scale[None, :],
        w_key * column_scale[None, :],
        maxima,
    )


def solution(mesh):
    tokens = P("wshard", "ctx", None)
    sequence = P("wshard", None)
    matrix = P(None, "wshard")
    vector = P("wshard")
    in_specs = (tokens, sequence, sequence, P(), P()) + (matrix,) * 6 + (vector,) * 9 + (tokens,)
    out_specs = (tokens, tokens) + (matrix,) * 6 + (vector,) * 9 + (matrix, matrix, P())
    return jax.shard_map(
        functools.partial(per_device, mesh.shape["ctx"], mesh.shape["wshard"]),
        mesh=mesh,
        in_specs=in_specs,
        out_specs=out_specs,
        check_vma=False,
    )
```

```python
import functools

import jax
import jax.numpy as jnp
from jax import lax
from jax.experimental import pallas as pl
from jax.experimental.pallas import tpu as pltpu
from jax.sharding import PartitionSpec as P

BLK = 64
EPSILON = 1e-05
NEG = -1e30
UNROLL = 4
LOW = jnp.bfloat16
F32 = jnp.float32


def dot_nn(left, right):
    return lax.dot_general(left, right, (((1,), (0,)), ((), ())), preferred_element_type=F32)


def dot_tn(left, right):
    return lax.dot_general(left, right, (((0,), (0,)), ((), ())), preferred_element_type=F32)


def dot_nt(left, right):
    return lax.dot_general(left, right, (((1,), (1,)), ((), ())), preferred_element_type=F32)


def normalise(values):
    centre = values - jnp.mean(values, axis=-1, keepdims=True)
    inverse = lax.rsqrt(jnp.mean(centre * centre, axis=-1, keepdims=True) + EPSILON)
    return centre * inverse, inverse


def norm_backward(upstream, normed, inverse, gain):
    scaled = upstream * gain
    mean_one = jnp.mean(scaled, axis=-1, keepdims=True)
    mean_two = jnp.mean(scaled * normed, axis=-1, keepdims=True)
    return inverse * (scaled - mean_one - normed * mean_two)


def gelu_and_slope(v):
    c = 0.7978845608028654
    t = jnp.tanh(c * (v + 0.044715 * v * v * v))
    half = 0.5 * (1.0 + t)
    slope = half + 0.5 * v * (1.0 - t * t) * (c * (1.0 + 3 * 0.044715 * v * v))
    return v * half, slope


def global_of(glob, number):
    block = glob[jnp.minimum(number, glob.shape[0] - 1)]
    on = number < glob.shape[0]
    for i in range(glob.shape[0]):
        on = on & ((i >= number) | (glob[i] != block))
    return block, on


def in_global(glob, place):
    found = glob[0] == place
    for i in range(1, glob.shape[0]):
        found = found | (glob[i] == place)
    return found


def halves():
    lane = lax.broadcasted_iota(jnp.int32, (BLK, 2 * BLK), 1)
    return lane < BLK


def stack_pair(tile):
    low = jnp.where(halves(), 1.0, 0.0).astype(tile.dtype)
    high = jnp.where(halves(), 0.0, 1.0).astype(tile.dtype)
    return jnp.concatenate([tile * low, tile * high], axis=0)


def unstack_pair(rows):
    return jnp.where(halves(), rows[:BLK], rows[BLK:])


def rows_of(ref, block, count=1):
    return ref[pl.ds(pl.multiple_of(block * BLK, BLK), count * BLK), :]


def shared_rows(ref, index, base):
    return jnp.concatenate([rows_of(ref, index[base], 3), rows_of(ref, index[base + 3])], axis=0)


def own_rows(ref, index, base):
    return jnp.concatenate([rows_of(ref, index[base + j]) for j in range(4, 8)], axis=0)


def attend_kernel(index, active, glob, where, q_ref, k_ref, v_ref, seg_q, seg_k, seg_row, o_ref, p_ref, og_ref, pg_ref, top_ref, score, *, heads, pair, shards, blocks):
    chip = where[shards + 1]
    my_glob, my_on = global_of(glob, chip)
    step = pl.program_id(0)
    wide = lax.broadcasted_iota(jnp.int32, (1, 2 * BLK), 1) < BLK
    length = k_ref.shape[0]

    @pl.when(step == 0)
    def _():
        top_ref[...] = jnp.full(top_ref.shape, NEG, F32)

        @pl.when(jnp.logical_not(my_on))
        def _():
            og_ref[...] = jnp.zeros(og_ref.shape, og_ref.dtype)
            pg_ref[...] = jnp.zeros(pg_ref.shape, pg_ref.dtype)

        @pl.when(my_on)
        def _():
            place = my_glob
            q2 = stack_pair(rows_of(q_ref, place))
            sq = rows_of(seg_q, place)
            sq = jnp.concatenate([sq, sq], axis=0)
            top = jnp.full((2 * BLK, 1), NEG, F32)
            cut = 512
            for j in range(length // cut):
                raw = dot_nt(q2, k_ref[j * cut : (j + 1) * cut, :])
                raw = jnp.where(seg_row[:, j * cut : (j + 1) * cut] == sq, raw, NEG)
                score[:, j * cut : (j + 1) * cut] = raw
                top = jnp.maximum(top, jnp.max(raw, axis=1, keepdims=True))
            total = jnp.zeros((2 * BLK, 1), F32)
            for j in range(length // cut):
                power = jnp.exp(score[:, j * cut : (j + 1) * cut] - top)
                score[:, j * cut : (j + 1) * cut] = power
                total = total + jnp.sum(power, axis=1, keepdims=True)
            scale = 1.0 / total
            acc = jnp.zeros((2 * BLK, 2 * BLK), F32)
            for j in range(length // cut):
                prob = (score[:, j * cut : (j + 1) * cut] * scale).astype(LOW)
                pg_ref[:, j * cut : (j + 1) * cut] = prob
                acc = acc + dot_nn(prob, v_ref[j * cut : (j + 1) * cut, :])
            og_ref[...] = unstack_pair(acc).astype(LOW)
            top_ref[...] = jnp.maximum(top_ref[...], jnp.broadcast_to(top, top_ref.shape))

    for u in range(UNROLL):
        b = step * UNROLL + u
        place = chip * blocks + b
        q2 = stack_pair(rows_of(q_ref, place))
        sq = rows_of(seg_q, place)
        sq = jnp.concatenate([sq, sq], axis=0)
        base = (b * heads + 2 * pair) * 8
        shared = dot_nt(q2, shared_rows(k_ref, index, base))
        own = jnp.concatenate(
            [dot_nt(q2[h * BLK : (h + 1) * BLK], own_rows(k_ref, index, base + 8 * h)) for h in range(2)],
            axis=0,
        )

        def seg_of(at, j):
            first = seg_k[pl.ds(active[at + j], 1), :]
            second = seg_k[pl.ds(active[at + j + 1], 1), :]
            return jnp.where(wide, first, second)

        raw_s = jnp.where(jnp.concatenate([seg_of(base, 0), seg_of(base, 2)], axis=1) == sq, shared, NEG)
        seg_own = [
            jnp.broadcast_to(
                jnp.concatenate([seg_of(base + 8 * h, 4), seg_of(base + 8 * h, 6)], axis=1), (BLK, 4 * BLK)
            )
            for h in range(2)
        ]
        raw_o = jnp.where(jnp.concatenate(seg_own, axis=0) == sq, own, NEG)
        top = jnp.maximum(jnp.max(raw_s, axis=1, keepdims=True), jnp.max(raw_o, axis=1, keepdims=True))
        power_s = jnp.exp(raw_s - top)
        power_o = jnp.exp(raw_o - top)
        scale = 1.0 / (jnp.sum(power_s, axis=1, keepdims=True) + jnp.sum(power_o, axis=1, keepdims=True))
        prob_s = (power_s * scale).astype(LOW)
        prob_o = (power_o * scale).astype(LOW)
        p_ref[u, :, : 4 * BLK] = prob_s
        p_ref[u, :, 4 * BLK :] = prob_o
        out = dot_nn(prob_s, shared_rows(v_ref, index, base))
        out = out + jnp.concatenate(
            [
                dot_nn(prob_o[h * BLK : (h + 1) * BLK], own_rows(v_ref, index, base + 8 * h))
                for h in range(2)
            ],
            axis=0,
        )
        o_ref[u * BLK : (u + 1) * BLK, :] = unstack_pair(out).astype(LOW)
        used = jnp.where(in_global(glob, place), jnp.full_like(top, NEG), top)
        top_ref[...] = jnp.maximum(top_ref[...], jnp.broadcast_to(used, top_ref.shape))


def pull_kernel(index, active, glob, where, q_ref, k_ref, v_ref, do_ref, p_ref, pg_ref, *refs, heads, pair, shards, blocks):
    *dog_refs, dq_ref, dk_ref, dv_ref, dk, dv, score = refs
    chip = where[shards + 1]
    my_glob, my_on = global_of(glob, chip)
    del active
    step = pl.program_id(0)
    steps = pl.num_programs(0)
    length = k_ref.shape[0]

    @pl.when(step == 0)
    def _():
        dk[...] = jnp.zeros(dk.shape, F32)
        dv[...] = jnp.zeros(dv.shape, F32)
        dq_ref[...] = jnp.zeros(dq_ref.shape, dq_ref.dtype)

    def add(ref, block, value):
        at = pl.ds(pl.multiple_of(block * BLK, BLK), value.shape[0])
        ref[at, :] += value

    for u in range(UNROLL):
        b = step * UNROLL + u
        place = chip * blocks + b
        q2 = stack_pair(rows_of(q_ref, place))
        keep = jnp.where(in_global(glob, place), 0.0, 1.0).astype(LOW)
        do2 = stack_pair(do_ref[u * BLK : (u + 1) * BLK, :] * keep)
        base = (b * heads + 2 * pair) * 8
        ks = shared_rows(k_ref, index, base)
        ko = [own_rows(k_ref, index, base + 8 * h) for h in range(2)]
        vs = shared_rows(v_ref, index, base)
        vo = [own_rows(v_ref, index, base + 8 * h) for h in range(2)]
        prob_s = p_ref[u, :, : 4 * BLK]
        prob_o = p_ref[u, :, 4 * BLK :]
        dp_s = dot_nt(do2, vs)
        dp_o = jnp.concatenate([dot_nt(do2[h * BLK : (h + 1) * BLK], vo[h]) for h in range(2)], axis=0)
        ps = prob_s.astype(F32)
        po = prob_o.astype(F32)
        ts = ps * dp_s
        to = po * dp_o
        total = jnp.sum(ts, axis=1, keepdims=True) + jnp.sum(to, axis=1, keepdims=True)
        ds_s = (ts - ps * total).astype(LOW)
        ds_o = (to - po * total).astype(LOW)
        dq = dot_nn(ds_s, ks) + jnp.concatenate(
            [dot_nn(ds_o[h * BLK : (h + 1) * BLK], ko[h]) for h in range(2)], axis=0
        )
        at = pl.ds(pl.multiple_of(place * BLK, BLK), BLK)
        dq_ref[at, :] = (unstack_pair(dq) * 0.125).astype(LOW)
        dks = dot_tn(ds_s, q2)
        dvs = dot_tn(prob_s, do2)
        add(dk, index[base], dks[: 3 * BLK])
        add(dk, index[base + 3], dks[3 * BLK :])
        add(dv, index[base], dvs[: 3 * BLK])
        add(dv, index[base + 3], dvs[3 * BLK :])
        for h in range(2):
            part = slice(h * BLK, (h + 1) * BLK)
            dko = dot_tn(ds_o[part], q2[part])
            dvo = dot_tn(prob_o[part], do2[part])
            for j in range(4):
                add(dk, index[base + 8 * h + 4 + j], dko[j * BLK : (j + 1) * BLK])
                add(dv, index[base + 8 * h + 4 + j], dvo[j * BLK : (j + 1) * BLK])

    @pl.when((step == steps - 1) & my_on)
    def _():
        place = my_glob
        q2 = stack_pair(rows_of(q_ref, place))
        dog = dog_refs[0][...].astype(F32)
        for ref in dog_refs[1:]:
            dog = dog + ref[...].astype(F32)
        do2 = stack_pair(dog.astype(LOW))
        cut = 512
        total = jnp.zeros((2 * BLK, 1), F32)
        for j in range(length // cut):
            part = slice(j * cut, (j + 1) * cut)
            dp = dot_nt(do2, v_ref[part, :])
            score[:, part] = dp
            total = total + jnp.sum(pg_ref[:, part].astype(F32) * dp, axis=1, keepdims=True)
        acc = jnp.zeros((2 * BLK, 2 * BLK), F32)
        for j in range(length // cut):
            part = slice(j * cut, (j + 1) * cut)
            prob = pg_ref[:, part]
            ds = (prob.astype(F32) * (score[:, part] - total)).astype(LOW)
            acc = acc + dot_nn(ds, k_ref[part, :])
            dk[part, :] += dot_tn(ds, q2)
            dv[part, :] += dot_tn(prob, do2)
        at = pl.ds(pl.multiple_of(place * BLK, BLK), BLK)
        dq_ref[at, :] = (unstack_pair(acc) * 0.125).astype(LOW)

    @pl.when(step == steps - 1)
    def _():
        dk_ref[...] = dk[...].astype(LOW)
        dv_ref[...] = dv[...].astype(LOW)


def attend(index, active, glob, where, query, key, value, seg_col, seg_rep, seg_row, blocks, heads, pair, shards):
    length = key.shape[0]
    column = pl.BlockSpec((length, 2 * BLK), lambda s, *_: (0, pair))
    whole = lambda shape: pl.BlockSpec(shape, lambda s, *_: (0,) * len(shape))
    grid = pltpu.PrefetchScalarGridSpec(
        num_scalar_prefetch=4,
        grid=(blocks // UNROLL,),
        in_specs=[column, column, column, whole(seg_col.shape), whole(seg_rep.shape), whole(seg_row.shape)],
        out_specs=[
            pl.BlockSpec((UNROLL * BLK, 2 * BLK), lambda s, *_: (s, 0)),
            pl.BlockSpec((UNROLL, 2 * BLK, 8 * BLK), lambda s, *_: (s, 0, 0)),
            whole((BLK, 2 * BLK)),
            whole((2 * BLK, length)),
            whole((2 * BLK, 2 * BLK)),
        ],
        scratch_shapes=[pltpu.VMEM((2 * BLK, length), F32)],
    )
    work = (blocks * 8 + length // BLK) * 2 * BLK * BLK
    return pl.pallas_call(
        functools.partial(attend_kernel, heads=heads, pair=pair, shards=shards, blocks=blocks),
        grid_spec=grid,
        out_shape=[
            jax.ShapeDtypeStruct((blocks * BLK, 2 * BLK), LOW),
            jax.ShapeDtypeStruct((blocks, 2 * BLK, 8 * BLK), LOW),
            jax.ShapeDtypeStruct((BLK, 2 * BLK), LOW),
            jax.ShapeDtypeStruct((2 * BLK, length), LOW),
            jax.ShapeDtypeStruct((2 * BLK, 2 * BLK), F32),
        ],
        compiler_params=pltpu.CompilerParams(vmem_limit_bytes=32 << 20),
        cost_estimate=pl.CostEstimate(flops=work * 8192, bytes_accessed=6 << 20, transcendentals=work),
        name="attend",
    )(index, active, glob, where, query, key, value, seg_col, seg_rep, seg_row)


def pull(index, active, glob, where, query, key, value, grad, grad_glob, probs, probs_glob, heads, pair, shards):
    length = key.shape[0]
    blocks = grad.shape[0] // BLK
    column = pl.BlockSpec((length, 2 * BLK), lambda s, *_: (0, pair))
    whole = lambda shape: pl.BlockSpec(shape, lambda s, *_: (0,) * len(shape))
    grid = pltpu.PrefetchScalarGridSpec(
        num_scalar_prefetch=4,
        grid=(blocks // UNROLL,),
        in_specs=[
            column,
            column,
            column,
            pl.BlockSpec((UNROLL * BLK, 2 * BLK), lambda s, *_: (s, pair)),
            pl.BlockSpec((UNROLL, 2 * BLK, 8 * BLK), lambda s, *_: (s, 0, 0)),
            whole((2 * BLK, length)),
        ]
        + [pl.BlockSpec((BLK, 2 * BLK), lambda s, *_: (0, pair))] * len(grad_glob),
        out_specs=[whole((length, 2 * BLK))] * 3,
        scratch_shapes=[
            pltpu.VMEM((length, 2 * BLK), F32),
            pltpu.VMEM((length, 2 * BLK), F32),
            pltpu.VMEM((2 * BLK, length), F32),
        ],
    )
    work = (blocks * 8 + length // BLK) * 2 * BLK * BLK
    return pl.pallas_call(
        functools.partial(pull_kernel, heads=heads, pair=pair, shards=shards, blocks=blocks),
        grid_spec=grid,
        out_shape=[jax.ShapeDtypeStruct((length, 2 * BLK), LOW)] * 3,
        compiler_params=pltpu.CompilerParams(vmem_limit_bytes=32 << 20),
        cost_estimate=pl.CostEstimate(flops=work * 8192, bytes_accessed=8 << 20, transcendentals=0),
        name="pull",
    )(index, active, glob, where, query, key, value, grad, probs, probs_glob, *grad_glob)


def eye(size):
    row = lax.broadcasted_iota(jnp.int32, (size, size), 0)
    column = lax.broadcasted_iota(jnp.int32, (size, size), 1)
    return jnp.where(row == column, 1.0, 0.0).astype(LOW)


def lanes(start, size):
    return pl.ds(pl.multiple_of(start, 128), size)


def simple_call(kernel, out_shape, args, scalars, name, cost, scratch=(), anywhere=0, limit=32):
    smem = pl.BlockSpec(memory_space=pltpu.SMEM)
    vmem = pl.BlockSpec(memory_space=pltpu.VMEM)
    free = pl.BlockSpec(memory_space=pl.ANY)
    specs = [smem] * len(scalars) + [free] * anywhere + [vmem] * (len(args) - anywhere)
    return pl.pallas_call(
        kernel,
        in_specs=specs,
        out_specs=jax.tree.map(lambda _: vmem, out_shape),
        out_shape=out_shape,
        scratch_shapes=list(scratch),
        compiler_params=pltpu.CompilerParams(vmem_limit_bytes=limit << 20),
        cost_estimate=pl.CostEstimate(flops=cost[0], bytes_accessed=cost[1], transcendentals=0),
        name=name,
    )(*scalars, *args)


def pack_heads_kernel(where, wq, wk, wv, *refs, shards):
    *vectors, out, rows_ref = refs
    half, cols = wq.shape[0] // 2, wq.shape[1]
    core = where[shards]
    unit = eye(cols)
    for i, ref in enumerate((wq, wk, wv)):
        rows = ref[pl.ds(pl.multiple_of(core * half, 128), half), :].astype(LOW)
        out[i * cols : (i + 1) * cols, :] = dot_nt(unit, rows).astype(LOW)
    rows_ref[...] = jnp.zeros(rows_ref.shape, F32)
    for v, ref in enumerate(vectors[:-1]):
        at = v % 3 * 128
        rows_ref[v // 3 : v // 3 + 1, at : at + cols] = ref[...]
    rows_ref[3:4, : vectors[-1].shape[1]] = vectors[-1][...]
    out[3 * cols :, :] = rows_ref[...].astype(LOW)


def pack_rest_kernel(where, inner, output, outer, out_one, out_two, *, shards):
    half, cols = output.shape[0] // 2, output.shape[1]
    wide = inner.shape[1]
    unit, unit_wide = eye(cols), eye(wide)
    core = where[shards]
    rows = inner[pl.ds(pl.multiple_of(core * half, 128), half), :].astype(LOW)
    out_one[...] = dot_nt(unit_wide, rows).astype(LOW)
    rows = output[pl.ds(pl.multiple_of(core * half, 128), half), :].astype(LOW)
    out_two[:cols, :] = dot_nt(unit, rows).astype(LOW)
    count = outer.shape[0] // 2 // half
    for j in range(count):
        start = (core * count + j) * half
        rows = outer[pl.ds(pl.multiple_of(start, 128), half), :].astype(LOW)
        at = cols * (1 + j)
        out_two[at : at + cols, :] = dot_nt(unit, rows).astype(LOW)


def project_kernel(
    where, got, passed, mine, theirs, q_ref, k_ref, v_ref, wh, vec, bias_inner, pieces, sem, *, rows, chips, cols, wide
):
    shards, half = pieces.shape[1], pieces.shape[3]
    core, chip = where[shards], where[shards + 1]
    copies = []
    for side, ref in enumerate((got, passed)):
        for i in range(shards):
            copies.append(pltpu.make_async_copy(ref.at[i], pieces.at[side, where[i]], sem.at[side, i]))
    for copy in copies:
        copy.start()
    for copy in copies:
        copy.wait()
    for side in range(2):
        for t in range(3):
            part = pieces[side, pl.ds(core * (shards // 2), shards // 2), t * cols : (t + 1) * cols, :]
            wh[side, t] = part.reshape(half, half)
    for i in range(shards):
        small = pieces[0, i, 3 * cols :, :].astype(F32)
        for v in range(8):
            at = v % 3 * 128
            vec[v : v + 1, i * cols : (i + 1) * cols] = small[v // 3 : v // 3 + 1, at : at + cols]
        unit, at = i * wide // half, i * wide % half
        bias_inner[unit : unit + 1, at : at + wide] = small[3:4, :wide]
    own_lanes, other_lanes = lanes(core * half, half), lanes((1 - core) * half, half)
    for j in range(chips):
        source = lax.rem(chip - j + chips, chips)
        for side, ref in enumerate((mine, theirs)):
            place = (2 * source + (core if side == 0 else 1 - core)) * rows
            at = pl.ds(pl.multiple_of(place, rows), rows)
            left = ref[j * rows : (j + 1) * rows, own_lanes]
            right = ref[j * rows : (j + 1) * rows, other_lanes]
            for t, out in enumerate((q_ref, k_ref, v_ref)):
                value = dot_nt(left, wh[0, t]) + dot_nt(right, wh[1, t])
                if t == 0:
                    value = (value + vec[0:1, own_lanes]).astype(LOW).astype(F32) * 0.125
                if t == 2:
                    value = value + vec[1:2, own_lanes]
                out[at, :] = value.astype(LOW)


def merge_kernel(where, glob, *refs, shards, chips, rows):
    outs = refs[-2:]
    parts, globs = refs[: -2 - chips], refs[-2 - chips : -2]
    core, chip = where[shards], where[shards + 1]
    full = jnp.concatenate
    for side, out in enumerate(outs):
        start = (core if side == 0 else 1 - core) * rows
        out[...] = full([p[pl.ds(pl.multiple_of(start, rows), rows), :] for p in parts], axis=1)
    per = 2 * rows // BLK
    for j in range(chips):
        number = lax.rem(chip - j + chips, chips)
        block, on = global_of(glob, number)
        local = block - chip * per
        for side, out in enumerate(outs):
            start = local - (core if side == 0 else 1 - core) * (per // 2)

            @pl.when(on & (start >= 0) & (start < per // 2))
            def _(out=out, start=start, j=j):
                out[pl.ds(pl.multiple_of(start * BLK, BLK), BLK), :] = globs[j][...]


def spread_kernel(where, glob, own, other, heads_grad, *sends, shards, chips, rows):
    core, chip = where[shards], where[shards + 1]
    heads_grad[pl.ds(pl.multiple_of(core * rows, rows), rows), :] = own[...]
    heads_grad[pl.ds(pl.multiple_of((1 - core) * rows, rows), rows), :] = other[...]
    per = 2 * rows // BLK
    for j, send in enumerate(sends):
        number = lax.rem(chip + j, chips)
        block, on = global_of(glob, number)
        local = block - chip * per
        send[...] = jnp.zeros(send.shape, send.dtype)

        @pl.when(on & (local >= 0) & (local < per))
        def _(send=send, local=local):
            send[...] = heads_grad[pl.ds(pl.multiple_of(local * BLK, BLK), BLK), :]


def weight_grad_kernel(
    where, *refs, rows, chips, pairs, cols, wide, shards, devices
):
    grads = refs[: 3 * pairs]
    tops = refs[3 * pairs : 4 * pairs]
    mine, theirs, vec_grad, inner_bias, layout, keep, give, small, vec = refs[4 * pairs :]
    core, chip = where[shards], where[shards + 1]
    half = mine.shape[1] // 2
    vec[...] = vec_grad[...]
    vec[0:2, :] = jnp.zeros((2, vec.shape[1]), F32)
    for t in range(3):
        whole = [jnp.zeros((half, half), F32)] * 2
        total = jnp.zeros((1, half), F32)
        for j in range(chips):
            source = lax.rem(chip - j + chips, chips)
            for side, ref in enumerate((mine, theirs)):
                place = (2 * source + (core if side == 0 else 1 - core)) * rows
                at = pl.ds(pl.multiple_of(place, rows), rows)
                part = jnp.concatenate([g[at, :] for g in grads[t * pairs : (t + 1) * pairs]], axis=1)
                if t != 1:
                    total = total + jnp.sum(part.astype(F32), axis=0, keepdims=True)
                for s in range(2):
                    which = core if s == 0 else 1 - core
                    whole[s] = whole[s] + dot_tn(part, ref[j * rows : (j + 1) * rows, lanes(which * half, half)])
        for s, out in enumerate((keep, give)):
            out[:, t * cols : (t + 1) * cols, :] = whole[s].astype(LOW).reshape(shards // 2, cols, half)
        if t != 1:
            vec[t // 2 : t // 2 + 1, lanes(core * half, half)] = total
    head, part, slot = layout[0:1, :], layout[1:2, :], layout[2:3, :]
    value = jnp.full((1, half), NEG, F32)
    for p in range(pairs):
        for i in range(2):
            top = jnp.max(tops[p][i * BLK : (i + 1) * BLK, :], axis=0, keepdims=True)
            value = jnp.where(head == core * 2 * pairs + 2 * p + i, top[:, 0:1], value)
    first = value.astype(LOW).astype(F32)
    second = (value - first).astype(LOW).astype(F32)
    third = value - first - second
    value = jnp.where(part == 0, first, jnp.where(part == 1, second, jnp.where(part == 2, third, 0.0)))
    small[...] = jnp.zeros(small.shape, F32)
    device = where[shards + 3]
    value = jnp.where(slot == lax.rem(device, 8), value, 0.0)
    for r in range(devices // 8):
        line = jnp.where(device // 8 == r, value, 0.0)
        for i in range(shards):
            small[i, 4 + r : 5 + r, :] = line
    for i in range(shards):
        for v in range(8):
            at = v % 3 * 128
            small[i, v // 3 : v // 3 + 1, at : at + cols] = vec[v : v + 1, i * cols : (i + 1) * cols]
        unit, at = i * wide // half, i * wide % half
        small[i, 3:4, :wide] = inner_bias[unit : unit + 1, at : at + wide]


def token_grad_kernel(where, *refs, rows, chips, pairs, shards):
    grads, (wh, mine, theirs) = refs[: 3 * pairs], refs[3 * pairs :]
    core, chip = where[shards], where[shards + 1]
    half = mine.shape[1] // 2
    for j in range(chips):
        source = lax.rem(chip - j + chips, chips)
        for side, out in enumerate((mine, theirs)):
            place = (2 * source + (core if side == 0 else 1 - core)) * rows
            at = pl.ds(pl.multiple_of(place, rows), rows)
            parts = [
                jnp.concatenate([g[at, :] for g in grads[t * pairs : (t + 1) * pairs]], axis=1) for t in range(3)
            ]
            for s in range(2):
                which = core if s == 0 else 1 - core
                total = dot_nn(parts[0], wh[s, 0]) + dot_nn(parts[1], wh[s, 1]) + dot_nn(parts[2], wh[s, 2])
                out[j * rows : (j + 1) * rows, lanes(which * half, half)] = total.astype(LOW)


def finish_heads_kernel(where, own, other, limits, wq, wk, *outs, shards, devices, head_dim):
    grads, vectors, (inner, maxima, cut_q, cut_k) = outs[:3], outs[3:11], outs[11:]
    core, shard = where[shards], where[shards + 2]
    half, cols = own.shape[1], wq.shape[1]
    unit = eye(half)
    for t, out in enumerate(grads):
        for ref, which in ((own, core), (other, 1 - core)):
            value = dot_nt(unit, ref[t * cols : (t + 1) * cols, :])
            out[pl.ds(pl.multiple_of(which * half, 128), half), :] = value
    small = own[3 * cols :, :].astype(F32) + other[3 * cols :, :].astype(F32)
    for v, out in enumerate(vectors):
        at = v % 3 * 128
        out[...] = small[v // 3 : v // 3 + 1, at : at + cols]
    inner[...] = small[3:4, : inner.shape[1]]
    heads = limits.shape[1]
    value = jnp.full((1, half), NEG, F32)
    for r in range(devices // 8):
        line = jnp.broadcast_to(small[4 + r : 5 + r, :], (8, half))
        line = line + pltpu.roll(line, half - heads, 1) + pltpu.roll(line, half - 2 * heads, 1)
        value = jnp.maximum(value, line)
    step = half // 2
    while step >= 48:
        value = jnp.maximum(value, pltpu.roll(value, step, 1))
        step //= 2
    top = value[0:1, :heads]
    maxima[...] = top
    root = jnp.sqrt(limits[...] / jnp.maximum(top, limits[...]))
    column = lax.broadcasted_iota(jnp.int32, (1, cols), 1) + shard * cols
    scale = jnp.zeros((1, cols), F32)
    for h in range(heads):
        inside = (column >= h * head_dim) & (column < (h + 1) * head_dim)
        scale = jnp.where(inside, root[:, h : h + 1], scale)
    cut_q[...] = wq[...] * scale
    cut_k[...] = wk[...] * scale


def finish_rest_kernel(where, own_one, other_one, own_two, other_two, inner, output, outer, *, shards):
    half, cols = own_one.shape[1], output.shape[1]
    unit = eye(half)
    core = where[shards]
    for one, two, which in ((own_one, own_two, core), (other_one, other_two, 1 - core)):
        inner[pl.ds(pl.multiple_of(which * half, 128), half), :] = dot_nt(unit, one[...])
        output[pl.ds(pl.multiple_of(which * half, 128), half), :] = dot_nt(unit, two[:cols, :])
        count = outer.shape[0] // 2 // half
        for j in range(count):
            at = cols * (1 + j)
            start = (which * count + j) * half
            outer[pl.ds(pl.multiple_of(start, 128), half), :] = dot_nt(unit, two[at : at + cols, :])


def dense_kernel(
    where, one_a, one_b, one_c, one_d, two_a, two_b, two_c, two_d, att_own, att_other, tokens, cotangent, vec, bias_inner,
    layer_out, resid, grad_own, grad_other, keep_one, give_one, keep_two, give_two, vec_grad, inner_bias_grad,
    one, two, low, hidden, normed, inverse, act, slope, acc, outer_grad, sem,
):
    shards, wide, half = one.shape[1:]
    rows, width = tokens.shape
    cols = width // shards
    core = where[shards]
    copies = []
    for n, (packed, sources) in enumerate(
        ((two, ((two_a, two_b), (two_c, two_d))), (one, ((one_a, one_b), (one_c, one_d))))
    ):
        for side, pair in enumerate(sources):
            at = 0
            for ref in pair:
                for i in range(ref.shape[0]):
                    copies.append(pltpu.make_async_copy(ref.at[i], packed.at[side, where[at]], sem.at[n, side, at]))
                    at += 1
    for copy in copies:
        copy.start()
    for copy in copies:
        copy.wait()
    own, other = lanes(core * half, half), lanes((1 - core) * half, half)
    sides = (own, other)
    units = shards * wide // half
    each = half // wide
    step = 128

    def inner_weights(side, u):
        return one[side, u * each : (u + 1) * each].reshape(half, half)

    def outer_at(u):
        begin = cols * (1 + u % (units // 2))
        return slice(begin, begin + cols)

    def outer_weights(u):
        side = jnp.where(core == u // (units // 2), 0, 1)
        return two[side, :, outer_at(u), :].reshape(width, half)

    def output_weights(side):
        return two[side, :, :cols, :].reshape(width, half)

    acc[...] = dot_nt(att_own[...], output_weights(0)) + dot_nt(att_other[...], output_weights(1))
    for r in range(0, rows, step):
        at = slice(r, r + step)
        n, inv = normalise(tokens[at, :] + (acc[at, :] + vec[2:3, :]))
        normed[at, :] = n
        inverse[at, :] = inv
        h = n * vec[4:5, :] + vec[5:6, :]
        hidden[at, :] = h
        low[at, :] = h.astype(LOW)

    for u in range(units):
        inner = dot_nt(low[:, own], inner_weights(0, u)) + dot_nt(low[:, other], inner_weights(1, u))
        a, d = gelu_and_slope(inner + bias_inner[u : u + 1, :])
        act[u] = a.astype(LOW)
        slope[u] = d
        product = dot_nt(act[u], outer_weights(u))
        acc[...] = product if u == 0 else acc[...] + product

    sums = [jnp.zeros((1, width), F32)] * 3
    for r in range(0, rows, step):
        at = slice(r, r + step)
        n, inv = normalise(hidden[at, :] + (acc[at, :] + vec[3:4, :]))
        layer_out[at, :] = n * vec[6:7, :] + vec[7:8, :]
        e = cotangent[at, :]
        dv = norm_backward(e, n, inv, vec[6:7, :])
        acc[at, :] = dv
        dl = dv.astype(LOW)
        outer_grad[at, :] = dl
        sums = [
            sums[0] + jnp.sum(dl.astype(F32), axis=0, keepdims=True),
            sums[1] + jnp.sum(e * n, axis=0, keepdims=True),
            sums[2] + jnp.sum(e, axis=0, keepdims=True),
        ]
    vec_grad[3:4, :] = sums[0]
    vec_grad[6:7, :] = sums[1]
    vec_grad[7:8, :] = sums[2]

    turned = outer_grad[...].T
    for u in range(units):
        inner_grad = dot_nn(outer_grad[...], outer_weights(u)) * slope[u]
        inner_low = inner_grad.astype(LOW)
        inner_bias_grad[u : u + 1, :] = jnp.sum(inner_low.astype(F32), axis=0, keepdims=True)
        for side, at in enumerate(sides):
            acc[:, at] += dot_nn(inner_low, inner_weights(side, u))
        inner_turned = inner_low.T
        for out, at in ((keep_one, own), (give_one, other)):
            part = dot_nn(inner_turned, low[:, at]).astype(LOW)
            out[u * each : (u + 1) * each] = part.reshape(each, wide, half)
        part = dot_nn(turned, act[u]).astype(LOW).reshape(shards, cols, half)

        @pl.when(core == u // (units // 2))
        def _(u=u, part=part):
            keep_two[:, outer_at(u), :] = part

        @pl.when(core != u // (units // 2))
        def _(u=u, part=part):
            give_two[:, outer_at(u), :] = part

    sums = [jnp.zeros((1, width), F32)] * 3
    for r in range(0, rows, step):
        at = slice(r, r + step)
        e, n = acc[at, :], normed[at, :]
        dv = norm_backward(e, n, inverse[at, :], vec[4:5, :])
        resid[at, :] = dv
        dl = dv.astype(LOW)
        outer_grad[at, :] = dl
        sums = [
            sums[0] + jnp.sum(dl.astype(F32), axis=0, keepdims=True),
            sums[1] + jnp.sum(e * n, axis=0, keepdims=True),
            sums[2] + jnp.sum(e, axis=0, keepdims=True),
        ]
    vec_grad[0:2, :] = jnp.zeros((2, width), F32)
    vec_grad[2:3, :] = sums[0]
    vec_grad[4:5, :] = sums[1]
    vec_grad[5:6, :] = sums[2]
    grad_own[...] = dot_nn(outer_grad[...], output_weights(0)).astype(LOW)
    grad_other[...] = dot_nn(outer_grad[...], output_weights(1)).astype(LOW)
    turned = outer_grad[...].T
    for out, ref in ((keep_two, att_own), (give_two, att_other)):
        part = dot_nn(turned, ref[...]).astype(LOW)
        out[:, :cols, :] = part.reshape(shards, cols, half)


def ring_kernel(where, *refs, counts, kind, cut):
    refs = list(refs)
    parts = []
    for count in counts:
        total = refs.pop(0)[0].astype(F32)
        for _ in range(count - 1):
            total = total + refs.pop(0)[0].astype(F32)
        parts.append(total)
    if kind == "first":
        up, down = refs
        up[...] = parts[0][:cut].astype(LOW)
        down[...] = parts[0][cut:].astype(LOW)
    elif kind == "second":
        above, below, up, down = refs
        up[:cut, :] = (parts[0][:cut] + above[...].astype(F32)).astype(LOW)
        up[cut:, :] = parts[0][cut:].astype(LOW)
        down[:cut, :] = parts[1][:cut].astype(LOW)
        down[cut:, :] = (parts[1][cut:] + below[...].astype(F32)).astype(LOW)
    elif kind == "later":
        above, below, up, down = refs
        up[...] = (parts[0] + above[...].astype(F32)).astype(LOW)
        down[...] = (parts[1] + below[...].astype(F32)).astype(LOW)
    else:
        above, below, out = refs
        out[...] = (parts[0] + above[...].astype(F32) + below[...].astype(F32)).astype(LOW)


def ring_step(where, arrays, slots, received, kind, cut):
    rows, half = arrays[0].shape[1:]
    specs = [
        pl.BlockSpec((1, rows, half), lambda i, where, slot=slot: (where[slot], 0, 0)) for slot in slots for _ in arrays
    ]
    specs += [pl.BlockSpec(a.shape, lambda i, where: (0, 0)) for a in received]
    shapes = [(rows, half)] if kind == "last" else [(rows, half)] * 2
    if kind == "first":
        shapes = [(cut, half), (rows - cut, half)]
    return pl.pallas_call(
        functools.partial(ring_kernel, counts=[len(arrays)] * len(slots), kind=kind, cut=cut),
        grid_spec=pltpu.PrefetchScalarGridSpec(
            num_scalar_prefetch=1,
            grid=(1,),
            in_specs=specs,
            out_specs=[pl.BlockSpec(s, lambda i, where: (0, 0)) for s in shapes],
        ),
        out_shape=[struct(s) for s in shapes],
        compiler_params=pltpu.CompilerParams(vmem_limit_bytes=32 << 20),
        cost_estimate=pl.CostEstimate(flops=10**6, bytes_accessed=3 << 20, transcendentals=0),
        name="ring_" + kind,
    )(where, *[a for _ in slots for a in arrays], *received)


class Moves:
    def __init__(self, ctx, wshard):
        self.ctx, self.wshard, self.chips = ctx, wshard, ctx // 2
        self.half = half = wshard // 2
        order = list(range(0, wshard, 2)) + list(range(wshard - 1, 0, -2))
        self.up_perm = [(order[i], order[(i + 1) % wshard]) for i in range(wshard)]
        self.down_perm = [(b, a) for a, b in self.up_perm]
        deltas = [0]
        for step in range(1, half):
            deltas += [-step, step]
        deltas.append(half)
        sums = [half]
        for step in range(half - 1, 0, -1):
            sums += [step, -step]
        sums.append(0)
        table = []
        for c in range(ctx):
            for w in range(wshard):
                at = order.index(w)
                goes = [order[(at + d) % wshard] for d in sums]
                placed = [(s // half != c % 2) * half + s % half for s in goes]
                table.append(
                    [order[(at + d) % wshard] for d in deltas] + [c % 2, c // 2, w, c * wshard + w] + goes + placed
                )
        self.sums, self.placed = wshard + 4, wshard + 4 + len(sums)
        here = lax.axis_index("ctx") * wshard + lax.axis_index("wshard")
        table = jnp.asarray(table, jnp.int32)
        self.where = lax.dynamic_slice(table, (here, 0), (1, table.shape[1]), allow_negative_indices=False)[0]

    def up(self, value):
        return lax.ppermute(value, "wshard", self.up_perm)

    def down(self, value):
        return lax.ppermute(value, "wshard", self.down_perm)

    def swap(self, value):
        return lax.ppermute(value, "ctx", [(c, c ^ 1) for c in range(self.ctx)])

    def chip_shift(self, value, j):
        return lax.ppermute(value, "ctx", [(c, (c + 2 * j) % self.ctx) for c in range(self.ctx)])

    def chip_flip(self, value, bit):
        return lax.ppermute(value, "ctx", [(c, c ^ (2 * bit)) for c in range(self.ctx)])

    def gather(self, piece, cut):
        above = below = piece
        pieces = [piece]
        for _ in range(1, self.half):
            above, below = self.up(above), self.down(below)
            pieces += [above, below]
        pieces.append(jnp.concatenate([self.up(above[:cut]), self.down(below[cut:])], axis=0))
        return pieces

    def scatter(self, step, cut):
        up, down = step("first", [0], [])
        yield up
        for s in range(self.half - 1):
            above, below = self.up(up), self.down(down)
            up, down = step("second" if s == 0 else "later", [1 + 2 * s, 2 + 2 * s], [above, below])
            yield up
        above, below = self.up(up), self.down(down)
        [total] = step("last", [2 * self.half - 1], [above, below])
        yield total

    def chip_sum(self, value):
        bit = 1
        while bit < self.chips:
            other = self.chip_flip(value, bit)
            value = (value.astype(F32) + other.astype(F32)).astype(LOW)
            bit *= 2
        return value


def slot_lists(first, count, nblocks, glob, random_rows, heads):
    blocks = first + jnp.arange(count, dtype=jnp.int32)
    offsets = jnp.arange(-1, 2, dtype=jnp.int32)
    start = jnp.clip(blocks - 1, 0, nblocks - 3)
    window = start[:, None] + jnp.arange(3, dtype=jnp.int32)[None, :]
    near = jnp.abs(window - blocks[:, None]) <= 1
    slide = jnp.clip(blocks[:, None] + offsets[None, :], 0, nblocks - 1)
    spread = lambda a: jnp.broadcast_to(a[:, None, :], (count, heads, a.shape[-1]))
    rest = jnp.concatenate(
        [jnp.broadcast_to(glob[None, None, :], (count, heads, glob.shape[0])), random_rows], axis=2
    )
    lists = jnp.concatenate([spread(slide), rest], axis=2)
    slots = lists.shape[2]
    equal = lists[..., :, None] == lists[..., None, :]
    earlier = jnp.arange(slots)[:, None] < jnp.arange(slots)[None, :]
    fresh = jnp.logical_not(jnp.any(equal & earlier[None, None], axis=-2))
    on = jnp.concatenate([spread(near), fresh[..., 3:]], axis=2)
    index = jnp.concatenate([spread(window), rest], axis=2)
    return index, jnp.where(on, index, nblocks)


def struct(shape, dtype=LOW):
    return jax.ShapeDtypeStruct(tuple(shape), dtype)


def after(value, *others):
    return lax.optimization_barrier((value,) + others)[0]


def per_device(ctx, wshard, layer_input, segments, global_blocks, random_blocks, thresholds, w_query, w_key, w_value, w_output, w_inner, w_outer, query_bias, value_bias, output_bias, inner_bias, outer_bias, gain_attn, shift_attn, gain_mlp, shift_mlp, out_grad):
    m = Moves(ctx, wshard)
    chips, where, devices = m.chips, m.where, ctx * wshard
    tokens = layer_input[0]
    rows_here, width = tokens.shape
    seg_all = segments[0]
    length = seg_all.shape[0]
    glob = global_blocks[0]
    heads = thresholds.shape[0]
    head_dim = width // heads
    nblocks = length // BLK
    count = 2 * rows_here // BLK
    half = width // 2
    own_heads = heads // 2
    pairs = own_heads // 2
    cols, wide = w_query.shape[1], w_inner.shape[1]
    units = wide * wshard // half
    sizes = dict(shards=wshard, rows=rows_here, chips=chips)

    small_least = 4 + devices // 8
    head_rows = -(-(3 * cols + 4) // 16) * 16
    vectors = (query_bias, value_bias, output_bias, outer_bias, gain_attn, shift_attn, gain_mlp, shift_mlp, inner_bias)
    head_piece = simple_call(
        functools.partial(pack_heads_kernel, shards=wshard),
        struct((head_rows, half)),
        (w_query, w_key, w_value) + tuple(v[None] for v in vectors),
        (where,),
        "pack_heads",
        (10**8, 10**6),
        scratch=[pltpu.VMEM((head_rows - 3 * cols, half), F32)],
    )
    inputs_low = tokens.astype(LOW)
    mine = jnp.concatenate([inputs_low] + [m.chip_shift(inputs_low, j) for j in range(1, chips)], axis=0)
    theirs = m.swap(mine)
    head_pieces = m.gather(head_piece, head_rows // 2 // 16 * 16)
    got = jnp.stack(head_pieces)
    passed = m.swap(got)
    query, key, value, head_weights, vec, bias_inner = simple_call(
        functools.partial(project_kernel, rows=rows_here, chips=chips, cols=cols, wide=wide),
        [struct((length, half))] * 3
        + [struct((2, 3, half, half)), struct((8, width), F32), struct((units, half), F32)],
        (got, passed, mine, theirs),
        (where,),
        "project",
        (2 * length * width * 3 * half, 12 << 20),
        scratch=[pltpu.VMEM((2, wshard, head_rows, half), LOW), pltpu.SemaphoreType.DMA((2, wshard))],
        anywhere=2,
        limit=40,
    )

    piece_one, piece_two = simple_call(
        functools.partial(pack_rest_kernel, shards=wshard),
        [struct((wide, half)), struct((5 * cols, half))],
        (w_inner, w_output, w_outer),
        (where,),
        "pack_rest",
        (10**9, 4 * 10**6),
    )
    piece_one, piece_two = after((piece_one, piece_two), head_pieces[-1])
    pieces_one = m.gather(piece_one, wide // 2)
    pieces_two = m.gather(piece_two, 5 * cols // 2 // 8 * 8)
    rest = []
    for pieces in (pieces_one, pieces_two):
        early, late = jnp.stack(pieces[:-3]), jnp.stack(pieces[-3:])
        rest += [early, late, m.swap(early), m.swap(late)]

    chip, core = where[wshard + 1], where[wshard]
    random_own = lax.dynamic_slice(
        random_blocks,
        (chip * count, core * own_heads, 0),
        (count, own_heads, random_blocks.shape[2]),
        allow_negative_indices=False,
    )
    index, active = slot_lists(chip * count, count, nblocks, glob, random_own, own_heads)
    seg_rep = seg_all.reshape(nblocks, BLK)
    seg_rep = jnp.concatenate([seg_rep, seg_rep], axis=1)
    seg_rep = jnp.concatenate([seg_rep, jnp.full((8, 2 * BLK), -1, jnp.int32)], axis=0)
    scalars = (index.reshape(-1), active.reshape(-1), glob, where)
    seg_args = (seg_all[:, None], seg_rep, seg_all[None, :])
    done = []
    for pair in range(pairs):
        at = min(1 + 2 * pair, len(pieces_one) - 1)
        turn = (pieces_one[at - 1], pieces_two[at - 1]) if pair else ()
        q = after(query, *turn) if turn else query
        done.append(attend(*scalars, q, key, value, *seg_args, count, own_heads, pair, wshard))
    attended_glob = jnp.concatenate([d[2] for d in done], axis=1)
    glob_rows = [attended_glob] + [m.chip_shift(attended_glob, j) for j in range(1, chips)]
    att_own, att_give = simple_call(
        functools.partial(merge_kernel, **sizes),
        [struct((rows_here, half))] * 2,
        tuple(d[0] for d in done) + tuple(glob_rows),
        (where, glob),
        "merge",
        (10**6, 2 << 20),
    )
    att_other = m.swap(att_give)

    big = lambda *shape: pltpu.VMEM(shape, F32)
    low = lambda *shape: pltpu.VMEM(shape, LOW)
    layer_output, resid_one, grad_own, grad_other, keep_one, give_one, keep_two, give_two, vec_grad, inner_bias_grad = (
        simple_call(
            dense_kernel,
            [struct((rows_here, width), F32)] * 2
            + [struct((rows_here, half))] * 2
            + [struct((wshard, wide, half))] * 2
            + [struct((wshard, 5 * cols, half))] * 2
            + [struct((8, width), F32), struct((units, half), F32)],
            tuple(rest) + (att_own, att_other, tokens, out_grad[0], vec, bias_inner),
            (where,),
            "dense",
            (32 * rows_here * width * width, 30 << 20),
            scratch=[
                low(2, wshard, wide, half),
                low(2, wshard, 5 * cols, half),
                low(rows_here, width),
                big(rows_here, width),
                big(rows_here, width),
                big(rows_here, 1),
                low(units, rows_here, half),
                big(units, rows_here, half),
                big(rows_here, width),
                low(rows_here, width),
                pltpu.SemaphoreType.DMA((2, 2, wshard)),
            ],
            anywhere=8,
            limit=60,
        )
    )

    from_other = m.swap(grad_other)
    given_two, given_one = m.swap(give_two), m.swap(give_one)
    heads_grad, *glob_sends = simple_call(
        functools.partial(spread_kernel, **sizes),
        [struct((2 * rows_here, half))] + [struct((BLK, half))] * chips,
        (grad_own, from_other),
        (where, glob),
        "spread",
        (10**6, 2 << 20),
    )
    glob_grads = [glob_sends[0]] + [m.chip_shift(glob_sends[j], j) for j in range(1, chips)]

    def ring_of(arrays, cut, base):
        def step(kind, slots, received):
            return ring_step(where, arrays, [base + s for s in slots], received, kind, cut)

        return m.scatter(step, cut)

    ring_one = ring_of([keep_one, given_one], wide // 2 // 16 * 16, m.sums)
    ring_two = ring_of([keep_two, given_two], 5 * cols // 2 // 16 * 16, m.sums)
    rings = (ring_two, ring_one)
    turn = ()
    pulled = []
    for pair in range(pairs):
        q = after(query, *turn) if turn else query
        pulled.append(
            pull(*scalars, q, key, value, heads_grad, glob_grads, done[pair][1], done[pair][3], own_heads, pair, wshard)
        )
        turn = tuple(next(ring) for ring in rings)
    grads = tuple(pulled[pair][t] for t in range(3) for pair in range(pairs))
    dense_cost = (2 * length * width * 3 * half, 12 << 20)
    small_rows = -(-(3 * cols + small_least) // 16) * 16 - 3 * cols
    lane = [i % 48 for i in range(half)]
    layout = jnp.asarray(
        [[i % heads if i < 3 * heads else -1 for i in lane], [i // heads for i in lane], [i // 48 for i in range(half)]],
        jnp.int32,
    )
    layout = jnp.concatenate([layout, jnp.zeros((5, half), jnp.int32)], axis=0)
    grads = after(grads, *turn)
    head_keep, head_give, small_parts = simple_call(
        functools.partial(weight_grad_kernel, pairs=pairs, cols=cols, wide=wide, devices=devices, **sizes),
        [struct((wshard // 2, 3 * cols, half))] * 2 + [struct((wshard, small_rows, half), F32)],
        grads + tuple(d[4] for d in done) + (mine, theirs, vec_grad, inner_bias_grad, layout),
        (where,),
        "weight_grad",
        dense_cost,
        scratch=[big(8, width)],
    )
    head_given = m.swap(head_give)
    turn = tuple(next(ring) for ring in rings)
    grads = after(grads, *turn)
    part_mine, part_theirs = simple_call(
        functools.partial(token_grad_kernel, pairs=pairs, **sizes),
        [struct((chips * rows_here, width))] * 2,
        grads + (head_weights,),
        (where,),
        "token_grad",
        dense_cost,
    )
    head_parts = jnp.concatenate([head_keep, head_given], axis=0)

    def head_step(kind, slots, received):
        return head_ring_step(where, head_parts, small_parts, m, slots, received, kind)

    *_, head_tail = m.scatter(head_step, None)
    rest_tail = []
    for ring in rings:
        *_, total = ring
        rest_tail.append(m.chip_sum(total))
    tail_two, tail_one = rest_tail
    grad_inner, grad_output, grad_outer = simple_call(
        functools.partial(finish_rest_kernel, shards=wshard),
        [struct(w_inner.shape, F32), struct(w_output.shape, F32), struct(w_outer.shape, F32)],
        (tail_one, m.swap(tail_one), tail_two, m.swap(tail_two)),
        (where,),
        "finish_rest",
        (10**9, 6 << 20),
    )
    head_tail = m.chip_sum(head_tail)
    vector = struct((1, cols), F32)
    finished = simple_call(
        functools.partial(finish_heads_kernel, shards=wshard, devices=devices, head_dim=head_dim),
        [struct(w_query.shape, F32)] * 3
        + [vector] * 8
        + [struct((1, wide), F32), struct((1, heads), F32), struct(w_query.shape, F32), struct(w_query.shape, F32)],
        (head_tail, m.swap(head_tail), thresholds[None], w_query, w_key),
        (where,),
        "finish_heads",
        (10**8, 3 << 20),
    )
    grad_query, grad_key, grad_value = finished[:3]
    vector_out = [v[0] for v in finished[3:11]]
    inner_out, maxima, clipped_query, clipped_key = finished[11][0], finished[12][0], finished[13], finished[14]

    summed = part_mine.astype(F32) + m.swap(part_theirs).astype(F32)
    summed = summed.reshape(chips, rows_here, width)
    input_grad = resid_one + summed[0]
    for j in range(1, chips):
        input_grad = input_grad + m.chip_shift(summed[j].astype(LOW), chips - j).astype(F32)
    return (
        layer_output[None],
        input_grad[None],
        grad_query,
        grad_key,
        grad_value,
        grad_output,
        grad_inner,
        grad_outer,
        vector_out[0],
        vector_out[1],
        vector_out[2],
        inner_out,
        vector_out[3],
        vector_out[4],
        vector_out[5],
        vector_out[6],
        vector_out[7],
        clipped_query,
        clipped_key,
        maxima,
    )


def head_ring_kernel(where, *refs, kind, targets, cut):
    refs = list(refs)
    parts = []
    for _ in range(targets):
        part, small = refs.pop(0), refs.pop(0)
        parts.append(jnp.concatenate([part[0].astype(F32), small[0]], axis=0))
    if kind == "first":
        up, down = refs
        up[...] = parts[0][:cut].astype(LOW)
        down[...] = parts[0][cut:].astype(LOW)
    elif kind == "second":
        above, below, up, down = refs
        up[:cut, :] = (parts[0][:cut] + above[...].astype(F32)).astype(LOW)
        up[cut:, :] = parts[0][cut:].astype(LOW)
        down[:cut, :] = parts[1][:cut].astype(LOW)
        down[cut:, :] = (parts[1][cut:] + below[...].astype(F32)).astype(LOW)
    elif kind == "later":
        above, below, up, down = refs
        up[...] = (parts[0] + above[...].astype(F32)).astype(LOW)
        down[...] = (parts[1] + below[...].astype(F32)).astype(LOW)
    else:
        above, below, out = refs
        out[...] = (parts[0] + above[...].astype(F32) + below[...].astype(F32)).astype(LOW)


def head_ring_step(where, parts, small, m, slots, received, kind):
    half = parts.shape[2]
    rows = parts.shape[1] + small.shape[1]
    cut = rows // 2 // 16 * 16
    specs, args = [], []
    for slot in slots:
        specs.append(
            pl.BlockSpec((1,) + parts.shape[1:], lambda i, where, at=m.placed + slot: (where[at], 0, 0))
        )
        specs.append(pl.BlockSpec((1,) + small.shape[1:], lambda i, where, at=m.sums + slot: (where[at], 0, 0)))
        args += [parts, small]
    specs += [pl.BlockSpec(a.shape, lambda i, where: (0, 0)) for a in received]
    shapes = [(rows, half)] if kind == "last" else [(rows, half)] * 2
    if kind == "first":
        shapes = [(cut, half), (rows - cut, half)]
    return pl.pallas_call(
        functools.partial(head_ring_kernel, kind=kind, targets=len(slots), cut=cut),
        grid_spec=pltpu.PrefetchScalarGridSpec(
            num_scalar_prefetch=1,
            grid=(1,),
            in_specs=specs,
            out_specs=[pl.BlockSpec(s, lambda i, where: (0, 0)) for s in shapes],
        ),
        out_shape=[struct(s) for s in shapes],
        compiler_params=pltpu.CompilerParams(vmem_limit_bytes=32 << 20),
        cost_estimate=pl.CostEstimate(flops=10**6, bytes_accessed=2 << 20, transcendentals=0),
        name="head_ring_" + kind,
    )(where, *args, *received)


def solution(mesh):
    tokens = P("wshard", "ctx", None)
    sequence = P("wshard", None)
    matrix = P(None, "wshard")
    vector = P("wshard")
    in_specs = (tokens, sequence, sequence, P(), P()) + (matrix,) * 6 + (vector,) * 9 + (tokens,)
    out_specs = (tokens, tokens) + (matrix,) * 6 + (vector,) * 9 + (matrix, matrix, P())
    return jax.shard_map(
        functools.partial(per_device, mesh.shape["ctx"], mesh.shape["wshard"]),
        mesh=mesh,
        in_specs=in_specs,
        out_specs=out_specs,
        check_vma=False,
    )
```

```python
import functools

import jax
import jax.numpy as jnp
from jax import lax
from jax.experimental import pallas as pl
from jax.experimental.pallas import tpu as pltpu
from jax.sharding import PartitionSpec as P

BLK = 64
EPSILON = 1e-05
NEG = -1e30
UNROLL = 4
LOW = jnp.bfloat16
F32 = jnp.float32


def dot_nn(left, right):
    return lax.dot_general(left, right, (((1,), (0,)), ((), ())), preferred_element_type=F32)


def dot_tn(left, right):
    return lax.dot_general(left, right, (((0,), (0,)), ((), ())), preferred_element_type=F32)


def dot_nt(left, right):
    return lax.dot_general(left, right, (((1,), (1,)), ((), ())), preferred_element_type=F32)


def normalise(values):
    centre = values - jnp.mean(values, axis=-1, keepdims=True)
    inverse = lax.rsqrt(jnp.mean(centre * centre, axis=-1, keepdims=True) + EPSILON)
    return centre * inverse, inverse


def norm_backward(upstream, normed, inverse, gain):
    scaled = upstream * gain
    mean_one = jnp.mean(scaled, axis=-1, keepdims=True)
    mean_two = jnp.mean(scaled * normed, axis=-1, keepdims=True)
    return inverse * (scaled - mean_one - normed * mean_two)


def gelu_and_slope(v):
    c = 0.7978845608028654
    t = jnp.tanh(c * (v + 0.044715 * v * v * v))
    half = 0.5 * (1.0 + t)
    slope = half + 0.5 * v * (1.0 - t * t) * (c * (1.0 + 3 * 0.044715 * v * v))
    return v * half, slope


def global_of(glob, number):
    block = glob[jnp.minimum(number, glob.shape[0] - 1)]
    on = number < glob.shape[0]
    for i in range(glob.shape[0]):
        on = on & ((i >= number) | (glob[i] != block))
    return block, on


def in_global(glob, place):
    found = glob[0] == place
    for i in range(1, glob.shape[0]):
        found = found | (glob[i] == place)
    return found


def halves():
    lane = lax.broadcasted_iota(jnp.int32, (BLK, 2 * BLK), 1)
    return lane < BLK


def stack_pair(tile):
    low = jnp.where(halves(), 1.0, 0.0).astype(tile.dtype)
    high = jnp.where(halves(), 0.0, 1.0).astype(tile.dtype)
    return jnp.concatenate([tile * low, tile * high], axis=0)


def unstack_pair(rows):
    return jnp.where(halves(), rows[:BLK], rows[BLK:])


def rows_of(ref, block, count=1):
    return ref[pl.ds(pl.multiple_of(block * BLK, BLK), count * BLK), :]


def shared_rows(ref, index, base):
    return jnp.concatenate([rows_of(ref, index[base], 3), rows_of(ref, index[base + 3])], axis=0)


def own_rows(ref, index, base):
    return jnp.concatenate([rows_of(ref, index[base + j]) for j in range(4, 8)], axis=0)


def attend_kernel(index, active, glob, where, q_ref, k_ref, v_ref, seg_q, seg_k, seg_row, o_ref, p_ref, og_ref, pg_ref, top_ref, score, *, heads, pair, shards, blocks):
    chip = where[shards + 1]
    my_glob, my_on = global_of(glob, chip)
    step = pl.program_id(0)
    wide = lax.broadcasted_iota(jnp.int32, (1, 2 * BLK), 1) < BLK
    length = k_ref.shape[0]

    @pl.when(step == 0)
    def _():
        top_ref[...] = jnp.full(top_ref.shape, NEG, F32)

        @pl.when(jnp.logical_not(my_on))
        def _():
            og_ref[...] = jnp.zeros(og_ref.shape, og_ref.dtype)
            pg_ref[...] = jnp.zeros(pg_ref.shape, pg_ref.dtype)

        @pl.when(my_on)
        def _():
            place = my_glob
            q2 = stack_pair(rows_of(q_ref, place))
            sq = rows_of(seg_q, place)
            sq = jnp.concatenate([sq, sq], axis=0)
            top = jnp.full((2 * BLK, 1), NEG, F32)
            cut = 512
            for j in range(length // cut):
                raw = dot_nt(q2, k_ref[j * cut : (j + 1) * cut, :])
                raw = jnp.where(seg_row[:, j * cut : (j + 1) * cut] == sq, raw, NEG)
                score[:, j * cut : (j + 1) * cut] = raw
                top = jnp.maximum(top, jnp.max(raw, axis=1, keepdims=True))
            total = jnp.zeros((2 * BLK, 1), F32)
            for j in range(length // cut):
                power = jnp.exp(score[:, j * cut : (j + 1) * cut] - top)
                score[:, j * cut : (j + 1) * cut] = power
                total = total + jnp.sum(power, axis=1, keepdims=True)
            scale = 1.0 / total
            acc = jnp.zeros((2 * BLK, 2 * BLK), F32)
            for j in range(length // cut):
                prob = (score[:, j * cut : (j + 1) * cut] * scale).astype(LOW)
                pg_ref[:, j * cut : (j + 1) * cut] = prob
                acc = acc + dot_nn(prob, v_ref[j * cut : (j + 1) * cut, :])
            og_ref[...] = unstack_pair(acc).astype(LOW)
            top_ref[...] = jnp.maximum(top_ref[...], jnp.broadcast_to(top, top_ref.shape))

    for u in range(UNROLL):
        b = step * UNROLL + u
        place = chip * blocks + b
        q2 = stack_pair(rows_of(q_ref, place))
        sq = rows_of(seg_q, place)
        sq = jnp.concatenate([sq, sq], axis=0)
        base = (b * heads + 2 * pair) * 8
        shared = dot_nt(q2, shared_rows(k_ref, index, base))
        own = jnp.concatenate(
            [dot_nt(q2[h * BLK : (h + 1) * BLK], own_rows(k_ref, index, base + 8 * h)) for h in range(2)],
            axis=0,
        )

        def seg_of(at, j):
            first = seg_k[pl.ds(active[at + j], 1), :]
            second = seg_k[pl.ds(active[at + j + 1], 1), :]
            return jnp.where(wide, first, second)

        raw_s = jnp.where(jnp.concatenate([seg_of(base, 0), seg_of(base, 2)], axis=1) == sq, shared, NEG)
        seg_own = [
            jnp.broadcast_to(
                jnp.concatenate([seg_of(base + 8 * h, 4), seg_of(base + 8 * h, 6)], axis=1), (BLK, 4 * BLK)
            )
            for h in range(2)
        ]
        raw_o = jnp.where(jnp.concatenate(seg_own, axis=0) == sq, own, NEG)
        top = jnp.maximum(jnp.max(raw_s, axis=1, keepdims=True), jnp.max(raw_o, axis=1, keepdims=True))
        power_s = jnp.exp(raw_s - top)
        power_o = jnp.exp(raw_o - top)
        scale = 1.0 / (jnp.sum(power_s, axis=1, keepdims=True) + jnp.sum(power_o, axis=1, keepdims=True))
        prob_s = (power_s * scale).astype(LOW)
        prob_o = (power_o * scale).astype(LOW)
        p_ref[u, :, : 4 * BLK] = prob_s
        p_ref[u, :, 4 * BLK :] = prob_o
        out = dot_nn(prob_s, shared_rows(v_ref, index, base))
        out = out + jnp.concatenate(
            [
                dot_nn(prob_o[h * BLK : (h + 1) * BLK], own_rows(v_ref, index, base + 8 * h))
                for h in range(2)
            ],
            axis=0,
        )
        o_ref[u * BLK : (u + 1) * BLK, :] = unstack_pair(out).astype(LOW)
        used = jnp.where(in_global(glob, place), jnp.full_like(top, NEG), top)
        top_ref[...] = jnp.maximum(top_ref[...], jnp.broadcast_to(used, top_ref.shape))


def pull_kernel(index, active, glob, where, q_ref, k_ref, v_ref, do_ref, p_ref, pg_ref, *refs, heads, pair, shards, blocks):
    *dog_refs, dq_ref, dk_ref, dv_ref, dk, dv, score = refs
    chip = where[shards + 1]
    my_glob, my_on = global_of(glob, chip)
    del active
    step = pl.program_id(0)
    steps = pl.num_programs(0)
    length = k_ref.shape[0]

    @pl.when(step == 0)
    def _():
        dk[...] = jnp.zeros(dk.shape, F32)
        dv[...] = jnp.zeros(dv.shape, F32)
        dq_ref[...] = jnp.zeros(dq_ref.shape, dq_ref.dtype)

    def add(ref, block, value):
        at = pl.ds(pl.multiple_of(block * BLK, BLK), value.shape[0])
        ref[at, :] += value

    for u in range(UNROLL):
        b = step * UNROLL + u
        place = chip * blocks + b
        q2 = stack_pair(rows_of(q_ref, place))
        keep = jnp.where(in_global(glob, place), 0.0, 1.0).astype(LOW)
        do2 = stack_pair(do_ref[u * BLK : (u + 1) * BLK, :] * keep)
        base = (b * heads + 2 * pair) * 8
        ks = shared_rows(k_ref, index, base)
        ko = [own_rows(k_ref, index, base + 8 * h) for h in range(2)]
        vs = shared_rows(v_ref, index, base)
        vo = [own_rows(v_ref, index, base + 8 * h) for h in range(2)]
        prob_s = p_ref[u, :, : 4 * BLK]
        prob_o = p_ref[u, :, 4 * BLK :]
        dp_s = dot_nt(do2, vs)
        dp_o = jnp.concatenate([dot_nt(do2[h * BLK : (h + 1) * BLK], vo[h]) for h in range(2)], axis=0)
        ps = prob_s.astype(F32)
        po = prob_o.astype(F32)
        ts = ps * dp_s
        to = po * dp_o
        total = jnp.sum(ts, axis=1, keepdims=True) + jnp.sum(to, axis=1, keepdims=True)
        ds_s = (ts - ps * total).astype(LOW)
        ds_o = (to - po * total).astype(LOW)
        dq = dot_nn(ds_s, ks) + jnp.concatenate(
            [dot_nn(ds_o[h * BLK : (h + 1) * BLK], ko[h]) for h in range(2)], axis=0
        )
        at = pl.ds(pl.multiple_of(place * BLK, BLK), BLK)
        dq_ref[at, :] = (unstack_pair(dq) * 0.125).astype(LOW)
        dks = dot_tn(ds_s, q2)
        dvs = dot_tn(prob_s, do2)
        add(dk, index[base], dks[: 3 * BLK])
        add(dk, index[base + 3], dks[3 * BLK :])
        add(dv, index[base], dvs[: 3 * BLK])
        add(dv, index[base + 3], dvs[3 * BLK :])
        for h in range(2):
            part = slice(h * BLK, (h + 1) * BLK)
            dko = dot_tn(ds_o[part], q2[part])
            dvo = dot_tn(prob_o[part], do2[part])
            for j in range(4):
                add(dk, index[base + 8 * h + 4 + j], dko[j * BLK : (j + 1) * BLK])
                add(dv, index[base + 8 * h + 4 + j], dvo[j * BLK : (j + 1) * BLK])

    @pl.when((step == steps - 1) & my_on)
    def _():
        place = my_glob
        q2 = stack_pair(rows_of(q_ref, place))
        dog = dog_refs[0][...].astype(F32)
        for ref in dog_refs[1:]:
            dog = dog + ref[...].astype(F32)
        do2 = stack_pair(dog.astype(LOW))
        cut = 512
        total = jnp.zeros((2 * BLK, 1), F32)
        for j in range(length // cut):
            part = slice(j * cut, (j + 1) * cut)
            dp = dot_nt(do2, v_ref[part, :])
            score[:, part] = dp
            total = total + jnp.sum(pg_ref[:, part].astype(F32) * dp, axis=1, keepdims=True)
        acc = jnp.zeros((2 * BLK, 2 * BLK), F32)
        for j in range(length // cut):
            part = slice(j * cut, (j + 1) * cut)
            prob = pg_ref[:, part]
            ds = (prob.astype(F32) * (score[:, part] - total)).astype(LOW)
            acc = acc + dot_nn(ds, k_ref[part, :])
            dk[part, :] += dot_tn(ds, q2)
            dv[part, :] += dot_tn(prob, do2)
        at = pl.ds(pl.multiple_of(place * BLK, BLK), BLK)
        dq_ref[at, :] = (unstack_pair(acc) * 0.125).astype(LOW)

    @pl.when(step == steps - 1)
    def _():
        dk_ref[...] = dk[...].astype(LOW)
        dv_ref[...] = dv[...].astype(LOW)


def attend(index, active, glob, where, query, key, value, seg_col, seg_rep, seg_row, blocks, heads, pair, shards):
    length = key.shape[0]
    column = pl.BlockSpec((length, 2 * BLK), lambda s, *_: (0, pair))
    whole = lambda shape: pl.BlockSpec(shape, lambda s, *_: (0,) * len(shape))
    grid = pltpu.PrefetchScalarGridSpec(
        num_scalar_prefetch=4,
        grid=(blocks // UNROLL,),
        in_specs=[column, column, column, whole(seg_col.shape), whole(seg_rep.shape), whole(seg_row.shape)],
        out_specs=[
            pl.BlockSpec((UNROLL * BLK, 2 * BLK), lambda s, *_: (s, 0)),
            pl.BlockSpec((UNROLL, 2 * BLK, 8 * BLK), lambda s, *_: (s, 0, 0)),
            whole((BLK, 2 * BLK)),
            whole((2 * BLK, length)),
            whole((2 * BLK, 2 * BLK)),
        ],
        scratch_shapes=[pltpu.VMEM((2 * BLK, length), F32)],
    )
    work = (blocks * 8 + length // BLK) * 2 * BLK * BLK
    return pl.pallas_call(
        functools.partial(attend_kernel, heads=heads, pair=pair, shards=shards, blocks=blocks),
        grid_spec=grid,
        out_shape=[
            jax.ShapeDtypeStruct((blocks * BLK, 2 * BLK), LOW),
            jax.ShapeDtypeStruct((blocks, 2 * BLK, 8 * BLK), LOW),
            jax.ShapeDtypeStruct((BLK, 2 * BLK), LOW),
            jax.ShapeDtypeStruct((2 * BLK, length), LOW),
            jax.ShapeDtypeStruct((2 * BLK, 2 * BLK), F32),
        ],
        compiler_params=pltpu.CompilerParams(vmem_limit_bytes=32 << 20),
        cost_estimate=pl.CostEstimate(flops=work * 8192, bytes_accessed=6 << 20, transcendentals=0),
        name="attend",
    )(index, active, glob, where, query, key, value, seg_col, seg_rep, seg_row)


def pull(index, active, glob, where, query, key, value, grad, grad_glob, probs, probs_glob, heads, pair, shards):
    length = key.shape[0]
    blocks = grad.shape[0] // BLK
    column = pl.BlockSpec((length, 2 * BLK), lambda s, *_: (0, pair))
    whole = lambda shape: pl.BlockSpec(shape, lambda s, *_: (0,) * len(shape))
    grid = pltpu.PrefetchScalarGridSpec(
        num_scalar_prefetch=4,
        grid=(blocks // UNROLL,),
        in_specs=[
            column,
            column,
            column,
            pl.BlockSpec((UNROLL * BLK, 2 * BLK), lambda s, *_: (s, pair)),
            pl.BlockSpec((UNROLL, 2 * BLK, 8 * BLK), lambda s, *_: (s, 0, 0)),
            whole((2 * BLK, length)),
        ]
        + [pl.BlockSpec((BLK, 2 * BLK), lambda s, *_: (0, pair))] * len(grad_glob),
        out_specs=[whole((length, 2 * BLK))] * 3,
        scratch_shapes=[
            pltpu.VMEM((length, 2 * BLK), F32),
            pltpu.VMEM((length, 2 * BLK), F32),
            pltpu.VMEM((2 * BLK, length), F32),
        ],
    )
    work = (blocks * 8 + length // BLK) * 2 * BLK * BLK
    return pl.pallas_call(
        functools.partial(pull_kernel, heads=heads, pair=pair, shards=shards, blocks=blocks),
        grid_spec=grid,
        out_shape=[jax.ShapeDtypeStruct((length, 2 * BLK), LOW)] * 3,
        compiler_params=pltpu.CompilerParams(vmem_limit_bytes=32 << 20),
        cost_estimate=pl.CostEstimate(flops=work * 8192, bytes_accessed=8 << 20, transcendentals=0),
        name="pull",
    )(index, active, glob, where, query, key, value, grad, probs, probs_glob, *grad_glob)


def eye(size):
    row = lax.broadcasted_iota(jnp.int32, (size, size), 0)
    column = lax.broadcasted_iota(jnp.int32, (size, size), 1)
    return jnp.where(row == column, 1.0, 0.0).astype(LOW)


def lanes(start, size):
    return pl.ds(pl.multiple_of(start, 128), size)


def simple_call(kernel, out_shape, args, scalars, name, cost, scratch=(), anywhere=0, limit=32):
    smem = pl.BlockSpec(memory_space=pltpu.SMEM)
    vmem = pl.BlockSpec(memory_space=pltpu.VMEM)
    free = pl.BlockSpec(memory_space=pl.ANY)
    specs = [smem] * len(scalars) + [free] * anywhere + [vmem] * (len(args) - anywhere)
    return pl.pallas_call(
        kernel,
        in_specs=specs,
        out_specs=jax.tree.map(lambda _: vmem, out_shape),
        out_shape=out_shape,
        scratch_shapes=list(scratch),
        compiler_params=pltpu.CompilerParams(vmem_limit_bytes=limit << 20),
        cost_estimate=pl.CostEstimate(flops=cost * 10**9, bytes_accessed=1 << 18, transcendentals=0),
        name=name,
    )(*scalars, *args)


def pack_heads_kernel(where, wq, wk, wv, *refs, shards):
    vectors, out, rows_ref = refs
    half, cols = wq.shape[1] // 2, wq.shape[0]
    here = lanes(where[shards] * half, half)
    for i, ref in enumerate((wq, wk, wv)):
        out[i * cols : (i + 1) * cols, :] = ref[:, here].astype(LOW)
    rows_ref[...] = jnp.zeros(rows_ref.shape, F32)
    for v in range(8):
        at = v % 3 * 128
        rows_ref[v // 3 : v // 3 + 1, at : at + cols] = vectors[:, v * cols : (v + 1) * cols]
    rows_ref[3:4, : vectors.shape[1] - 8 * cols] = vectors[:, 8 * cols :]
    out[3 * cols :, :] = rows_ref[...].astype(LOW)


def pack_rest_kernel(where, inner, output, outer, out, *, shards):
    half, cols = output.shape[1] // 2, output.shape[0]
    core = where[shards]
    rows = inner[pl.ds(pl.multiple_of(core * half, 128), half), :].astype(LOW)
    wide = inner.shape[1]
    out[:wide, :] = dot_nt(eye(wide), rows).astype(LOW)
    out[wide : wide + cols, :] = output[:, lanes(core * half, half)].astype(LOW)
    count = outer.shape[1] // 2 // half
    for j in range(count):
        at = wide + cols * (1 + j)
        out[at : at + cols, :] = outer[:, lanes((core * count + j) * half, half)].astype(LOW)


def project_kernel(
    where, got, passed, mine, theirs, q_ref, k_ref, v_ref, wh, vec, bias_inner, pieces, sem, *, rows, chips, cols, wide
):
    shards, half = pieces.shape[1], pieces.shape[3]
    core, chip = where[shards], where[shards + 1]
    copies = []
    for side, ref in enumerate((got, passed)):
        for i in range(shards):
            copies.append(pltpu.make_async_copy(ref.at[i], pieces.at[side, where[i]], sem.at[side, i]))
    for copy in copies:
        copy.start()
    for copy in copies:
        copy.wait()
    for side in range(2):
        for t in range(3):
            part = pieces[side, pl.ds(core * (shards // 2), shards // 2), t * cols : (t + 1) * cols, :]
            wh[side, t] = part.reshape(half, half)
    for i in range(shards):
        small = pieces[0, i, 3 * cols :, :].astype(F32)
        for v in range(8):
            at = v % 3 * 128
            vec[v : v + 1, i * cols : (i + 1) * cols] = small[v // 3 : v // 3 + 1, at : at + cols]
        unit, at = i * wide // half, i * wide % half
        bias_inner[unit : unit + 1, at : at + wide] = small[3:4, :wide]
    own_lanes, other_lanes = lanes(core * half, half), lanes((1 - core) * half, half)
    for j in range(chips):
        source = lax.rem(chip - j + chips, chips)
        for side, ref in enumerate((mine, theirs)):
            place = (2 * source + (core if side == 0 else 1 - core)) * rows
            at = pl.ds(pl.multiple_of(place, rows), rows)
            left = ref[j * rows : (j + 1) * rows, own_lanes]
            right = ref[j * rows : (j + 1) * rows, other_lanes]
            for t, out in enumerate((q_ref, k_ref, v_ref)):
                value = dot_nt(left, wh[0, t]) + dot_nt(right, wh[1, t])
                if t == 0:
                    value = (value + vec[0:1, own_lanes]).astype(LOW).astype(F32) * 0.125
                if t == 2:
                    value = value + vec[1:2, own_lanes]
                out[at, :] = value.astype(LOW)


def merge_kernel(where, glob, *refs, shards, chips, rows):
    outs = refs[-2:]
    parts, globs = refs[: -2 - chips], refs[-2 - chips : -2]
    core, chip = where[shards], where[shards + 1]
    full = jnp.concatenate
    for side, out in enumerate(outs):
        start = (core if side == 0 else 1 - core) * rows
        out[...] = full([p[pl.ds(pl.multiple_of(start, rows), rows), :] for p in parts], axis=1)
    per = 2 * rows // BLK
    for j in range(chips):
        number = lax.rem(chip - j + chips, chips)
        block, on = global_of(glob, number)
        local = block - chip * per
        for side, out in enumerate(outs):
            start = local - (core if side == 0 else 1 - core) * (per // 2)

            @pl.when(on & (start >= 0) & (start < per // 2))
            def _(out=out, start=start, j=j):
                out[pl.ds(pl.multiple_of(start * BLK, BLK), BLK), :] = globs[j][...]


def spread_kernel(where, glob, own, other, heads_grad, *sends, shards, chips, rows):
    core, chip = where[shards], where[shards + 1]
    heads_grad[pl.ds(pl.multiple_of(core * rows, rows), rows), :] = own[...]
    heads_grad[pl.ds(pl.multiple_of((1 - core) * rows, rows), rows), :] = other[...]
    per = 2 * rows // BLK
    for j, send in enumerate(sends):
        number = lax.rem(chip + j, chips)
        block, on = global_of(glob, number)
        local = block - chip * per
        send[...] = jnp.zeros(send.shape, send.dtype)

        @pl.when(on & (local >= 0) & (local < per))
        def _(send=send, local=local):
            send[...] = heads_grad[pl.ds(pl.multiple_of(local * BLK, BLK), BLK), :]


def weight_grad_kernel(
    where, *refs, rows, chips, pairs, cols, wide, shards, devices
):
    grads = refs[: 3 * pairs]
    tops = refs[3 * pairs : 4 * pairs]
    mine, theirs, vec_grad, inner_bias, layout, keep, give, small, vec = refs[4 * pairs :]
    core, chip = where[shards], where[shards + 1]
    half = mine.shape[1] // 2
    vec[...] = vec_grad[...]
    vec[0:2, :] = jnp.zeros((2, vec.shape[1]), F32)
    for t in range(3):
        whole = [jnp.zeros((half, half), F32)] * 2
        total = jnp.zeros((1, half), F32)
        for j in range(chips):
            source = lax.rem(chip - j + chips, chips)
            for side, ref in enumerate((mine, theirs)):
                place = (2 * source + (core if side == 0 else 1 - core)) * rows
                at = pl.ds(pl.multiple_of(place, rows), rows)
                part = jnp.concatenate([g[at, :] for g in grads[t * pairs : (t + 1) * pairs]], axis=1)
                if t != 1:
                    total = total + jnp.sum(part.astype(F32), axis=0, keepdims=True)
                for s in range(2):
                    which = core if s == 0 else 1 - core
                    whole[s] = whole[s] + dot_tn(part, ref[j * rows : (j + 1) * rows, lanes(which * half, half)])
        for s, out in enumerate((keep, give)):
            out[:, t * cols : (t + 1) * cols, :] = whole[s].astype(LOW).reshape(shards // 2, cols, half)
        if t != 1:
            vec[t // 2 : t // 2 + 1, lanes(core * half, half)] = total
    head, part, slot = layout[0:1, :], layout[1:2, :], layout[2:3, :]
    value = jnp.full((1, half), NEG, F32)
    for p in range(pairs):
        for i in range(2):
            top = jnp.max(tops[p][i * BLK : (i + 1) * BLK, :], axis=0, keepdims=True)
            value = jnp.where(head == core * 2 * pairs + 2 * p + i, top[:, 0:1], value)
    first = value.astype(LOW).astype(F32)
    second = (value - first).astype(LOW).astype(F32)
    third = value - first - second
    value = jnp.where(part == 0, first, jnp.where(part == 1, second, jnp.where(part == 2, third, 0.0)))
    small[...] = jnp.zeros(small.shape, F32)
    device = where[shards + 3]
    value = jnp.where(slot == lax.rem(device, 8), value, 0.0)
    for r in range(devices // 8):
        line = jnp.where(device // 8 == r, value, 0.0)
        for i in range(shards):
            small[i, 4 + r : 5 + r, :] = line
    for i in range(shards):
        for v in range(8):
            at = v % 3 * 128
            small[i, v // 3 : v // 3 + 1, at : at + cols] = vec[v : v + 1, i * cols : (i + 1) * cols]
        unit, at = i * wide // half, i * wide % half
        small[i, 3:4, :wide] = inner_bias[unit : unit + 1, at : at + wide]


def token_grad_kernel(where, *refs, rows, chips, pairs, shards):
    grads, (wh, mine, theirs) = refs[: 3 * pairs], refs[3 * pairs :]
    core, chip = where[shards], where[shards + 1]
    half = mine.shape[1] // 2
    for j in range(chips):
        source = lax.rem(chip - j + chips, chips)
        for side, out in enumerate((mine, theirs)):
            place = (2 * source + (core if side == 0 else 1 - core)) * rows
            at = pl.ds(pl.multiple_of(place, rows), rows)
            parts = [
                jnp.concatenate([g[at, :] for g in grads[t * pairs : (t + 1) * pairs]], axis=1) for t in range(3)
            ]
            for s in range(2):
                which = core if s == 0 else 1 - core
                total = dot_nn(parts[0], wh[s, 0]) + dot_nn(parts[1], wh[s, 1]) + dot_nn(parts[2], wh[s, 2])
                out[j * rows : (j + 1) * rows, lanes(which * half, half)] = total.astype(LOW)


def finish_heads_kernel(where, own, other, limits, wq, wk, *outs, shards, devices, head_dim):
    grads, vectors, (inner, maxima, cut_q, cut_k) = outs[:3], outs[3:11], outs[11:]
    core, shard = where[shards], where[shards + 2]
    half, cols = own.shape[1], wq.shape[0]
    for t, out in enumerate(grads):
        for ref, which in ((own, core), (other, 1 - core)):
            out[:, lanes(which * half, half)] = ref[t * cols : (t + 1) * cols, :].astype(F32)
    small = own[3 * cols :, :].astype(F32) + other[3 * cols :, :].astype(F32)
    for v, out in enumerate(vectors):
        at = v % 3 * 128
        out[...] = small[v // 3 : v // 3 + 1, at : at + cols]
    inner[...] = small[3:4, : inner.shape[1]]
    heads = limits.shape[1]
    value = jnp.full((1, half), NEG, F32)
    for r in range(devices // 8):
        line = jnp.broadcast_to(small[4 + r : 5 + r, :], (8, half))
        line = line + pltpu.roll(line, half - heads, 1) + pltpu.roll(line, half - 2 * heads, 1)
        value = jnp.maximum(value, line)
    step = half // 2
    while step >= 48:
        value = jnp.maximum(value, pltpu.roll(value, step, 1))
        step //= 2
    top = value[0:1, :heads]
    maxima[...] = top
    root = jnp.sqrt(limits[...] / jnp.maximum(top, limits[...]))
    column = lax.broadcasted_iota(jnp.int32, (cols, 1), 0) + shard * cols
    scale = jnp.zeros((cols, 1), F32)
    for h in range(heads):
        inside = (column >= h * head_dim) & (column < (h + 1) * head_dim)
        scale = jnp.where(inside, root[:, h : h + 1], scale)
    cut_q[...] = wq[...] * scale
    cut_k[...] = wk[...] * scale


def finish_rest_kernel(where, own, other, inner, output, outer, *, shards):
    half, cols, wide = own.shape[1], output.shape[0], inner.shape[1]
    unit = eye(half)
    core = where[shards]
    for ref, which in ((own, core), (other, 1 - core)):
        inner[pl.ds(pl.multiple_of(which * half, 128), half), :] = dot_nt(unit, ref[:wide, :])
        output[:, lanes(which * half, half)] = ref[wide : wide + cols, :].astype(F32)
        count = outer.shape[1] // 2 // half
        for j in range(count):
            at = wide + cols * (1 + j)
            outer[:, lanes((which * count + j) * half, half)] = ref[at : at + cols, :].astype(F32)


def dense_kernel(
    where, rest_a, rest_b, rest_c, rest_d, att_own, att_other, tokens, cotangent, vec, bias_inner,
    layer_out, resid, grad_own, grad_other, keep, give, vec_grad, inner_bias_grad,
    packed, low, hidden, normed, inverse, act, slope, acc, outer_grad, sem, *, wide,
):
    shards, half = packed.shape[1], packed.shape[3]
    rows, width = tokens.shape
    cols = width // shards
    core = where[shards]
    copies = []
    for side, pair in enumerate(((rest_a, rest_b), (rest_c, rest_d))):
        at = 0
        for ref in pair:
            for i in range(ref.shape[0]):
                copies.append(pltpu.make_async_copy(ref.at[i], packed.at[side, where[at]], sem.at[side, at]))
                at += 1
    for copy in copies:
        copy.start()
    for copy in copies:
        copy.wait()
    own, other = lanes(core * half, half), lanes((1 - core) * half, half)
    sides = (own, other)
    units = shards * wide // half
    each = half // wide
    step = 128

    def inner_weights(side, u):
        return packed[side, u * each : (u + 1) * each, :wide, :].reshape(half, half)

    def outer_at(u):
        begin = wide + cols * (1 + u % (units // 2))
        return slice(begin, begin + cols)

    def outer_weights(u):
        side = jnp.where(core == u // (units // 2), 0, 1)
        return packed[side, :, outer_at(u), :].reshape(width, half)

    def output_weights(side):
        return packed[side, :, wide : wide + cols, :].reshape(width, half)

    acc[...] = dot_nt(att_own[...], output_weights(0)) + dot_nt(att_other[...], output_weights(1))
    for r in range(0, rows, step):
        at = slice(r, r + step)
        n, inv = normalise(tokens[at, :] + (acc[at, :] + vec[2:3, :]))
        normed[at, :] = n
        inverse[at, :] = inv
        h = n * vec[4:5, :] + vec[5:6, :]
        hidden[at, :] = h
        low[at, :] = h.astype(LOW)

    for u in range(units):
        inner = dot_nt(low[:, own], inner_weights(0, u)) + dot_nt(low[:, other], inner_weights(1, u))
        a, d = gelu_and_slope(inner + bias_inner[u : u + 1, :])
        act[u] = a.astype(LOW)
        slope[u] = d
        product = dot_nt(act[u], outer_weights(u))
        acc[...] = product if u == 0 else acc[...] + product

    sums = [jnp.zeros((1, width), F32)] * 3
    for r in range(0, rows, step):
        at = slice(r, r + step)
        n, inv = normalise(hidden[at, :] + (acc[at, :] + vec[3:4, :]))
        layer_out[at, :] = n * vec[6:7, :] + vec[7:8, :]
        e = cotangent[at, :]
        dv = norm_backward(e, n, inv, vec[6:7, :])
        acc[at, :] = dv
        dl = dv.astype(LOW)
        outer_grad[at, :] = dl
        sums = [
            sums[0] + jnp.sum(dl.astype(F32), axis=0, keepdims=True),
            sums[1] + jnp.sum(e * n, axis=0, keepdims=True),
            sums[2] + jnp.sum(e, axis=0, keepdims=True),
        ]
    vec_grad[3:4, :] = sums[0]
    vec_grad[6:7, :] = sums[1]
    vec_grad[7:8, :] = sums[2]

    turned = outer_grad[...].T
    for u in range(units):
        inner_grad = dot_nn(outer_grad[...], outer_weights(u)) * slope[u]
        inner_low = inner_grad.astype(LOW)
        inner_bias_grad[u : u + 1, :] = jnp.sum(inner_low.astype(F32), axis=0, keepdims=True)
        for side, at in enumerate(sides):
            acc[:, at] += dot_nn(inner_low, inner_weights(side, u))
        inner_turned = inner_low.T
        for out, at in ((keep, own), (give, other)):
            part = dot_nn(inner_turned, low[:, at]).astype(LOW)
            out[u * each : (u + 1) * each, :wide, :] = part.reshape(each, wide, half)
        part = dot_nn(turned, act[u]).astype(LOW).reshape(shards, cols, half)

        @pl.when(core == u // (units // 2))
        def _(u=u, part=part):
            keep[:, outer_at(u), :] = part

        @pl.when(core != u // (units // 2))
        def _(u=u, part=part):
            give[:, outer_at(u), :] = part

    sums = [jnp.zeros((1, width), F32)] * 3
    for r in range(0, rows, step):
        at = slice(r, r + step)
        e, n = acc[at, :], normed[at, :]
        dv = norm_backward(e, n, inverse[at, :], vec[4:5, :])
        resid[at, :] = dv
        dl = dv.astype(LOW)
        outer_grad[at, :] = dl
        sums = [
            sums[0] + jnp.sum(dl.astype(F32), axis=0, keepdims=True),
            sums[1] + jnp.sum(e * n, axis=0, keepdims=True),
            sums[2] + jnp.sum(e, axis=0, keepdims=True),
        ]
    vec_grad[0:2, :] = jnp.zeros((2, width), F32)
    vec_grad[2:3, :] = sums[0]
    vec_grad[4:5, :] = sums[1]
    vec_grad[5:6, :] = sums[2]
    grad_own[...] = dot_nn(outer_grad[...], output_weights(0)).astype(LOW)
    grad_other[...] = dot_nn(outer_grad[...], output_weights(1)).astype(LOW)
    turned = outer_grad[...].T
    for out, ref in ((keep, att_own), (give, att_other)):
        part = dot_nn(turned, ref[...]).astype(LOW)
        out[:, wide : wide + cols, :] = part.reshape(shards, cols, half)


def ring_kernel(where, *refs, counts, kind, cut):
    refs = list(refs)
    parts = []
    for count in counts:
        total = refs.pop(0)[0].astype(F32)
        for _ in range(count - 1):
            total = total + refs.pop(0)[0].astype(F32)
        parts.append(total)
    if kind == "first":
        up, down = refs
        up[...] = parts[0][:cut].astype(LOW)
        down[...] = parts[0][cut:].astype(LOW)
    elif kind == "second":
        above, below, up, down = refs
        up[:cut, :] = (parts[0][:cut] + above[...].astype(F32)).astype(LOW)
        up[cut:, :] = parts[0][cut:].astype(LOW)
        down[:cut, :] = parts[1][:cut].astype(LOW)
        down[cut:, :] = (parts[1][cut:] + below[...].astype(F32)).astype(LOW)
    elif kind == "later":
        above, below, up, down = refs
        up[...] = (parts[0] + above[...].astype(F32)).astype(LOW)
        down[...] = (parts[1] + below[...].astype(F32)).astype(LOW)
    else:
        above, below, out = refs
        out[...] = (parts[0] + above[...].astype(F32) + below[...].astype(F32)).astype(LOW)


def ring_step(where, arrays, slots, received, kind, cut):
    rows, half = arrays[0].shape[1:]
    specs = [
        pl.BlockSpec((1, rows, half), lambda i, where, slot=slot: (where[slot], 0, 0)) for slot in slots for _ in arrays
    ]
    specs += [pl.BlockSpec(a.shape, lambda i, where: (0, 0)) for a in received]
    shapes = [(rows, half)] if kind == "last" else [(rows, half)] * 2
    if kind == "first":
        shapes = [(cut, half), (rows - cut, half)]
    return pl.pallas_call(
        functools.partial(ring_kernel, counts=[len(arrays)] * len(slots), kind=kind, cut=cut),
        grid_spec=pltpu.PrefetchScalarGridSpec(
            num_scalar_prefetch=1,
            grid=(1,),
            in_specs=specs,
            out_specs=[pl.BlockSpec(s, lambda i, where: (0, 0)) for s in shapes],
        ),
        out_shape=[struct(s) for s in shapes],
        compiler_params=pltpu.CompilerParams(vmem_limit_bytes=32 << 20),
        cost_estimate=pl.CostEstimate(flops=10**9, bytes_accessed=1 << 18, transcendentals=0),
        name="ring_" + kind,
    )(where, *[a for _ in slots for a in arrays], *received)


class Moves:
    def __init__(self, ctx, wshard):
        self.ctx, self.wshard, self.chips = ctx, wshard, ctx // 2
        self.half = half = wshard // 2
        order = list(range(0, wshard, 2)) + list(range(wshard - 1, 0, -2))
        self.up_perm = [(order[i], order[(i + 1) % wshard]) for i in range(wshard)]
        self.down_perm = [(b, a) for a, b in self.up_perm]
        deltas = [0]
        for step in range(1, half):
            deltas += [-step, step]
        deltas.append(half)
        sums = [half]
        for step in range(half - 1, 0, -1):
            sums += [step, -step]
        sums.append(0)
        table = []
        for c in range(ctx):
            for w in range(wshard):
                at = order.index(w)
                goes = [order[(at + d) % wshard] for d in sums]
                placed = [(s // half != c % 2) * half + s % half for s in goes]
                table.append(
                    [order[(at + d) % wshard] for d in deltas] + [c % 2, c // 2, w, c * wshard + w] + goes + placed
                )
        self.sums, self.placed = wshard + 4, wshard + 4 + len(sums)
        here = lax.axis_index("ctx") * wshard + lax.axis_index("wshard")
        table = jnp.asarray(table, jnp.int32)
        self.where = lax.dynamic_slice(table, (here, 0), (1, table.shape[1]), allow_negative_indices=False)[0]

    def up(self, value):
        return lax.ppermute(value, "wshard", self.up_perm)

    def down(self, value):
        return lax.ppermute(value, "wshard", self.down_perm)

    def swap(self, value):
        return lax.ppermute(value, "ctx", [(c, c ^ 1) for c in range(self.ctx)])

    def chip_shift(self, value, j):
        return lax.ppermute(value, "ctx", [(c, (c + 2 * j) % self.ctx) for c in range(self.ctx)])

    def chip_flip(self, value, bit):
        return lax.ppermute(value, "ctx", [(c, c ^ (2 * bit)) for c in range(self.ctx)])

    def gather(self, piece, cut):
        above = below = piece
        pieces = [piece]
        for _ in range(1, self.half):
            above, below = self.up(above), self.down(below)
            pieces += [above, below]
            turn = yield pieces
            if turn is not None:
                above, below = after((above, below), turn)
        pieces.append(jnp.concatenate([self.up(above[:cut]), self.down(below[cut:])], axis=0))
        yield pieces

    def scatter(self, step, cut):
        up, down = step("first", [0], [])
        yield up
        for s in range(self.half - 1):
            above, below = self.up(up), self.down(down)
            up, down = step("second" if s == 0 else "later", [1 + 2 * s, 2 + 2 * s], [above, below])
            yield up
        above, below = self.up(up), self.down(down)
        [total] = step("last", [2 * self.half - 1], [above, below])
        yield total

    def chip_sum(self, value):
        bit = 1
        while bit < self.chips:
            other = self.chip_flip(value, bit)
            value = (value.astype(F32) + other.astype(F32)).astype(LOW)
            bit *= 2
        return value


def slot_lists(first, count, nblocks, glob, random_rows, heads):
    blocks = first + jnp.arange(count, dtype=jnp.int32)
    offsets = jnp.arange(-1, 2, dtype=jnp.int32)
    start = jnp.clip(blocks - 1, 0, nblocks - 3)
    window = start[:, None] + jnp.arange(3, dtype=jnp.int32)[None, :]
    near = jnp.abs(window - blocks[:, None]) <= 1
    slide = jnp.clip(blocks[:, None] + offsets[None, :], 0, nblocks - 1)
    spread = lambda a: jnp.broadcast_to(a[:, None, :], (count, heads, a.shape[-1]))
    rest = jnp.concatenate(
        [jnp.broadcast_to(glob[None, None, :], (count, heads, glob.shape[0])), random_rows], axis=2
    )
    lists = jnp.concatenate([spread(slide), rest], axis=2)
    slots = lists.shape[2]
    equal = lists[..., :, None] == lists[..., None, :]
    earlier = jnp.arange(slots)[:, None] < jnp.arange(slots)[None, :]
    fresh = jnp.logical_not(jnp.any(equal & earlier[None, None], axis=-2))
    on = jnp.concatenate([spread(near), fresh[..., 3:]], axis=2)
    index = jnp.concatenate([spread(window), rest], axis=2)
    return index, jnp.where(on, index, nblocks)


def struct(shape, dtype=LOW):
    return jax.ShapeDtypeStruct(tuple(shape), dtype)


def after(value, *others):
    return lax.optimization_barrier((value,) + others)[0]


def per_device(ctx, wshard, layer_input, segments, global_blocks, random_blocks, thresholds, w_query, w_key, w_value, w_output, w_inner, w_outer, query_bias, value_bias, output_bias, inner_bias, outer_bias, gain_attn, shift_attn, gain_mlp, shift_mlp, out_grad):
    m = Moves(ctx, wshard)
    chips, where, devices = m.chips, m.where, ctx * wshard
    tokens = layer_input[0]
    rows_here, width = tokens.shape
    seg_all = segments[0]
    length = seg_all.shape[0]
    glob = global_blocks[0]
    heads = thresholds.shape[0]
    head_dim = width // heads
    nblocks = length // BLK
    count = 2 * rows_here // BLK
    half = width // 2
    own_heads = heads // 2
    pairs = own_heads // 2
    cols, wide = w_query.shape[1], w_inner.shape[1]
    units = wide * wshard // half
    sizes = dict(shards=wshard, rows=rows_here, chips=chips)

    small_least = 4 + devices // 8
    head_rows = -(-(3 * cols + 4) // 16) * 16
    vectors = (query_bias, value_bias, output_bias, outer_bias, gain_attn, shift_attn, gain_mlp, shift_mlp, inner_bias)
    head_piece = simple_call(
        functools.partial(pack_heads_kernel, shards=wshard),
        struct((head_rows, half)),
        (w_query.T, w_key.T, w_value.T, jnp.concatenate(vectors)[None]),
        (where,),
        "pack_heads",
        1,
        scratch=[pltpu.VMEM((head_rows - 3 * cols, half), F32)],
    )
    inputs_low = tokens.astype(LOW)
    mine = jnp.concatenate([inputs_low] + [m.chip_shift(inputs_low, j) for j in range(1, chips)], axis=0)
    theirs = m.swap(mine)
    *_, head_pieces = m.gather(head_piece, head_rows // 2 // 16 * 16)
    got = jnp.stack(head_pieces)
    passed = m.swap(got)
    query, key, value, head_weights, vec, bias_inner = simple_call(
        functools.partial(project_kernel, rows=rows_here, chips=chips, cols=cols, wide=wide),
        [struct((length, half))] * 3
        + [struct((2, 3, half, half)), struct((8, width), F32), struct((units, half), F32)],
        (got, passed, mine, theirs),
        (where,),
        "project",
        10,
        scratch=[pltpu.VMEM((2, wshard, head_rows, half), LOW), pltpu.SemaphoreType.DMA((2, wshard))],
        anywhere=2,
        limit=40,
    )

    rest_rows = wide + 5 * cols
    rest_cut = rest_rows // 2 // 16 * 16
    rest_piece = simple_call(
        functools.partial(pack_rest_kernel, shards=wshard),
        struct((rest_rows, half)),
        (w_inner, w_output.T, w_outer.T),
        (where,),
        "pack_rest",
        1,
    )
    rest_piece = after(rest_piece, passed, theirs)
    gather = m.gather(rest_piece, rest_cut)
    gathered = next(gather)

    chip, core = where[wshard + 1], where[wshard]
    random_own = lax.dynamic_slice(
        random_blocks,
        (chip * count, core * own_heads, 0),
        (count, own_heads, random_blocks.shape[2]),
        allow_negative_indices=False,
    )
    index, active = slot_lists(chip * count, count, nblocks, glob, random_own, own_heads)
    seg_rep = seg_all.reshape(nblocks, BLK)
    seg_rep = jnp.concatenate([seg_rep, seg_rep], axis=1)
    seg_rep = jnp.concatenate([seg_rep, jnp.full((8, 2 * BLK), -1, jnp.int32)], axis=0)
    scalars = (index.reshape(-1), active.reshape(-1), glob, where)
    seg_args = (seg_all[:, None], seg_rep, seg_all[None, :])
    done = []
    gathered = gather.send(query)
    for pair in range(pairs):
        q = after(query, gathered[-1]) if pair else query
        done.append(attend(*scalars, q, key, value, *seg_args, count, own_heads, pair, wshard))
        if len(gathered) < wshard:
            gathered = gather.send(done[-1][4])
    while len(gathered) < wshard:
        gathered = next(gather)
    early, late = jnp.stack(gathered[:-3]), jnp.stack(gathered[-3:])
    rest = (early, late, m.swap(early), m.swap(late))
    attended_glob = jnp.concatenate([d[2] for d in done], axis=1)
    glob_rows = [attended_glob] + [m.chip_shift(attended_glob, j) for j in range(1, chips)]
    att_own, att_give = simple_call(
        functools.partial(merge_kernel, **sizes),
        [struct((rows_here, half))] * 2,
        tuple(d[0] for d in done) + tuple(glob_rows),
        (where, glob),
        "merge",
        1,
    )
    att_other = m.swap(att_give)

    big = lambda *shape: pltpu.VMEM(shape, F32)
    low = lambda *shape: pltpu.VMEM(shape, LOW)
    layer_output, resid_one, grad_own, grad_other, keep, give, vec_grad, inner_bias_grad = (
        simple_call(
            functools.partial(dense_kernel, wide=wide),
            [struct((rows_here, width), F32)] * 2
            + [struct((rows_here, half))] * 2
            + [struct((wshard, rest_rows, half))] * 2
            + [struct((8, width), F32), struct((units, half), F32)],
            rest + (att_own, att_other, tokens, out_grad[0], vec, bias_inner),
            (where,),
            "dense",
            40,
            scratch=[
                low(2, wshard, rest_rows, half),
                low(rows_here, width),
                big(rows_here, width),
                big(rows_here, width),
                big(rows_here, 1),
                low(units, rows_here, half),
                big(units, rows_here, half),
                big(rows_here, width),
                low(rows_here, width),
                pltpu.SemaphoreType.DMA((2, wshard)),
            ],
            anywhere=4,
            limit=60,
        )
    )

    from_other = m.swap(grad_other)
    given = m.swap(after(give, from_other))
    heads_grad, *glob_sends = simple_call(
        functools.partial(spread_kernel, **sizes),
        [struct((2 * rows_here, half))] + [struct((BLK, half))] * chips,
        (grad_own, from_other),
        (where, glob),
        "spread",
        1,
    )
    glob_grads = [glob_sends[0]] + [m.chip_shift(glob_sends[j], j) for j in range(1, chips)]

    def ring_of(arrays, cut, base):
        def step(kind, slots, received):
            return ring_step(where, arrays, [base + s for s in slots], received, kind, cut)

        return m.scatter(step, cut)

    ring = ring_of([keep, given], rest_cut, m.sums)
    turn = ()
    pulled = []
    for pair in range(pairs):
        q = after(query, *turn) if turn else query
        pulled.append(
            pull(*scalars, q, key, value, heads_grad, glob_grads, done[pair][1], done[pair][3], own_heads, pair, wshard)
        )
        turn = (next(ring),)
    grads = tuple(pulled[pair][t] for t in range(3) for pair in range(pairs))
    dense_cost = 7
    small_rows = -(-(3 * cols + small_least) // 16) * 16 - 3 * cols
    lane = [i % 48 for i in range(half)]
    layout = jnp.asarray(
        [[i % heads if i < 3 * heads else -1 for i in lane], [i // heads for i in lane], [i // 48 for i in range(half)]],
        jnp.int32,
    )
    layout = jnp.concatenate([layout, jnp.zeros((5, half), jnp.int32)], axis=0)
    part_mine, part_theirs = simple_call(
        functools.partial(token_grad_kernel, pairs=pairs, **sizes),
        [struct((chips * rows_here, width))] * 2,
        grads + (head_weights,),
        (where,),
        "token_grad",
        dense_cost,
    )
    passed_theirs = m.swap(part_theirs)
    turn = (next(ring),)
    grads = after(grads, *turn)
    head_keep, head_give, small_parts = simple_call(
        functools.partial(weight_grad_kernel, pairs=pairs, cols=cols, wide=wide, devices=devices, **sizes),
        [struct((wshard // 2, 3 * cols, half))] * 2 + [struct((wshard, small_rows, half), F32)],
        grads + tuple(d[4] for d in done) + (mine, theirs, vec_grad, inner_bias_grad, layout),
        (where,),
        "weight_grad",
        dense_cost,
        scratch=[big(8, width)],
    )
    head_given = m.swap(head_give)
    summed = part_mine.astype(F32) + passed_theirs.astype(F32)
    summed = summed.reshape(chips, rows_here, width)
    sent = [summed[j].astype(LOW) for j in range(1, chips)]
    input_grad = resid_one + summed[0]
    for j in range(1, chips):
        input_grad = input_grad + m.chip_shift(sent[j - 1], chips - j).astype(F32)

    head_parts = jnp.concatenate([head_keep, head_given], axis=0)
    *_, total = ring
    head_parts = [after(head_parts, total, *sent)]

    def head_step(kind, slots, received):
        return head_ring_step(where, head_parts[0], small_parts, m, slots, received, kind)

    head_ring = m.scatter(head_step, None)
    next(head_ring)
    next(head_ring)
    head_parts[0] = after(head_parts[0], input_grad)
    *_, head_tail = head_ring
    rest_tail = m.chip_sum(total)
    grad_inner, grad_output, grad_outer = simple_call(
        functools.partial(finish_rest_kernel, shards=wshard),
        [struct(w_inner.shape, F32), struct(w_output.shape[::-1], F32), struct(w_outer.shape[::-1], F32)],
        (rest_tail, m.swap(rest_tail)),
        (where,),
        "finish_rest",
        2,
    )
    head_tail = m.chip_sum(head_tail)
    vector, turned = struct((1, cols), F32), struct((cols, width), F32)
    finished = simple_call(
        functools.partial(finish_heads_kernel, shards=wshard, devices=devices, head_dim=head_dim),
        [turned] * 3 + [vector] * 8 + [struct((1, wide), F32), struct((1, heads), F32), turned, turned],
        (head_tail, m.swap(head_tail), thresholds[None], w_query.T, w_key.T),
        (where,),
        "finish_heads",
        2,
    )
    grad_query, grad_key, grad_value = finished[:3]
    vector_out = [v[0] for v in finished[3:11]]
    inner_out, maxima, clipped_query, clipped_key = finished[11][0], finished[12][0], finished[13], finished[14]

    return (
        layer_output[None],
        input_grad[None],
        grad_query.T,
        grad_key.T,
        grad_value.T,
        grad_output.T,
        grad_inner,
        grad_outer.T,
        vector_out[0],
        vector_out[1],
        vector_out[2],
        inner_out,
        vector_out[3],
        vector_out[4],
        vector_out[5],
        vector_out[6],
        vector_out[7],
        clipped_query.T,
        clipped_key.T,
        maxima,
    )


def head_ring_kernel(where, *refs, kind, targets, cut):
    refs = list(refs)
    parts = []
    for _ in range(targets):
        part, small = refs.pop(0), refs.pop(0)
        parts.append(jnp.concatenate([part[0].astype(F32), small[0]], axis=0))
    if kind == "first":
        up, down = refs
        up[...] = parts[0][:cut].astype(LOW)
        down[...] = parts[0][cut:].astype(LOW)
    elif kind == "second":
        above, below, up, down = refs
        up[:cut, :] = (parts[0][:cut] + above[...].astype(F32)).astype(LOW)
        up[cut:, :] = parts[0][cut:].astype(LOW)
        down[:cut, :] = parts[1][:cut].astype(LOW)
        down[cut:, :] = (parts[1][cut:] + below[...].astype(F32)).astype(LOW)
    elif kind == "later":
        above, below, up, down = refs
        up[...] = (parts[0] + above[...].astype(F32)).astype(LOW)
        down[...] = (parts[1] + below[...].astype(F32)).astype(LOW)
    else:
        above, below, out = refs
        out[...] = (parts[0] + above[...].astype(F32) + below[...].astype(F32)).astype(LOW)


def head_ring_step(where, parts, small, m, slots, received, kind):
    half = parts.shape[2]
    rows = parts.shape[1] + small.shape[1]
    cut = rows // 2 // 16 * 16
    specs, args = [], []
    for slot in slots:
        specs.append(
            pl.BlockSpec((1,) + parts.shape[1:], lambda i, where, at=m.placed + slot: (where[at], 0, 0))
        )
        specs.append(pl.BlockSpec((1,) + small.shape[1:], lambda i, where, at=m.sums + slot: (where[at], 0, 0)))
        args += [parts, small]
    specs += [pl.BlockSpec(a.shape, lambda i, where: (0, 0)) for a in received]
    shapes = [(rows, half)] if kind == "last" else [(rows, half)] * 2
    if kind == "first":
        shapes = [(cut, half), (rows - cut, half)]
    return pl.pallas_call(
        functools.partial(head_ring_kernel, kind=kind, targets=len(slots), cut=cut),
        grid_spec=pltpu.PrefetchScalarGridSpec(
            num_scalar_prefetch=1,
            grid=(1,),
            in_specs=specs,
            out_specs=[pl.BlockSpec(s, lambda i, where: (0, 0)) for s in shapes],
        ),
        out_shape=[struct(s) for s in shapes],
        compiler_params=pltpu.CompilerParams(vmem_limit_bytes=32 << 20),
        cost_estimate=pl.CostEstimate(flops=10**9, bytes_accessed=1 << 18, transcendentals=0),
        name="head_ring_" + kind,
    )(where, *args, *received)


def solution(mesh):
    tokens = P("wshard", "ctx", None)
    sequence = P("wshard", None)
    matrix = P(None, "wshard")
    vector = P("wshard")
    in_specs = (tokens, sequence, sequence, P(), P()) + (matrix,) * 6 + (vector,) * 9 + (tokens,)
    out_specs = (tokens, tokens) + (matrix,) * 6 + (vector,) * 9 + (matrix, matrix, P())
    return jax.shard_map(
        functools.partial(per_device, mesh.shape["ctx"], mesh.shape["wshard"]),
        mesh=mesh,
        in_specs=in_specs,
        out_specs=out_specs,
        check_vma=False,
    )
```

```python
import functools

import jax
import jax.numpy as jnp
from jax import lax
from jax.experimental import pallas as pl
from jax.experimental.pallas import tpu as pltpu
from jax.sharding import PartitionSpec as P

BLK = 64
EPSILON = 1e-05
NEG = -1e30
UNROLL = 4
LOW = jnp.bfloat16
F32 = jnp.float32


def dot_nn(left, right):
    return lax.dot_general(left, right, (((1,), (0,)), ((), ())), preferred_element_type=F32)


def dot_tn(left, right):
    return lax.dot_general(left, right, (((0,), (0,)), ((), ())), preferred_element_type=F32)


def dot_nt(left, right):
    return lax.dot_general(left, right, (((1,), (1,)), ((), ())), preferred_element_type=F32)


def normalise(values):
    centre = values - jnp.mean(values, axis=-1, keepdims=True)
    inverse = lax.rsqrt(jnp.mean(centre * centre, axis=-1, keepdims=True) + EPSILON)
    return centre * inverse, inverse


def norm_backward(upstream, normed, inverse, gain):
    scaled = upstream * gain
    mean_one = jnp.mean(scaled, axis=-1, keepdims=True)
    mean_two = jnp.mean(scaled * normed, axis=-1, keepdims=True)
    return inverse * (scaled - mean_one - normed * mean_two)


def gelu_and_slope(v):
    c = 0.7978845608028654
    k = c * 0.044715
    square = v * v
    t = jnp.tanh(v * (c + k * square))
    half = 0.5 + 0.5 * t
    return v * half, half + (half - half * t) * (v * (c + 3 * k * square))


def global_of(glob, number):
    block = glob[jnp.minimum(number, glob.shape[0] - 1)]
    on = number < glob.shape[0]
    for i in range(glob.shape[0]):
        on = on & ((i >= number) | (glob[i] != block))
    return block, on


def in_global(glob, place):
    found = glob[0] == place
    for i in range(1, glob.shape[0]):
        found = found | (glob[i] == place)
    return found


def halves():
    lane = lax.broadcasted_iota(jnp.int32, (BLK, 2 * BLK), 1)
    return lane < BLK


def stack_pair(tile):
    low = jnp.where(halves(), 1.0, 0.0).astype(tile.dtype)
    high = jnp.where(halves(), 0.0, 1.0).astype(tile.dtype)
    return jnp.concatenate([tile * low, tile * high], axis=0)


def unstack_pair(rows):
    return jnp.where(halves(), rows[:BLK], rows[BLK:])


def rows_of(ref, block, count=1):
    return ref[pl.ds(pl.multiple_of(block * BLK, BLK), count * BLK), :]


def shared_rows(ref, index, base):
    return jnp.concatenate([rows_of(ref, index[base], 3), rows_of(ref, index[base + 3])], axis=0)


def own_rows(ref, index, base):
    return jnp.concatenate([rows_of(ref, index[base + j]) for j in range(4, 8)], axis=0)


def attend_kernel(index, active, glob, where, q_ref, k_ref, v_ref, seg_q, seg_k, seg_row, o_ref, p_ref, og_ref, pg_ref, top_ref, score, *, heads, pair, shards, blocks):
    chip = where[shards + 1]
    my_glob, my_on = global_of(glob, chip)
    step = pl.program_id(0)
    wide = lax.broadcasted_iota(jnp.int32, (1, 2 * BLK), 1) < BLK
    length = k_ref.shape[0]

    @pl.when(step == 0)
    def _():
        top_ref[...] = jnp.full(top_ref.shape, NEG, F32)

        @pl.when(jnp.logical_not(my_on))
        def _():
            og_ref[...] = jnp.zeros(og_ref.shape, og_ref.dtype)
            pg_ref[...] = jnp.zeros(pg_ref.shape, pg_ref.dtype)

        @pl.when(my_on)
        def _():
            place = my_glob
            q2 = stack_pair(rows_of(q_ref, place))
            sq = rows_of(seg_q, place)
            sq = jnp.concatenate([sq, sq], axis=0)
            top = jnp.full((2 * BLK, 1), NEG, F32)
            cut = 512
            for j in range(length // cut):
                raw = dot_nt(q2, k_ref[j * cut : (j + 1) * cut, :])
                raw = jnp.where(seg_row[:, j * cut : (j + 1) * cut] == sq, raw, NEG)
                score[:, j * cut : (j + 1) * cut] = raw
                top = jnp.maximum(top, jnp.max(raw, axis=1, keepdims=True))
            total = jnp.zeros((2 * BLK, 1), F32)
            for j in range(length // cut):
                power = jnp.exp(score[:, j * cut : (j + 1) * cut] - top)
                score[:, j * cut : (j + 1) * cut] = power
                total = total + jnp.sum(power, axis=1, keepdims=True)
            scale = 1.0 / total
            acc = jnp.zeros((2 * BLK, 2 * BLK), F32)
            for j in range(length // cut):
                prob = (score[:, j * cut : (j + 1) * cut] * scale).astype(LOW)
                pg_ref[:, j * cut : (j + 1) * cut] = prob
                acc = acc + dot_nn(prob, v_ref[j * cut : (j + 1) * cut, :])
            og_ref[...] = unstack_pair(acc).astype(LOW)
            top_ref[...] = jnp.maximum(top_ref[...], jnp.broadcast_to(top, top_ref.shape))

    for u in range(UNROLL):
        b = step * UNROLL + u
        place = chip * blocks + b
        q2 = stack_pair(rows_of(q_ref, place))
        sq = rows_of(seg_q, place)
        sq = jnp.concatenate([sq, sq], axis=0)
        base = (b * heads + 2 * pair) * 8
        shared = dot_nt(q2, shared_rows(k_ref, index, base))
        own = jnp.concatenate(
            [dot_nt(q2[h * BLK : (h + 1) * BLK], own_rows(k_ref, index, base + 8 * h)) for h in range(2)],
            axis=0,
        )

        def seg_of(at, j):
            first = seg_k[pl.ds(active[at + j], 1), :]
            second = seg_k[pl.ds(active[at + j + 1], 1), :]
            return jnp.where(wide, first, second)

        raw_s = jnp.where(jnp.concatenate([seg_of(base, 0), seg_of(base, 2)], axis=1) == sq, shared, NEG)
        seg_own = [
            jnp.broadcast_to(
                jnp.concatenate([seg_of(base + 8 * h, 4), seg_of(base + 8 * h, 6)], axis=1), (BLK, 4 * BLK)
            )
            for h in range(2)
        ]
        raw_o = jnp.where(jnp.concatenate(seg_own, axis=0) == sq, own, NEG)
        top = jnp.maximum(jnp.max(raw_s, axis=1, keepdims=True), jnp.max(raw_o, axis=1, keepdims=True))
        power_s = jnp.exp(raw_s - top)
        power_o = jnp.exp(raw_o - top)
        scale = 1.0 / (jnp.sum(power_s, axis=1, keepdims=True) + jnp.sum(power_o, axis=1, keepdims=True))
        prob_s = (power_s * scale).astype(LOW)
        prob_o = (power_o * scale).astype(LOW)
        p_ref[u, :, : 4 * BLK] = prob_s
        p_ref[u, :, 4 * BLK :] = prob_o
        out = dot_nn(prob_s, shared_rows(v_ref, index, base))
        out = out + jnp.concatenate(
            [
                dot_nn(prob_o[h * BLK : (h + 1) * BLK], own_rows(v_ref, index, base + 8 * h))
                for h in range(2)
            ],
            axis=0,
        )
        o_ref[u * BLK : (u + 1) * BLK, :] = unstack_pair(out).astype(LOW)
        used = jnp.where(in_global(glob, place), jnp.full_like(top, NEG), top)
        top_ref[...] = jnp.maximum(top_ref[...], jnp.broadcast_to(used, top_ref.shape))


def pull_kernel(index, active, glob, where, q_ref, k_ref, v_ref, do_ref, p_ref, pg_ref, *refs, heads, pair, shards, blocks):
    *dog_refs, dq_ref, dk_ref, dv_ref, dk, dv, score = refs
    chip = where[shards + 1]
    my_glob, my_on = global_of(glob, chip)
    del active
    step = pl.program_id(0)
    steps = pl.num_programs(0)
    length = k_ref.shape[0]

    @pl.when(step == 0)
    def _():
        dk[...] = jnp.zeros(dk.shape, F32)
        dv[...] = jnp.zeros(dv.shape, F32)
        dq_ref[...] = jnp.zeros(dq_ref.shape, dq_ref.dtype)

    def add(ref, block, value):
        at = pl.ds(pl.multiple_of(block * BLK, BLK), value.shape[0])
        ref[at, :] += value

    for u in range(UNROLL):
        b = step * UNROLL + u
        place = chip * blocks + b
        q2 = stack_pair(rows_of(q_ref, place))
        keep = jnp.where(in_global(glob, place), 0.0, 1.0).astype(LOW)
        do2 = stack_pair(do_ref[u * BLK : (u + 1) * BLK, :] * keep)
        base = (b * heads + 2 * pair) * 8
        ks = shared_rows(k_ref, index, base)
        ko = [own_rows(k_ref, index, base + 8 * h) for h in range(2)]
        vs = shared_rows(v_ref, index, base)
        vo = [own_rows(v_ref, index, base + 8 * h) for h in range(2)]
        prob_s = p_ref[u, :, : 4 * BLK]
        prob_o = p_ref[u, :, 4 * BLK :]
        dp_s = dot_nt(do2, vs)
        dp_o = jnp.concatenate([dot_nt(do2[h * BLK : (h + 1) * BLK], vo[h]) for h in range(2)], axis=0)
        ps = prob_s.astype(F32)
        po = prob_o.astype(F32)
        ts = ps * dp_s
        to = po * dp_o
        total = jnp.sum(ts, axis=1, keepdims=True) + jnp.sum(to, axis=1, keepdims=True)
        ds_s = (ts - ps * total).astype(LOW)
        ds_o = (to - po * total).astype(LOW)
        dq = dot_nn(ds_s, ks) + jnp.concatenate(
            [dot_nn(ds_o[h * BLK : (h + 1) * BLK], ko[h]) for h in range(2)], axis=0
        )
        at = pl.ds(pl.multiple_of(place * BLK, BLK), BLK)
        dq_ref[at, :] = (unstack_pair(dq) * 0.125).astype(LOW)
        dks = dot_tn(ds_s, q2)
        dvs = dot_tn(prob_s, do2)
        add(dk, index[base], dks[: 3 * BLK])
        add(dk, index[base + 3], dks[3 * BLK :])
        add(dv, index[base], dvs[: 3 * BLK])
        add(dv, index[base + 3], dvs[3 * BLK :])
        for h in range(2):
            part = slice(h * BLK, (h + 1) * BLK)
            dko = dot_tn(ds_o[part], q2[part])
            dvo = dot_tn(prob_o[part], do2[part])
            for j in range(4):
                add(dk, index[base + 8 * h + 4 + j], dko[j * BLK : (j + 1) * BLK])
                add(dv, index[base + 8 * h + 4 + j], dvo[j * BLK : (j + 1) * BLK])

    @pl.when((step == steps - 1) & my_on)
    def _():
        place = my_glob
        q2 = stack_pair(rows_of(q_ref, place))
        dog = dog_refs[0][...].astype(F32)
        for ref in dog_refs[1:]:
            dog = dog + ref[...].astype(F32)
        do2 = stack_pair(dog.astype(LOW))
        cut = 512
        total = jnp.zeros((2 * BLK, 1), F32)
        for j in range(length // cut):
            part = slice(j * cut, (j + 1) * cut)
            dp = dot_nt(do2, v_ref[part, :])
            score[:, part] = dp
            total = total + jnp.sum(pg_ref[:, part].astype(F32) * dp, axis=1, keepdims=True)
        acc = jnp.zeros((2 * BLK, 2 * BLK), F32)
        for j in range(length // cut):
            part = slice(j * cut, (j + 1) * cut)
            prob = pg_ref[:, part]
            ds = (prob.astype(F32) * (score[:, part] - total)).astype(LOW)
            acc = acc + dot_nn(ds, k_ref[part, :])
            dk[part, :] += dot_tn(ds, q2)
            dv[part, :] += dot_tn(prob, do2)
        at = pl.ds(pl.multiple_of(place * BLK, BLK), BLK)
        dq_ref[at, :] = (unstack_pair(acc) * 0.125).astype(LOW)

    @pl.when(step == steps - 1)
    def _():
        dk_ref[...] = dk[...].astype(LOW)
        dv_ref[...] = dv[...].astype(LOW)


def attend(index, active, glob, where, query, key, value, seg_col, seg_rep, seg_row, blocks, heads, pair, shards):
    length = key.shape[0]
    column = pl.BlockSpec((length, 2 * BLK), lambda s, *_: (0, pair))
    whole = lambda shape: pl.BlockSpec(shape, lambda s, *_: (0,) * len(shape))
    grid = pltpu.PrefetchScalarGridSpec(
        num_scalar_prefetch=4,
        grid=(blocks // UNROLL,),
        in_specs=[column, column, column, whole(seg_col.shape), whole(seg_rep.shape), whole(seg_row.shape)],
        out_specs=[
            pl.BlockSpec((UNROLL * BLK, 2 * BLK), lambda s, *_: (s, 0)),
            pl.BlockSpec((UNROLL, 2 * BLK, 8 * BLK), lambda s, *_: (s, 0, 0)),
            whole((BLK, 2 * BLK)),
            whole((2 * BLK, length)),
            whole((2 * BLK, 2 * BLK)),
        ],
        scratch_shapes=[pltpu.VMEM((2 * BLK, length), F32)],
    )
    work = (blocks * 8 + length // BLK) * 2 * BLK * BLK
    return pl.pallas_call(
        functools.partial(attend_kernel, heads=heads, pair=pair, shards=shards, blocks=blocks),
        grid_spec=grid,
        out_shape=[
            jax.ShapeDtypeStruct((blocks * BLK, 2 * BLK), LOW),
            jax.ShapeDtypeStruct((blocks, 2 * BLK, 8 * BLK), LOW),
            jax.ShapeDtypeStruct((BLK, 2 * BLK), LOW),
            jax.ShapeDtypeStruct((2 * BLK, length), LOW),
            jax.ShapeDtypeStruct((2 * BLK, 2 * BLK), F32),
        ],
        compiler_params=pltpu.CompilerParams(vmem_limit_bytes=32 << 20),
        cost_estimate=pl.CostEstimate(flops=work * 8192, bytes_accessed=27 << 20, transcendentals=0),
        name="attend",
    )(index, active, glob, where, query, key, value, seg_col, seg_rep, seg_row)


def pull(index, active, glob, where, query, key, value, grad, grad_glob, probs, probs_glob, heads, pair, shards):
    length = key.shape[0]
    blocks = grad.shape[0] // BLK
    column = pl.BlockSpec((length, 2 * BLK), lambda s, *_: (0, pair))
    whole = lambda shape: pl.BlockSpec(shape, lambda s, *_: (0,) * len(shape))
    grid = pltpu.PrefetchScalarGridSpec(
        num_scalar_prefetch=4,
        grid=(blocks // UNROLL,),
        in_specs=[
            column,
            column,
            column,
            pl.BlockSpec((UNROLL * BLK, 2 * BLK), lambda s, *_: (s, pair)),
            pl.BlockSpec((UNROLL, 2 * BLK, 8 * BLK), lambda s, *_: (s, 0, 0)),
            whole((2 * BLK, length)),
        ]
        + [pl.BlockSpec((BLK, 2 * BLK), lambda s, *_: (0, pair))] * len(grad_glob),
        out_specs=[whole((length, 2 * BLK))] * 3,
        scratch_shapes=[
            pltpu.VMEM((length, 2 * BLK), F32),
            pltpu.VMEM((length, 2 * BLK), F32),
            pltpu.VMEM((2 * BLK, length), F32),
        ],
    )
    work = (blocks * 8 + length // BLK) * 2 * BLK * BLK
    return pl.pallas_call(
        functools.partial(pull_kernel, heads=heads, pair=pair, shards=shards, blocks=blocks),
        grid_spec=grid,
        out_shape=[jax.ShapeDtypeStruct((length, 2 * BLK), LOW)] * 3,
        compiler_params=pltpu.CompilerParams(vmem_limit_bytes=32 << 20),
        cost_estimate=pl.CostEstimate(flops=work * 8192, bytes_accessed=30 << 20, transcendentals=0),
        name="pull",
    )(index, active, glob, where, query, key, value, grad, probs, probs_glob, *grad_glob)


def eye(size):
    row = lax.broadcasted_iota(jnp.int32, (size, size), 0)
    column = lax.broadcasted_iota(jnp.int32, (size, size), 1)
    return jnp.where(row == column, 1.0, 0.0).astype(LOW)


def lanes(start, size):
    return pl.ds(pl.multiple_of(start, 128), size)


def simple_call(kernel, out_shape, args, scalars, name, cost, scratch=(), anywhere=0, limit=32, away=()):
    many = isinstance(out_shape, list)
    smem = pl.BlockSpec(memory_space=pltpu.SMEM)
    vmem = pl.BlockSpec(memory_space=pltpu.VMEM)
    free = pl.BlockSpec(memory_space=pl.ANY)
    specs = [smem] * len(scalars) + [free] * anywhere + [vmem] * (len(args) - anywhere)
    return pl.pallas_call(
        kernel,
        in_specs=specs,
        out_specs=[free if i in away else vmem for i in range(len(out_shape))] if many else vmem,
        out_shape=out_shape,
        scratch_shapes=list(scratch),
        compiler_params=pltpu.CompilerParams(vmem_limit_bytes=limit << 20),
        cost_estimate=pl.CostEstimate(flops=cost * 10**9, bytes_accessed=cost * 3 << 20, transcendentals=0),
        name=name,
    )(*scalars, *args)


def pack_heads_kernel(where, wq, wk, wv, *refs, shards):
    vectors, out, rows_ref = refs
    half, cols = wq.shape[1] // 2, wq.shape[0]
    here = lanes(where[shards] * half, half)
    for i, ref in enumerate((wq, wk, wv)):
        out[i * cols : (i + 1) * cols, :] = ref[:, here].astype(LOW)
    rows_ref[...] = jnp.zeros(rows_ref.shape, F32)
    for v in range(8):
        at = v % 3 * 128
        rows_ref[v // 3 : v // 3 + 1, at : at + cols] = vectors[:, v * cols : (v + 1) * cols]
    rows_ref[3:4, : vectors.shape[1] - 8 * cols] = vectors[:, 8 * cols :]
    out[3 * cols :, :] = rows_ref[...].astype(LOW)


def pack_rest_kernel(where, inner, output, outer, out, *, shards):
    half, cols = output.shape[1] // 2, output.shape[0]
    core = where[shards]
    rows = inner[pl.ds(pl.multiple_of(core * half, 128), half), :].astype(LOW)
    wide = inner.shape[1]
    out[:wide, :] = rows if wide == half else dot_nt(eye(wide), rows).astype(LOW)
    out[wide : wide + cols, :] = output[:, lanes(core * half, half)].astype(LOW)
    count = outer.shape[1] // 2 // half
    for j in range(count):
        at = wide + cols * (1 + j)
        out[at : at + cols, :] = outer[:, lanes((core * count + j) * half, half)].astype(LOW)


def project_kernel(
    where, got, passed, mine, theirs, q_ref, k_ref, v_ref, wh, vec, bias_inner, pieces, sem, *, rows, chips, cols, wide
):
    shards, width = pieces.shape[0], pieces.shape[2]
    half = width // 2
    core, chip = where[shards], where[shards + 1]
    copies = []
    for side, ref in enumerate((got, passed)):
        at = lanes((core if side == 0 else 1 - core) * half, half)
        for i in range(shards):
            copies.append(pltpu.make_async_copy(ref.at[i], pieces.at[where[i], :, at], sem.at[side, i]))
    for copy in copies:
        copy.start()
    for copy in copies:
        copy.wait()
    for t in range(3):
        part = pieces[pl.ds(core * (shards // 2), shards // 2), t * cols : (t + 1) * cols, :]
        wh[t * half : (t + 1) * half, :] = part.reshape(half, width)
    for i in range(shards):
        small = pieces[i, 3 * cols :, :half].astype(F32)
        for v in range(8):
            at = v % 3 * 128
            vec[v : v + 1, i * cols : (i + 1) * cols] = small[v // 3 : v // 3 + 1, at : at + cols]
        unit, at = i * wide // half, i * wide % half
        bias_inner[unit : unit + 1, at : at + wide] = small[3:4, :wide]
    own_lanes = lanes(core * half, half)
    bias_query, bias_value = vec[0:1, own_lanes], vec[1:2, own_lanes]
    for j in range(chips):
        source = lax.rem(chip - j + chips, chips)
        for side, ref in enumerate((mine, theirs)):
            place = (2 * source + (core if side == 0 else 1 - core)) * rows
            at = pl.ds(pl.multiple_of(place, rows), rows)
            value = dot_nt(ref[j * rows : (j + 1) * rows, :], wh[...])
            query = (value[:, :half] + bias_query).astype(LOW).astype(F32) * 0.125
            q_ref[at, :] = query.astype(LOW)
            k_ref[at, :] = value[:, half : 2 * half].astype(LOW)
            v_ref[at, :] = (value[:, 2 * half :] + bias_value).astype(LOW)


def merge_kernel(where, glob, *refs, shards, chips, rows):
    outs = refs[-2:]
    parts, globs = refs[: -2 - chips], refs[-2 - chips : -2]
    core, chip = where[shards], where[shards + 1]
    full = jnp.concatenate
    for side, out in enumerate(outs):
        start = (core if side == 0 else 1 - core) * rows
        out[...] = full([p[pl.ds(pl.multiple_of(start, rows), rows), :] for p in parts], axis=1)
    per = 2 * rows // BLK
    for j in range(chips):
        number = lax.rem(chip - j + chips, chips)
        block, on = global_of(glob, number)
        local = block - chip * per
        for side, out in enumerate(outs):
            start = local - (core if side == 0 else 1 - core) * (per // 2)

            @pl.when(on & (start >= 0) & (start < per // 2))
            def _(out=out, start=start, j=j):
                out[pl.ds(pl.multiple_of(start * BLK, BLK), BLK), :] = globs[j][...]


def spread_kernel(where, glob, own, other, heads_grad, *sends, shards, chips, rows):
    core, chip = where[shards], where[shards + 1]
    heads_grad[pl.ds(pl.multiple_of(core * rows, rows), rows), :] = own[...]
    heads_grad[pl.ds(pl.multiple_of((1 - core) * rows, rows), rows), :] = other[...]
    per = 2 * rows // BLK
    for j, send in enumerate(sends):
        number = lax.rem(chip + j, chips)
        block, on = global_of(glob, number)
        local = block - chip * per
        send[...] = jnp.zeros(send.shape, send.dtype)

        @pl.when(on & (local >= 0) & (local < per))
        def _(send=send, local=local):
            send[...] = heads_grad[pl.ds(pl.multiple_of(local * BLK, BLK), BLK), :]


def head_grads_kernel(
    where, *refs, rows, chips, pairs, cols, wide, shards, devices
):
    grads = refs[: 3 * pairs]
    tops = refs[3 * pairs : 4 * pairs]
    mine, theirs, wh, vec_grad, inner_bias, layout, keep, give, small, part_mine, part_theirs, vec, both = refs[4 * pairs :]
    core, chip = where[shards], where[shards + 1]
    half = mine.shape[1] // 2
    for j in range(chips):
        source = lax.rem(chip - j + chips, chips)
        for side, out in enumerate((part_mine, part_theirs)):
            place = (2 * source + (core if side == 0 else 1 - core)) * rows
            at = pl.ds(pl.multiple_of(place, rows), rows)
            part = jnp.concatenate([g[at, :] for g in grads], axis=1)
            out[j * rows : (j + 1) * rows, :] = dot_nn(part, wh[...]).astype(LOW)
    vec[...] = vec_grad[...]
    vec[0:2, :] = jnp.zeros((2, vec.shape[1]), F32)
    for t in range(3):
        whole = None
        total = jnp.zeros((1, half), F32)
        for j in range(chips):
            source = lax.rem(chip - j + chips, chips)
            for side, ref in enumerate((mine, theirs)):
                place = (2 * source + (core if side == 0 else 1 - core)) * rows
                at = pl.ds(pl.multiple_of(place, rows), rows)
                part = jnp.concatenate([g[at, :] for g in grads[t * pairs : (t + 1) * pairs]], axis=1)
                if t != 1:
                    total = total + jnp.sum(part.astype(F32), axis=0, keepdims=True)
                product = dot_tn(part, ref[j * rows : (j + 1) * rows, :])
                whole = product if whole is None else whole + product
        here = slice(t * cols, (t + 1) * cols)
        both[...] = whole.astype(LOW).reshape(shards // 2, cols, 2 * half)
        keep[:, here, :] = both[:, :, lanes(core * half, half)]
        give[:, here, :] = both[:, :, lanes((1 - core) * half, half)]
        if t != 1:
            vec[t // 2 : t // 2 + 1, lanes(core * half, half)] = total
    head, part, slot = layout[0:1, :], layout[1:2, :], layout[2:3, :]
    value = jnp.full((1, half), NEG, F32)
    for p in range(pairs):
        for i in range(2):
            top = jnp.max(tops[p][i * BLK : (i + 1) * BLK, :], axis=0, keepdims=True)
            value = jnp.where(head == core * 2 * pairs + 2 * p + i, top[:, 0:1], value)
    first = value.astype(LOW).astype(F32)
    second = (value - first).astype(LOW).astype(F32)
    third = value - first - second
    value = jnp.where(part == 0, first, jnp.where(part == 1, second, jnp.where(part == 2, third, 0.0)))
    small[...] = jnp.zeros(small.shape, F32)
    device = where[shards + 3]
    value = jnp.where(slot == lax.rem(device, 8), value, 0.0)
    for r in range(devices // 8):
        line = jnp.where(device // 8 == r, value, 0.0)
        for i in range(shards):
            small[i, 4 + r : 5 + r, :] = line
    for i in range(shards):
        for v in range(8):
            at = v % 3 * 128
            small[i, v // 3 : v // 3 + 1, at : at + cols] = vec[v : v + 1, i * cols : (i + 1) * cols]
        unit, at = i * wide // half, i * wide % half
        small[i, 3:4, :wide] = inner_bias[unit : unit + 1, at : at + wide]


def finish_heads_kernel(where, own, other, limits, wq, wk, *outs, shards, devices, head_dim):
    grads, vectors, (inner, maxima, cut_q, cut_k) = outs[:3], outs[3:11], outs[11:]
    core, shard = where[shards], where[shards + 2]
    half, cols = own.shape[1], wq.shape[0]
    for t, out in enumerate(grads):
        for ref, which in ((own, core), (other, 1 - core)):
            out[:, lanes(which * half, half)] = ref[t * cols : (t + 1) * cols, :].astype(F32)
    small = own[3 * cols :, :].astype(F32) + other[3 * cols :, :].astype(F32)
    for v, out in enumerate(vectors):
        at = v % 3 * 128
        out[...] = small[v // 3 : v // 3 + 1, at : at + cols]
    inner[...] = small[3:4, : inner.shape[1]]
    heads = limits.shape[1]
    value = jnp.full((1, half), NEG, F32)
    for r in range(devices // 8):
        line = jnp.broadcast_to(small[4 + r : 5 + r, :], (8, half))
        line = line + pltpu.roll(line, half - heads, 1) + pltpu.roll(line, half - 2 * heads, 1)
        value = jnp.maximum(value, line)
    step = half // 2
    while step >= 48:
        value = jnp.maximum(value, pltpu.roll(value, step, 1))
        step //= 2
    top = value[0:1, :heads]
    maxima[...] = top
    root = jnp.sqrt(limits[...] / jnp.maximum(top, limits[...]))
    column = lax.broadcasted_iota(jnp.int32, (cols, 1), 0) + shard * cols
    scale = jnp.zeros((cols, 1), F32)
    for h in range(heads):
        inside = (column >= h * head_dim) & (column < (h + 1) * head_dim)
        scale = jnp.where(inside, root[:, h : h + 1], scale)
    cut_q[...] = wq[...] * scale
    cut_k[...] = wk[...] * scale


def finish_rest_kernel(where, own, other, inner, output, outer, *, shards):
    half, cols, wide = own.shape[1], output.shape[0], inner.shape[1]
    core = where[shards]
    for ref, which in ((own, core), (other, 1 - core)):
        rows = ref[:wide, :]
        inner[pl.ds(pl.multiple_of(which * half, 128), half), :] = (
            rows.astype(F32) if wide == half else dot_nt(eye(half), rows)
        )
        output[:, lanes(which * half, half)] = ref[wide : wide + cols, :].astype(F32)
        count = outer.shape[1] // 2 // half
        for j in range(count):
            at = wide + cols * (1 + j)
            outer[:, lanes((which * count + j) * half, half)] = ref[at : at + cols, :].astype(F32)


def dense_kernel(
    where, early, late, early_other, late_other, att_own, att_other, tokens, cotangent, vec, bias_inner,
    layer_out, resid, grad_own, grad_other, keep, give, vec_grad, inner_bias_grad,
    inner_w, rest_w, att, low, normed, inverse, act, slope, acc, outer_grad, inner_g, rest_g, sem, out_sem,
    *, wide,
):
    shards, _, width = rest_w.shape
    rows, half = tokens.shape[0], width // 2
    cols = width // shards
    core = where[shards]
    natural = wide == half
    lead = wide if natural else 0
    rest_copies, inner_copies = [], []
    for side, pair in enumerate(((early, late), (early_other, late_other))):
        which = core if side == 0 else 1 - core
        at = 0
        for ref in pair:
            for i in range(ref.shape[0]):
                shard = where[at]
                rest_copies.append(
                    pltpu.make_async_copy(
                        ref.at[i, pl.ds(lead, ref.shape[1] - lead), :],
                        rest_w.at[shard, :, lanes(which * half, half)],
                        sem.at[0, side, at],
                    )
                )
                if natural:
                    inner_copies.append(
                        pltpu.make_async_copy(
                            ref.at[i, pl.ds(0, wide), :],
                            inner_w.at[pl.ds(pl.multiple_of(which * half, 128), half), lanes(shard * wide, wide)],
                            sem.at[1, side, at],
                        )
                    )
                at += 1
    for copy in rest_copies + inner_copies:
        copy.start()
    groups = act.shape[0]
    each = half // wide
    begin = 0 if natural else wide
    step = 128

    def inner_weights(g):
        if natural:
            return jnp.concatenate([inner_w[:, u * half : (u + 1) * half] for u in (g, g + groups)], axis=1)
        parts = [rest_w[u * each : (u + 1) * each, :wide, :].reshape(half, width) for u in (g, g + groups)]
        return jnp.concatenate(parts, axis=0)

    def outer_weights(g):
        at = begin + cols * (1 + g)
        return rest_w[:, at : at + cols, :].reshape(width, width)

    def output_weights():
        return rest_w[:, begin : begin + cols, :].reshape(width, width)

    sends = []

    def send(pairs):
        for source, target in pairs:
            copy = pltpu.make_async_copy(source, target, out_sem.at[len(sends)])
            copy.start()
            sends.append(copy)

    def send_rest(at, source_at, count, shard_from=0, shard_count=shards):
        which = pl.ds(shard_from, shard_count)
        send(
            (rest_g.at[which, pl.ds(source_at, count), here], target.at[which, pl.ds(at, count), :])
            for here, target in ((lanes(core * half, half), keep), (lanes((1 - core) * half, half), give))
        )

    att[:, lanes(core * half, half)] = att_own[...]
    att[:, lanes((1 - core) * half, half)] = att_other[...]
    for copy in rest_copies:
        copy.wait()
    acc[...] = dot_nt(att[...], output_weights())
    for r in range(0, rows, step):
        at = slice(r, r + step)
        n, inv = normalise(tokens[at, :] + (acc[at, :] + vec[2:3, :]))
        normed[at, :] = n
        inverse[at, :] = inv
        low[at, :] = (n * vec[4:5, :] + vec[5:6, :]).astype(LOW)
    for copy in inner_copies:
        copy.wait()

    for g in range(groups):
        product = (dot_nn if natural else dot_nt)(low[...], inner_weights(g))
        bias = jnp.concatenate([bias_inner[u : u + 1, :] for u in (g, g + groups)], axis=1)
        a, d = gelu_and_slope(product + bias)
        act[g] = a.astype(LOW)
        slope[g] = d.astype(LOW)
        product = dot_nt(act[g], outer_weights(g))
        acc[...] = product if g == 0 else acc[...] + product

    sums = [jnp.zeros((1, width), F32)] * 3
    for r in range(0, rows, step):
        at = slice(r, r + step)
        hidden = normed[at, :] * vec[4:5, :] + vec[5:6, :]
        n, inv = normalise(hidden + (acc[at, :] + vec[3:4, :]))
        layer_out[at, :] = n * vec[6:7, :] + vec[7:8, :]
        e = cotangent[at, :]
        dv = norm_backward(e, n, inv, vec[6:7, :])
        acc[at, :] = dv
        dl = dv.astype(LOW)
        outer_grad[at, :] = dl
        sums = [
            sums[0] + jnp.sum(dl.astype(F32), axis=0, keepdims=True),
            sums[1] + jnp.sum(e * n, axis=0, keepdims=True),
            sums[2] + jnp.sum(e, axis=0, keepdims=True),
        ]
    vec_grad[3:4, :] = sums[0]
    vec_grad[6:7, :] = sums[1]
    vec_grad[7:8, :] = sums[2]

    turned = outer_grad[...].T
    low_turned = low[...].T
    for g in range(groups):
        at = begin + cols * (1 + g)
        rest_g[:, at : at + cols, :] = dot_nn(turned, act[g]).astype(LOW).reshape(shards, cols, width)
        send_rest(at + lead, at, cols)
        inner_low = (dot_nn(outer_grad[...], outer_weights(g)) * slope[g].astype(F32)).astype(LOW)
        bias = jnp.sum(inner_low.astype(F32), axis=0, keepdims=True)
        inner_bias_grad[g : g + 1, :] = bias[:, :half]
        inner_bias_grad[g + groups : g + groups + 1, :] = bias[:, half:]
        acc[...] += (dot_nt if natural else dot_nn)(inner_low, inner_weights(g))
        if natural:
            part = dot_nn(low_turned, inner_low).astype(LOW)
            for i, u in enumerate((g, g + groups)):
                here = slice(i * half, (i + 1) * half)
                inner_g[0, u] = part[:half, here]
                inner_g[1, u] = part[half:, here]
                send(
                    (inner_g.at[which, u], target.at[u, pl.ds(0, wide), :])
                    for which, target in ((core, keep), (1 - core, give))
                )
        else:
            part = dot_nn(inner_low.T, low[...]).astype(LOW)
            for i, u in enumerate((g, g + groups)):
                block = part[i * half : (i + 1) * half].reshape(each, wide, width)
                rest_g[u * each : (u + 1) * each, :wide, :] = block
                send_rest(0, 0, wide, u * each, each)

    sums = [jnp.zeros((1, width), F32)] * 3
    for r in range(0, rows, step):
        at = slice(r, r + step)
        e, n = acc[at, :], normed[at, :]
        dv = norm_backward(e, n, inverse[at, :], vec[4:5, :])
        resid[at, :] = dv
        dl = dv.astype(LOW)
        outer_grad[at, :] = dl
        sums = [
            sums[0] + jnp.sum(dl.astype(F32), axis=0, keepdims=True),
            sums[1] + jnp.sum(e * n, axis=0, keepdims=True),
            sums[2] + jnp.sum(e, axis=0, keepdims=True),
        ]
    vec_grad[0:2, :] = jnp.zeros((2, width), F32)
    vec_grad[2:3, :] = sums[0]
    vec_grad[4:5, :] = sums[1]
    vec_grad[5:6, :] = sums[2]
    low[...] = dot_nn(outer_grad[...], output_weights()).astype(LOW)
    grad_own[...] = low[:, lanes(core * half, half)]
    grad_other[...] = low[:, lanes((1 - core) * half, half)]
    part = dot_nn(outer_grad[...].T, att[...]).astype(LOW).reshape(shards, cols, width)
    rest_g[:, begin : begin + cols, :] = part
    send_rest(begin + lead, begin, cols)
    for copy in sends:
        copy.wait()


def ring_kernel(where, *refs, counts, kind, cut):
    refs = list(refs)
    parts = []
    for count in counts:
        total = refs.pop(0)[0].astype(F32)
        for _ in range(count - 1):
            total = total + refs.pop(0)[0].astype(F32)
        parts.append(total)
    if kind == "first":
        up, down = refs
        up[...] = parts[0][:cut].astype(LOW)
        down[...] = parts[0][cut:].astype(LOW)
    elif kind == "second":
        above, below, up, down = refs
        up[:cut, :] = (parts[0][:cut] + above[...].astype(F32)).astype(LOW)
        up[cut:, :] = parts[0][cut:].astype(LOW)
        down[:cut, :] = parts[1][:cut].astype(LOW)
        down[cut:, :] = (parts[1][cut:] + below[...].astype(F32)).astype(LOW)
    elif kind == "later":
        above, below, up, down = refs
        up[...] = (parts[0] + above[...].astype(F32)).astype(LOW)
        down[...] = (parts[1] + below[...].astype(F32)).astype(LOW)
    else:
        above, below, out = refs
        out[...] = (parts[0] + above[...].astype(F32) + below[...].astype(F32)).astype(LOW)


def ring_step(where, arrays, slots, received, kind, cut):
    rows, half = arrays[0].shape[1:]
    specs = [
        pl.BlockSpec((1, rows, half), lambda i, where, slot=slot: (where[slot], 0, 0)) for slot in slots for _ in arrays
    ]
    specs += [pl.BlockSpec(a.shape, lambda i, where: (0, 0)) for a in received]
    shapes = [(rows, half)] if kind == "last" else [(rows, half)] * 2
    if kind == "first":
        shapes = [(cut, half), (rows - cut, half)]
    return pl.pallas_call(
        functools.partial(ring_kernel, counts=[len(arrays)] * len(slots), kind=kind, cut=cut),
        grid_spec=pltpu.PrefetchScalarGridSpec(
            num_scalar_prefetch=1,
            grid=(1,),
            in_specs=specs,
            out_specs=[pl.BlockSpec(s, lambda i, where: (0, 0)) for s in shapes],
        ),
        out_shape=[struct(s) for s in shapes],
        compiler_params=pltpu.CompilerParams(vmem_limit_bytes=32 << 20),
        cost_estimate=pl.CostEstimate(flops=10**9, bytes_accessed=3 << 20, transcendentals=0),
        name="ring_" + kind,
    )(where, *[a for _ in slots for a in arrays], *received)


class Moves:
    def __init__(self, ctx, wshard):
        self.ctx, self.wshard, self.chips = ctx, wshard, ctx // 2
        self.half = half = wshard // 2
        order = list(range(0, wshard, 2)) + list(range(wshard - 1, 0, -2))
        self.up_perm = [(order[i], order[(i + 1) % wshard]) for i in range(wshard)]
        self.down_perm = [(b, a) for a, b in self.up_perm]
        deltas = [0]
        for step in range(1, half):
            deltas += [-step, step]
        deltas.append(half)
        sums = [half]
        for step in range(half - 1, 0, -1):
            sums += [step, -step]
        sums.append(0)
        table = []
        for c in range(ctx):
            for w in range(wshard):
                at = order.index(w)
                goes = [order[(at + d) % wshard] for d in sums]
                placed = [(s // half != c % 2) * half + s % half for s in goes]
                table.append(
                    [order[(at + d) % wshard] for d in deltas] + [c % 2, c // 2, w, c * wshard + w] + goes + placed
                )
        self.sums, self.placed = wshard + 4, wshard + 4 + len(sums)
        here = lax.axis_index("ctx") * wshard + lax.axis_index("wshard")
        table = jnp.asarray(table, jnp.int32)
        self.where = lax.dynamic_slice(table, (here, 0), (1, table.shape[1]), allow_negative_indices=False)[0]

    def up(self, value):
        return lax.ppermute(value, "wshard", self.up_perm)

    def down(self, value):
        return lax.ppermute(value, "wshard", self.down_perm)

    def swap(self, value):
        return lax.ppermute(value, "ctx", [(c, c ^ 1) for c in range(self.ctx)])

    def chip_shift(self, value, j):
        return lax.ppermute(value, "ctx", [(c, (c + 2 * j) % self.ctx) for c in range(self.ctx)])

    def chip_flip(self, value, bit):
        return lax.ppermute(value, "ctx", [(c, c ^ (2 * bit)) for c in range(self.ctx)])

    def gather(self, piece, cut):
        above = below = piece
        pieces = [piece]
        for _ in range(1, self.half):
            above, below = self.up(above), self.down(below)
            pieces += [above, below]
            turn = yield pieces
            if turn is not None:
                above, below = after((above, below), turn)
        pieces.append(jnp.concatenate([self.up(above[:cut]), self.down(below[cut:])], axis=0))
        yield pieces

    def scatter(self, step, cut):
        up, down = step("first", [0], [])
        yield up
        for s in range(self.half - 1):
            above, below = self.up(up), self.down(down)
            up, down = step("second" if s == 0 else "later", [1 + 2 * s, 2 + 2 * s], [above, below])
            yield up
        above, below = self.up(up), self.down(down)
        [total] = step("last", [2 * self.half - 1], [above, below])
        yield total

    def chip_sum(self, value):
        bit = 1
        while bit < self.chips:
            other = self.chip_flip(value, bit)
            value = (value.astype(F32) + other.astype(F32)).astype(LOW)
            bit *= 2
        return value


def slot_lists(first, count, nblocks, glob, random_rows, heads):
    blocks = first + jnp.arange(count, dtype=jnp.int32)
    offsets = jnp.arange(-1, 2, dtype=jnp.int32)
    start = jnp.clip(blocks - 1, 0, nblocks - 3)
    window = start[:, None] + jnp.arange(3, dtype=jnp.int32)[None, :]
    near = jnp.abs(window - blocks[:, None]) <= 1
    slide = jnp.clip(blocks[:, None] + offsets[None, :], 0, nblocks - 1)
    spread = lambda a: jnp.broadcast_to(a[:, None, :], (count, heads, a.shape[-1]))
    rest = jnp.concatenate(
        [jnp.broadcast_to(glob[None, None, :], (count, heads, glob.shape[0])), random_rows], axis=2
    )
    lists = jnp.concatenate([spread(slide), rest], axis=2)
    slots = lists.shape[2]
    equal = lists[..., :, None] == lists[..., None, :]
    earlier = jnp.arange(slots)[:, None] < jnp.arange(slots)[None, :]
    fresh = jnp.logical_not(jnp.any(equal & earlier[None, None], axis=-2))
    on = jnp.concatenate([spread(near), fresh[..., 3:]], axis=2)
    index = jnp.concatenate([spread(window), rest], axis=2)
    return index, jnp.where(on, index, nblocks)


def struct(shape, dtype=LOW):
    return jax.ShapeDtypeStruct(tuple(shape), dtype)


def after(value, *others):
    return lax.optimization_barrier((value,) + others)[0]


def per_device(ctx, wshard, layer_input, segments, global_blocks, random_blocks, thresholds, w_query, w_key, w_value, w_output, w_inner, w_outer, query_bias, value_bias, output_bias, inner_bias, outer_bias, gain_attn, shift_attn, gain_mlp, shift_mlp, out_grad):
    m = Moves(ctx, wshard)
    chips, where, devices = m.chips, m.where, ctx * wshard
    tokens = layer_input[0]
    rows_here, width = tokens.shape
    seg_all = segments[0]
    length = seg_all.shape[0]
    glob = global_blocks[0]
    heads = thresholds.shape[0]
    head_dim = width // heads
    nblocks = length // BLK
    count = 2 * rows_here // BLK
    half = width // 2
    own_heads = heads // 2
    pairs = own_heads // 2
    cols, wide = w_query.shape[1], w_inner.shape[1]
    units = wide * wshard // half
    sizes = dict(shards=wshard, rows=rows_here, chips=chips)

    small_least = 4 + devices // 8
    head_rows = -(-(3 * cols + 4) // 16) * 16
    vectors = (query_bias, value_bias, output_bias, outer_bias, gain_attn, shift_attn, gain_mlp, shift_mlp, inner_bias)
    head_piece = simple_call(
        functools.partial(pack_heads_kernel, shards=wshard),
        struct((head_rows, half)),
        (w_query.T, w_key.T, w_value.T, jnp.concatenate(vectors)[None]),
        (where,),
        "pack_heads",
        1,
        scratch=[pltpu.VMEM((head_rows - 3 * cols, half), F32)],
    )
    inputs_low = tokens.astype(LOW)
    mine = jnp.concatenate([inputs_low] + [m.chip_shift(inputs_low, j) for j in range(1, chips)], axis=0)
    theirs = m.swap(mine)
    *_, head_pieces = m.gather(head_piece, head_rows // 2 // 16 * 16)
    got = jnp.stack(head_pieces)
    passed = m.swap(got)
    query, key, value, head_weights, vec, bias_inner = simple_call(
        functools.partial(project_kernel, rows=rows_here, chips=chips, cols=cols, wide=wide),
        [struct((length, half))] * 3
        + [struct((3 * half, width)), struct((8, width), F32), struct((units, half), F32)],
        (got, passed, mine, theirs),
        (where,),
        "project",
        10,
        scratch=[pltpu.VMEM((wshard, head_rows, width), LOW), pltpu.SemaphoreType.DMA((2, wshard))],
        anywhere=2,
        limit=40,
    )

    rest_rows = wide + 5 * cols
    rest_cut = rest_rows // 2 // 16 * 16
    rest_piece = simple_call(
        functools.partial(pack_rest_kernel, shards=wshard),
        struct((rest_rows, half)),
        (w_inner, w_output.T, w_outer.T),
        (where,),
        "pack_rest",
        1,
    )
    rest_piece = after(rest_piece, passed, theirs)
    gather = m.gather(rest_piece, rest_cut)
    gathered = next(gather)

    chip, core = where[wshard + 1], where[wshard]
    random_own = lax.dynamic_slice(
        random_blocks,
        (chip * count, core * own_heads, 0),
        (count, own_heads, random_blocks.shape[2]),
        allow_negative_indices=False,
    )
    index, active = slot_lists(chip * count, count, nblocks, glob, random_own, own_heads)
    seg_rep = seg_all.reshape(nblocks, BLK)
    seg_rep = jnp.concatenate([seg_rep, seg_rep], axis=1)
    seg_rep = jnp.concatenate([seg_rep, jnp.full((8, 2 * BLK), -1, jnp.int32)], axis=0)
    scalars = (index.reshape(-1), active.reshape(-1), glob, where)
    seg_args = (seg_all[:, None], seg_rep, seg_all[None, :])
    done = []
    for pair in range(pairs):
        q = after(query, gathered[2 * pair]) if 0 < 2 * pair < len(gathered) else query
        done.append(attend(*scalars, q, key, value, *seg_args, count, own_heads, pair, wshard))
        if len(gathered) < wshard:
            gathered = gather.send(done[-1][4])
    while len(gathered) < wshard:
        gathered = next(gather)
    early, late = jnp.stack(gathered[:-3]), jnp.stack(gathered[-3:])
    rest = (early, late, m.swap(early), m.swap(late))
    attended_glob = jnp.concatenate([d[2] for d in done], axis=1)
    glob_rows = [attended_glob] + [m.chip_shift(attended_glob, j) for j in range(1, chips)]
    att_own, att_give = simple_call(
        functools.partial(merge_kernel, **sizes),
        [struct((rows_here, half))] * 2,
        tuple(d[0] for d in done) + tuple(glob_rows),
        (where, glob),
        "merge",
        1,
    )
    att_other = m.swap(att_give)

    big = lambda *shape: pltpu.VMEM(shape, F32)
    low = lambda *shape: pltpu.VMEM(shape, LOW)
    layer_output, resid_one, grad_own, grad_other, keep, give, vec_grad, inner_bias_grad = (
        simple_call(
            functools.partial(dense_kernel, wide=wide),
            [struct((rows_here, width), F32)] * 2
            + [struct((rows_here, half))] * 2
            + [struct((wshard, rest_rows, half))] * 2
            + [struct((8, width), F32), struct((units, half), F32)],
            rest + (att_own, att_other, tokens, out_grad[0], vec, bias_inner),
            (where,),
            "dense",
            40,
            scratch=[
                low(width, wide * wshard) if wide == half else low(16, 128),
                low(wshard, rest_rows - wide if wide == half else rest_rows, width),
                low(rows_here, width),
                low(rows_here, width),
                big(rows_here, width),
                big(rows_here, 1),
                low(units // 2, rows_here, width),
                low(units // 2, rows_here, width),
                big(rows_here, width),
                low(rows_here, width),
                low(2, units, half, half) if wide == half else low(1, 1, 16, 128),
                low(wshard, rest_rows - wide if wide == half else rest_rows, width),
                pltpu.SemaphoreType.DMA((2, 2, wshard)),
                pltpu.SemaphoreType.DMA((2 * (units + units // 2 + 1),)),
            ],
            anywhere=4,
            away=(4, 5),
            limit=60,
        )
    )

    from_other = m.swap(grad_other)
    given = m.swap(after(give, from_other))
    heads_grad, *glob_sends = simple_call(
        functools.partial(spread_kernel, **sizes),
        [struct((2 * rows_here, half))] + [struct((BLK, half))] * chips,
        (grad_own, from_other),
        (where, glob),
        "spread",
        1,
    )
    glob_grads = [glob_sends[0]] + [m.chip_shift(glob_sends[j], j) for j in range(1, chips)]

    def ring_of(arrays, cut, base):
        def step(kind, slots, received):
            return ring_step(where, arrays, [base + s for s in slots], received, kind, cut)

        return m.scatter(step, cut)

    ring = ring_of([keep, given], rest_cut, m.sums)
    turn = (next(ring),)
    pulled = []
    for pair in range(pairs):
        q = after(query, *turn)
        pulled.append(
            pull(*scalars, q, key, value, heads_grad, glob_grads, done[pair][1], done[pair][3], own_heads, pair, wshard)
        )
        turn = (next(ring),)
    grads = tuple(pulled[pair][t] for t in range(3) for pair in range(pairs))
    small_rows = -(-(3 * cols + small_least) // 16) * 16 - 3 * cols
    lane = [i % 48 for i in range(half)]
    layout = jnp.asarray(
        [[i % heads if i < 3 * heads else -1 for i in lane], [i // heads for i in lane], [i // 48 for i in range(half)]],
        jnp.int32,
    )
    layout = jnp.concatenate([layout, jnp.zeros((5, half), jnp.int32)], axis=0)
    head_keep, head_give, small_parts, part_mine, part_theirs = simple_call(
        functools.partial(head_grads_kernel, pairs=pairs, cols=cols, wide=wide, devices=devices, **sizes),
        [struct((wshard // 2, 3 * cols, half))] * 2
        + [struct((wshard, small_rows, half), F32)]
        + [struct((chips * rows_here, width))] * 2,
        after(grads, *turn) + tuple(d[4] for d in done) + (mine, theirs, head_weights, vec_grad, inner_bias_grad, layout),
        (where,),
        "head_grads",
        12,
        scratch=[big(8, width), low(wshard // 2, cols, width)],
        limit=48,
    )
    passed_theirs = m.swap(part_theirs)
    head_given = m.swap(head_give)
    *_, total = ring
    summed = part_mine.astype(F32) + passed_theirs.astype(F32)
    summed = summed.reshape(chips, rows_here, width)
    sent = [summed[j].astype(LOW) for j in range(1, chips)]
    input_grad = resid_one + summed[0]
    for j in range(1, chips):
        input_grad = input_grad + m.chip_shift(sent[j - 1], chips - j).astype(F32)

    head_parts = jnp.concatenate([head_keep, head_given], axis=0)
    head_parts = [after(head_parts, total, *sent)]

    def head_step(kind, slots, received):
        return head_ring_step(where, head_parts[0], small_parts, m, slots, received, kind)

    head_ring = m.scatter(head_step, None)
    next(head_ring)
    next(head_ring)
    head_parts[0] = after(head_parts[0], input_grad)
    *_, head_tail = head_ring
    rest_tail = m.chip_sum(total)
    grad_inner, grad_output, grad_outer = simple_call(
        functools.partial(finish_rest_kernel, shards=wshard),
        [struct(w_inner.shape, F32), struct(w_output.shape[::-1], F32), struct(w_outer.shape[::-1], F32)],
        (rest_tail, m.swap(rest_tail)),
        (where,),
        "finish_rest",
        2,
    )
    head_tail = m.chip_sum(head_tail)
    vector, turned = struct((1, cols), F32), struct((cols, width), F32)
    finished = simple_call(
        functools.partial(finish_heads_kernel, shards=wshard, devices=devices, head_dim=head_dim),
        [turned] * 3 + [vector] * 8 + [struct((1, wide), F32), struct((1, heads), F32), turned, turned],
        (head_tail, m.swap(head_tail), thresholds[None], w_query.T, w_key.T),
        (where,),
        "finish_heads",
        2,
    )
    grad_query, grad_key, grad_value = finished[:3]
    vector_out = [v[0] for v in finished[3:11]]
    inner_out, maxima, clipped_query, clipped_key = finished[11][0], finished[12][0], finished[13], finished[14]

    return (
        layer_output[None],
        input_grad[None],
        grad_query.T,
        grad_key.T,
        grad_value.T,
        grad_output.T,
        grad_inner,
        grad_outer.T,
        vector_out[0],
        vector_out[1],
        vector_out[2],
        inner_out,
        vector_out[3],
        vector_out[4],
        vector_out[5],
        vector_out[6],
        vector_out[7],
        clipped_query.T,
        clipped_key.T,
        maxima,
    )


def head_ring_kernel(where, *refs, kind, targets, cut):
    refs = list(refs)
    parts = []
    for _ in range(targets):
        part, small = refs.pop(0), refs.pop(0)
        parts.append(jnp.concatenate([part[0].astype(F32), small[0]], axis=0))
    if kind == "first":
        up, down = refs
        up[...] = parts[0][:cut].astype(LOW)
        down[...] = parts[0][cut:].astype(LOW)
    elif kind == "second":
        above, below, up, down = refs
        up[:cut, :] = (parts[0][:cut] + above[...].astype(F32)).astype(LOW)
        up[cut:, :] = parts[0][cut:].astype(LOW)
        down[:cut, :] = parts[1][:cut].astype(LOW)
        down[cut:, :] = (parts[1][cut:] + below[...].astype(F32)).astype(LOW)
    elif kind == "later":
        above, below, up, down = refs
        up[...] = (parts[0] + above[...].astype(F32)).astype(LOW)
        down[...] = (parts[1] + below[...].astype(F32)).astype(LOW)
    else:
        above, below, out = refs
        out[...] = (parts[0] + above[...].astype(F32) + below[...].astype(F32)).astype(LOW)


def head_ring_step(where, parts, small, m, slots, received, kind):
    half = parts.shape[2]
    rows = parts.shape[1] + small.shape[1]
    cut = rows // 2 // 16 * 16
    specs, args = [], []
    for slot in slots:
        specs.append(
            pl.BlockSpec((1,) + parts.shape[1:], lambda i, where, at=m.placed + slot: (where[at], 0, 0))
        )
        specs.append(pl.BlockSpec((1,) + small.shape[1:], lambda i, where, at=m.sums + slot: (where[at], 0, 0)))
        args += [parts, small]
    specs += [pl.BlockSpec(a.shape, lambda i, where: (0, 0)) for a in received]
    shapes = [(rows, half)] if kind == "last" else [(rows, half)] * 2
    if kind == "first":
        shapes = [(cut, half), (rows - cut, half)]
    return pl.pallas_call(
        functools.partial(head_ring_kernel, kind=kind, targets=len(slots), cut=cut),
        grid_spec=pltpu.PrefetchScalarGridSpec(
            num_scalar_prefetch=1,
            grid=(1,),
            in_specs=specs,
            out_specs=[pl.BlockSpec(s, lambda i, where: (0, 0)) for s in shapes],
        ),
        out_shape=[struct(s) for s in shapes],
        compiler_params=pltpu.CompilerParams(vmem_limit_bytes=32 << 20),
        cost_estimate=pl.CostEstimate(flops=10**9, bytes_accessed=3 << 20, transcendentals=0),
        name="head_ring_" + kind,
    )(where, *args, *received)


def solution(mesh):
    tokens = P("wshard", "ctx", None)
    sequence = P("wshard", None)
    matrix = P(None, "wshard")
    vector = P("wshard")
    in_specs = (tokens, sequence, sequence, P(), P()) + (matrix,) * 6 + (vector,) * 9 + (tokens,)
    out_specs = (tokens, tokens) + (matrix,) * 6 + (vector,) * 9 + (matrix, matrix, P())
    return jax.shard_map(
        functools.partial(per_device, mesh.shape["ctx"], mesh.shape["wshard"]),
        mesh=mesh,
        in_specs=in_specs,
        out_specs=out_specs,
        check_vma=False,
    )
```

```python
import functools

import jax
import jax.numpy as jnp
from jax import lax
from jax.experimental import pallas as pl
from jax.experimental.pallas import tpu as pltpu
from jax.sharding import PartitionSpec as P

BLK = 64
EPSILON = 1e-05
NEG = -1e30
UNROLL = 4
LOW = jnp.bfloat16
F32 = jnp.float32


def dot_nn(left, right):
    return lax.dot_general(left, right, (((1,), (0,)), ((), ())), preferred_element_type=F32)


def dot_tn(left, right):
    return lax.dot_general(left, right, (((0,), (0,)), ((), ())), preferred_element_type=F32)


def dot_nt(left, right):
    return lax.dot_general(left, right, (((1,), (1,)), ((), ())), preferred_element_type=F32)


def normalise(values):
    centre = values - jnp.mean(values, axis=-1, keepdims=True)
    inverse = lax.rsqrt(jnp.mean(centre * centre, axis=-1, keepdims=True) + EPSILON)
    return centre * inverse, inverse


def norm_backward(upstream, normed, inverse, gain):
    scaled = upstream * gain
    mean_one = jnp.mean(scaled, axis=-1, keepdims=True)
    mean_two = jnp.mean(scaled * normed, axis=-1, keepdims=True)
    return inverse * (scaled - mean_one - normed * mean_two)


def gelu_and_slope(v):
    c = 0.7978845608028654
    k = c * 0.044715
    square = v * v
    t = jnp.tanh(v * (c + k * square))
    half = 0.5 + 0.5 * t
    return v * half, half + (half - half * t) * (v * (c + 3 * k * square))


def global_of(glob, number):
    block = glob[jnp.minimum(number, glob.shape[0] - 1)]
    on = number < glob.shape[0]
    for i in range(glob.shape[0]):
        on = on & ((i >= number) | (glob[i] != block))
    return block, on


def in_global(glob, place):
    found = glob[0] == place
    for i in range(1, glob.shape[0]):
        found = found | (glob[i] == place)
    return found


def halves():
    lane = lax.broadcasted_iota(jnp.int32, (BLK, 2 * BLK), 1)
    return lane < BLK


def stack_pair(tile):
    low = jnp.where(halves(), 1.0, 0.0).astype(tile.dtype)
    high = jnp.where(halves(), 0.0, 1.0).astype(tile.dtype)
    return jnp.concatenate([tile * low, tile * high], axis=0)


def unstack_pair(rows):
    return jnp.where(halves(), rows[:BLK], rows[BLK:])


def rows_of(ref, block, count=1):
    return ref[pl.ds(pl.multiple_of(block * BLK, BLK), count * BLK), :]


def shared_rows(ref, index, base):
    return jnp.concatenate([rows_of(ref, index[base], 3), rows_of(ref, index[base + 3])], axis=0)


def own_rows(ref, index, base):
    return jnp.concatenate([rows_of(ref, index[base + j]) for j in range(4, 8)], axis=0)


def attend_kernel(index, active, glob, where, q_ref, k_ref, v_ref, seg_q, seg_k, seg_row, o_ref, p_ref, og_ref, pg_ref, top_ref, score, *, heads, pair, shards, blocks):
    chip = where[shards + 1]
    my_glob, my_on = global_of(glob, chip)
    step = pl.program_id(0)
    wide = lax.broadcasted_iota(jnp.int32, (1, 2 * BLK), 1) < BLK
    length = k_ref.shape[0]

    @pl.when(step == 0)
    def _():
        top_ref[...] = jnp.full(top_ref.shape, NEG, F32)

        @pl.when(jnp.logical_not(my_on))
        def _():
            og_ref[...] = jnp.zeros(og_ref.shape, og_ref.dtype)
            pg_ref[...] = jnp.zeros(pg_ref.shape, pg_ref.dtype)

        @pl.when(my_on)
        def _():
            place = my_glob
            q2 = stack_pair(rows_of(q_ref, place))
            sq = rows_of(seg_q, place)
            sq = jnp.concatenate([sq, sq], axis=0)
            top = jnp.full((2 * BLK, 1), NEG, F32)
            cut = 512
            for j in range(length // cut):
                raw = dot_nt(q2, k_ref[j * cut : (j + 1) * cut, :])
                raw = jnp.where(seg_row[:, j * cut : (j + 1) * cut] == sq, raw, NEG)
                score[:, j * cut : (j + 1) * cut] = raw
                top = jnp.maximum(top, jnp.max(raw, axis=1, keepdims=True))
            total = jnp.zeros((2 * BLK, 1), F32)
            for j in range(length // cut):
                power = jnp.exp(score[:, j * cut : (j + 1) * cut] - top)
                score[:, j * cut : (j + 1) * cut] = power
                total = total + jnp.sum(power, axis=1, keepdims=True)
            scale = 1.0 / total
            acc = jnp.zeros((2 * BLK, 2 * BLK), F32)
            for j in range(length // cut):
                prob = (score[:, j * cut : (j + 1) * cut] * scale).astype(LOW)
                pg_ref[:, j * cut : (j + 1) * cut] = prob
                acc = acc + dot_nn(prob, v_ref[j * cut : (j + 1) * cut, :])
            og_ref[...] = unstack_pair(acc).astype(LOW)
            top_ref[...] = jnp.maximum(top_ref[...], jnp.broadcast_to(top, top_ref.shape))

    for u in range(UNROLL):
        b = step * UNROLL + u
        place = chip * blocks + b
        q2 = stack_pair(rows_of(q_ref, place))
        sq = rows_of(seg_q, place)
        sq = jnp.concatenate([sq, sq], axis=0)
        base = (b * heads + 2 * pair) * 8
        shared = dot_nt(q2, shared_rows(k_ref, index, base))
        own = jnp.concatenate(
            [dot_nt(q2[h * BLK : (h + 1) * BLK], own_rows(k_ref, index, base + 8 * h)) for h in range(2)],
            axis=0,
        )

        def seg_of(at, j):
            first = seg_k[pl.ds(active[at + j], 1), :]
            second = seg_k[pl.ds(active[at + j + 1], 1), :]
            return jnp.where(wide, first, second)

        raw_s = jnp.where(jnp.concatenate([seg_of(base, 0), seg_of(base, 2)], axis=1) == sq, shared, NEG)
        seg_own = [
            jnp.broadcast_to(
                jnp.concatenate([seg_of(base + 8 * h, 4), seg_of(base + 8 * h, 6)], axis=1), (BLK, 4 * BLK)
            )
            for h in range(2)
        ]
        raw_o = jnp.where(jnp.concatenate(seg_own, axis=0) == sq, own, NEG)
        top = jnp.maximum(jnp.max(raw_s, axis=1, keepdims=True), jnp.max(raw_o, axis=1, keepdims=True))
        power_s = jnp.exp(raw_s - top)
        power_o = jnp.exp(raw_o - top)
        scale = 1.0 / (jnp.sum(power_s, axis=1, keepdims=True) + jnp.sum(power_o, axis=1, keepdims=True))
        prob_s = (power_s * scale).astype(LOW)
        prob_o = (power_o * scale).astype(LOW)
        p_ref[u, :, : 4 * BLK] = prob_s
        p_ref[u, :, 4 * BLK :] = prob_o
        out = dot_nn(prob_s, shared_rows(v_ref, index, base))
        out = out + jnp.concatenate(
            [
                dot_nn(prob_o[h * BLK : (h + 1) * BLK], own_rows(v_ref, index, base + 8 * h))
                for h in range(2)
            ],
            axis=0,
        )
        o_ref[u * BLK : (u + 1) * BLK, :] = unstack_pair(out).astype(LOW)
        used = jnp.where(in_global(glob, place), jnp.full_like(top, NEG), top)
        top_ref[...] = jnp.maximum(top_ref[...], jnp.broadcast_to(used, top_ref.shape))


def pull_kernel(index, active, glob, where, q_ref, k_ref, v_ref, do_ref, p_ref, pg_ref, *refs, heads, pair, shards, blocks):
    *dog_refs, dq_ref, dk_ref, dv_ref, dk, dv, score = refs
    chip = where[shards + 1]
    my_glob, my_on = global_of(glob, chip)
    del active
    step = pl.program_id(0)
    steps = pl.num_programs(0)
    length = k_ref.shape[0]

    @pl.when(step == 0)
    def _():
        dk[...] = jnp.zeros(dk.shape, F32)
        dv[...] = jnp.zeros(dv.shape, F32)
        dq_ref[...] = jnp.zeros(dq_ref.shape, dq_ref.dtype)

    def add(ref, block, value):
        at = pl.ds(pl.multiple_of(block * BLK, BLK), value.shape[0])
        ref[at, :] += value

    for u in range(UNROLL):
        b = step * UNROLL + u
        place = chip * blocks + b
        q2 = stack_pair(rows_of(q_ref, place))
        keep = jnp.where(in_global(glob, place), 0.0, 1.0).astype(LOW)
        do2 = stack_pair(do_ref[u * BLK : (u + 1) * BLK, :] * keep)
        base = (b * heads + 2 * pair) * 8
        ks = shared_rows(k_ref, index, base)
        ko = [own_rows(k_ref, index, base + 8 * h) for h in range(2)]
        vs = shared_rows(v_ref, index, base)
        vo = [own_rows(v_ref, index, base + 8 * h) for h in range(2)]
        prob_s = p_ref[u, :, : 4 * BLK]
        prob_o = p_ref[u, :, 4 * BLK :]
        dp_s = dot_nt(do2, vs)
        dp_o = jnp.concatenate([dot_nt(do2[h * BLK : (h + 1) * BLK], vo[h]) for h in range(2)], axis=0)
        ps = prob_s.astype(F32)
        po = prob_o.astype(F32)
        ts = ps * dp_s
        to = po * dp_o
        total = jnp.sum(ts, axis=1, keepdims=True) + jnp.sum(to, axis=1, keepdims=True)
        ds_s = (ts - ps * total).astype(LOW)
        ds_o = (to - po * total).astype(LOW)
        dq = dot_nn(ds_s, ks) + jnp.concatenate(
            [dot_nn(ds_o[h * BLK : (h + 1) * BLK], ko[h]) for h in range(2)], axis=0
        )
        at = pl.ds(pl.multiple_of(place * BLK, BLK), BLK)
        dq_ref[at, :] = (unstack_pair(dq) * 0.125).astype(LOW)
        dks = dot_tn(ds_s, q2)
        dvs = dot_tn(prob_s, do2)
        add(dk, index[base], dks[: 3 * BLK])
        add(dk, index[base + 3], dks[3 * BLK :])
        add(dv, index[base], dvs[: 3 * BLK])
        add(dv, index[base + 3], dvs[3 * BLK :])
        for h in range(2):
            part = slice(h * BLK, (h + 1) * BLK)
            dko = dot_tn(ds_o[part], q2[part])
            dvo = dot_tn(prob_o[part], do2[part])
            for j in range(4):
                add(dk, index[base + 8 * h + 4 + j], dko[j * BLK : (j + 1) * BLK])
                add(dv, index[base + 8 * h + 4 + j], dvo[j * BLK : (j + 1) * BLK])

    @pl.when((step == steps - 1) & my_on)
    def _():
        place = my_glob
        q2 = stack_pair(rows_of(q_ref, place))
        dog = dog_refs[0][...].astype(F32)
        for ref in dog_refs[1:]:
            dog = dog + ref[...].astype(F32)
        do2 = stack_pair(dog.astype(LOW))
        cut = 512
        total = jnp.zeros((2 * BLK, 1), F32)
        for j in range(length // cut):
            part = slice(j * cut, (j + 1) * cut)
            dp = dot_nt(do2, v_ref[part, :])
            score[:, part] = dp
            total = total + jnp.sum(pg_ref[:, part].astype(F32) * dp, axis=1, keepdims=True)
        acc = jnp.zeros((2 * BLK, 2 * BLK), F32)
        for j in range(length // cut):
            part = slice(j * cut, (j + 1) * cut)
            prob = pg_ref[:, part]
            ds = (prob.astype(F32) * (score[:, part] - total)).astype(LOW)
            acc = acc + dot_nn(ds, k_ref[part, :])
            dk[part, :] += dot_tn(ds, q2)
            dv[part, :] += dot_tn(prob, do2)
        at = pl.ds(pl.multiple_of(place * BLK, BLK), BLK)
        dq_ref[at, :] = (unstack_pair(acc) * 0.125).astype(LOW)

    @pl.when(step == steps - 1)
    def _():
        dk_ref[...] = dk[...].astype(LOW)
        dv_ref[...] = dv[...].astype(LOW)


def attend(index, active, glob, where, query, key, value, seg_col, seg_rep, seg_row, blocks, heads, pair, shards):
    length = key.shape[0]
    column = pl.BlockSpec((length, 2 * BLK), lambda s, *_: (0, pair))
    whole = lambda shape: pl.BlockSpec(shape, lambda s, *_: (0,) * len(shape))
    grid = pltpu.PrefetchScalarGridSpec(
        num_scalar_prefetch=4,
        grid=(blocks // UNROLL,),
        in_specs=[column, column, column, whole(seg_col.shape), whole(seg_rep.shape), whole(seg_row.shape)],
        out_specs=[
            pl.BlockSpec((UNROLL * BLK, 2 * BLK), lambda s, *_: (s, 0)),
            pl.BlockSpec((UNROLL, 2 * BLK, 8 * BLK), lambda s, *_: (s, 0, 0)),
            whole((BLK, 2 * BLK)),
            whole((2 * BLK, length)),
            whole((2 * BLK, 2 * BLK)),
        ],
        scratch_shapes=[pltpu.VMEM((2 * BLK, length), F32)],
    )
    work = (blocks * 8 + length // BLK) * 2 * BLK * BLK
    return pl.pallas_call(
        functools.partial(attend_kernel, heads=heads, pair=pair, shards=shards, blocks=blocks),
        grid_spec=grid,
        out_shape=[
            jax.ShapeDtypeStruct((blocks * BLK, 2 * BLK), LOW),
            jax.ShapeDtypeStruct((blocks, 2 * BLK, 8 * BLK), LOW),
            jax.ShapeDtypeStruct((BLK, 2 * BLK), LOW),
            jax.ShapeDtypeStruct((2 * BLK, length), LOW),
            jax.ShapeDtypeStruct((2 * BLK, 2 * BLK), F32),
        ],
        compiler_params=pltpu.CompilerParams(vmem_limit_bytes=32 << 20),
        cost_estimate=pl.CostEstimate(flops=work * 8192, bytes_accessed=27 << 20, transcendentals=0),
        name="attend",
    )(index, active, glob, where, query, key, value, seg_col, seg_rep, seg_row)


def pull(index, active, glob, where, query, key, value, grad, grad_glob, probs, probs_glob, heads, pair, shards):
    length = key.shape[0]
    blocks = grad.shape[0] // BLK
    column = pl.BlockSpec((length, 2 * BLK), lambda s, *_: (0, pair))
    whole = lambda shape: pl.BlockSpec(shape, lambda s, *_: (0,) * len(shape))
    grid = pltpu.PrefetchScalarGridSpec(
        num_scalar_prefetch=4,
        grid=(blocks // UNROLL,),
        in_specs=[
            column,
            column,
            column,
            pl.BlockSpec((UNROLL * BLK, 2 * BLK), lambda s, *_: (s, pair)),
            pl.BlockSpec((UNROLL, 2 * BLK, 8 * BLK), lambda s, *_: (s, 0, 0)),
            whole((2 * BLK, length)),
        ]
        + [pl.BlockSpec((BLK, 2 * BLK), lambda s, *_: (0, pair))] * len(grad_glob),
        out_specs=[whole((length, 2 * BLK))] * 3,
        scratch_shapes=[
            pltpu.VMEM((length, 2 * BLK), F32),
            pltpu.VMEM((length, 2 * BLK), F32),
            pltpu.VMEM((2 * BLK, length), F32),
        ],
    )
    work = (blocks * 8 + length // BLK) * 2 * BLK * BLK
    return pl.pallas_call(
        functools.partial(pull_kernel, heads=heads, pair=pair, shards=shards, blocks=blocks),
        grid_spec=grid,
        out_shape=[jax.ShapeDtypeStruct((length, 2 * BLK), LOW)] * 3,
        compiler_params=pltpu.CompilerParams(vmem_limit_bytes=32 << 20),
        cost_estimate=pl.CostEstimate(flops=work * 8192, bytes_accessed=30 << 20, transcendentals=0),
        name="pull",
    )(index, active, glob, where, query, key, value, grad, probs, probs_glob, *grad_glob)


def eye(size):
    row = lax.broadcasted_iota(jnp.int32, (size, size), 0)
    column = lax.broadcasted_iota(jnp.int32, (size, size), 1)
    return jnp.where(row == column, 1.0, 0.0).astype(LOW)


def lanes(start, size):
    return pl.ds(pl.multiple_of(start, 128), size)


def simple_call(kernel, out_shape, args, scalars, name, cost, scratch=(), anywhere=0, limit=32, away=()):
    many = isinstance(out_shape, list)
    smem = pl.BlockSpec(memory_space=pltpu.SMEM)
    vmem = pl.BlockSpec(memory_space=pltpu.VMEM)
    free = pl.BlockSpec(memory_space=pl.ANY)
    specs = [smem] * len(scalars) + [free] * anywhere + [vmem] * (len(args) - anywhere)
    return pl.pallas_call(
        kernel,
        in_specs=specs,
        out_specs=[free if i in away else vmem for i in range(len(out_shape))] if many else vmem,
        out_shape=out_shape,
        scratch_shapes=list(scratch),
        compiler_params=pltpu.CompilerParams(vmem_limit_bytes=limit << 20),
        cost_estimate=pl.CostEstimate(flops=cost * 10**9, bytes_accessed=cost * 3 << 20, transcendentals=0),
        name=name,
    )(*scalars, *args)


def pack_heads_kernel(where, wq, wk, wv, *refs, shards):
    vectors, out, rows_ref = refs
    half, cols = wq.shape[1] // 2, wq.shape[0]
    here = lanes(where[shards] * half, half)
    for i, ref in enumerate((wq, wk, wv)):
        out[i * cols : (i + 1) * cols, :] = ref[:, here].astype(LOW)
    rows_ref[...] = jnp.zeros(rows_ref.shape, F32)
    for v in range(8):
        at = v % 3 * 128
        rows_ref[v // 3 : v // 3 + 1, at : at + cols] = vectors[:, v * cols : (v + 1) * cols]
    rows_ref[3:4, : vectors.shape[1] - 8 * cols] = vectors[:, 8 * cols :]
    out[3 * cols :, :] = rows_ref[...].astype(LOW)


def pack_rest_kernel(where, inner, output, outer, out, *, shards):
    half, cols = output.shape[1] // 2, output.shape[0]
    core = where[shards]
    rows = inner[pl.ds(pl.multiple_of(core * half, 128), half), :].astype(LOW)
    wide = inner.shape[1]
    out[:wide, :] = rows if wide == half else dot_nt(eye(wide), rows).astype(LOW)
    out[wide : wide + cols, :] = output[:, lanes(core * half, half)].astype(LOW)
    count = outer.shape[1] // 2 // half
    for j in range(count):
        at = wide + cols * (1 + j)
        out[at : at + cols, :] = outer[:, lanes((core * count + j) * half, half)].astype(LOW)


def project_kernel(
    where, got, passed, mine, theirs, q_ref, k_ref, v_ref, wh, vec, bias_inner, pieces, sem, *, rows, chips, cols, wide
):
    shards, width = pieces.shape[0], pieces.shape[2]
    half = width // 2
    core, chip = where[shards], where[shards + 1]
    copies = []
    for side, ref in enumerate((got, passed)):
        at = lanes((core if side == 0 else 1 - core) * half, half)
        for i in range(shards):
            copies.append(pltpu.make_async_copy(ref.at[i], pieces.at[where[i], :, at], sem.at[side, i]))
    for copy in copies:
        copy.start()
    for copy in copies:
        copy.wait()
    for t in range(3):
        part = pieces[pl.ds(core * (shards // 2), shards // 2), t * cols : (t + 1) * cols, :]
        wh[t * half : (t + 1) * half, :] = part.reshape(half, width)
    for i in range(shards):
        small = pieces[i, 3 * cols :, :half].astype(F32)
        for v in range(8):
            at = v % 3 * 128
            vec[v : v + 1, i * cols : (i + 1) * cols] = small[v // 3 : v // 3 + 1, at : at + cols]
        unit, at = i * wide // half, i * wide % half
        bias_inner[unit : unit + 1, at : at + wide] = small[3:4, :wide]
    own_lanes = lanes(core * half, half)
    bias_query, bias_value = vec[0:1, own_lanes], vec[1:2, own_lanes]
    for j in range(chips):
        source = lax.rem(chip - j + chips, chips)
        for side, ref in enumerate((mine, theirs)):
            place = (2 * source + (core if side == 0 else 1 - core)) * rows
            at = pl.ds(pl.multiple_of(place, rows), rows)
            value = dot_nt(ref[j * rows : (j + 1) * rows, :], wh[...])
            query = (value[:, :half] + bias_query).astype(LOW).astype(F32) * 0.125
            q_ref[at, :] = query.astype(LOW)
            k_ref[at, :] = value[:, half : 2 * half].astype(LOW)
            v_ref[at, :] = (value[:, 2 * half :] + bias_value).astype(LOW)


def merge_kernel(where, glob, *refs, shards, chips, rows):
    outs = refs[-2:]
    parts, globs = refs[: -2 - chips], refs[-2 - chips : -2]
    core, chip = where[shards], where[shards + 1]
    full = jnp.concatenate
    for side, out in enumerate(outs):
        start = (core if side == 0 else 1 - core) * rows
        out[...] = full([p[pl.ds(pl.multiple_of(start, rows), rows), :] for p in parts], axis=1)
    per = 2 * rows // BLK
    for j in range(chips):
        number = lax.rem(chip - j + chips, chips)
        block, on = global_of(glob, number)
        local = block - chip * per
        for side, out in enumerate(outs):
            start = local - (core if side == 0 else 1 - core) * (per // 2)

            @pl.when(on & (start >= 0) & (start < per // 2))
            def _(out=out, start=start, j=j):
                out[pl.ds(pl.multiple_of(start * BLK, BLK), BLK), :] = globs[j][...]


def spread_kernel(where, glob, own, other, heads_grad, *sends, shards, chips, rows):
    core, chip = where[shards], where[shards + 1]
    heads_grad[pl.ds(pl.multiple_of(core * rows, rows), rows), :] = own[...]
    heads_grad[pl.ds(pl.multiple_of((1 - core) * rows, rows), rows), :] = other[...]
    per = 2 * rows // BLK
    for j, send in enumerate(sends):
        number = lax.rem(chip + j, chips)
        block, on = global_of(glob, number)
        local = block - chip * per
        send[...] = jnp.zeros(send.shape, send.dtype)

        @pl.when(on & (local >= 0) & (local < per))
        def _(send=send, local=local):
            send[...] = heads_grad[pl.ds(pl.multiple_of(local * BLK, BLK), BLK), :]


def head_grads_kernel(
    where, *refs, rows, chips, pairs, cols, wide, shards, devices
):
    grads = refs[: 3 * pairs]
    tops = refs[3 * pairs : 4 * pairs]
    mine, theirs, wh, vec_grad, inner_bias, layout, keep, give, small, part_mine, part_theirs, vec, both = refs[4 * pairs :]
    core, chip = where[shards], where[shards + 1]
    half = mine.shape[1] // 2
    for j in range(chips):
        source = lax.rem(chip - j + chips, chips)
        for side, out in enumerate((part_mine, part_theirs)):
            place = (2 * source + (core if side == 0 else 1 - core)) * rows
            at = pl.ds(pl.multiple_of(place, rows), rows)
            part = jnp.concatenate([g[at, :] for g in grads], axis=1)
            out[j * rows : (j + 1) * rows, :] = dot_nn(part, wh[...]).astype(LOW)
    vec[...] = vec_grad[...]
    vec[0:2, :] = jnp.zeros((2, vec.shape[1]), F32)
    for t in range(3):
        whole = None
        total = jnp.zeros((1, half), F32)
        for j in range(chips):
            source = lax.rem(chip - j + chips, chips)
            for side, ref in enumerate((mine, theirs)):
                place = (2 * source + (core if side == 0 else 1 - core)) * rows
                at = pl.ds(pl.multiple_of(place, rows), rows)
                part = jnp.concatenate([g[at, :] for g in grads[t * pairs : (t + 1) * pairs]], axis=1)
                if t != 1:
                    total = total + jnp.sum(part.astype(F32), axis=0, keepdims=True)
                product = dot_tn(part, ref[j * rows : (j + 1) * rows, :])
                whole = product if whole is None else whole + product
        here = slice(t * cols, (t + 1) * cols)
        both[...] = whole.astype(LOW).reshape(shards // 2, cols, 2 * half)
        keep[:, here, :] = both[:, :, lanes(core * half, half)]
        give[:, here, :] = both[:, :, lanes((1 - core) * half, half)]
        if t != 1:
            vec[t // 2 : t // 2 + 1, lanes(core * half, half)] = total
    head, part, slot = layout[0:1, :], layout[1:2, :], layout[2:3, :]
    value = jnp.full((1, half), NEG, F32)
    for p in range(pairs):
        for i in range(2):
            top = jnp.max(tops[p][i * BLK : (i + 1) * BLK, :], axis=0, keepdims=True)
            value = jnp.where(head == core * 2 * pairs + 2 * p + i, top[:, 0:1], value)
    first = value.astype(LOW).astype(F32)
    second = (value - first).astype(LOW).astype(F32)
    third = value - first - second
    value = jnp.where(part == 0, first, jnp.where(part == 1, second, jnp.where(part == 2, third, 0.0)))
    small[...] = jnp.zeros(small.shape, F32)
    device = where[shards + 3]
    value = jnp.where(slot == lax.rem(device, 8), value, 0.0)
    for r in range(devices // 8):
        line = jnp.where(device // 8 == r, value, 0.0)
        for i in range(shards):
            small[i, 4 + r : 5 + r, :] = line
    for i in range(shards):
        for v in range(8):
            at = v % 3 * 128
            small[i, v // 3 : v // 3 + 1, at : at + cols] = vec[v : v + 1, i * cols : (i + 1) * cols]
        unit, at = i * wide // half, i * wide % half
        small[i, 3:4, :wide] = inner_bias[unit : unit + 1, at : at + wide]


def finish_heads_kernel(where, own, other, limits, wq, wk, *outs, shards, devices, head_dim):
    grads, vectors, (inner, maxima, cut_q, cut_k) = outs[:3], outs[3:11], outs[11:]
    core, shard = where[shards], where[shards + 2]
    half, cols = own.shape[1], wq.shape[0]
    for t, out in enumerate(grads):
        for ref, which in ((own, core), (other, 1 - core)):
            out[:, lanes(which * half, half)] = ref[t * cols : (t + 1) * cols, :].astype(F32)
    small = own[3 * cols :, :].astype(F32) + other[3 * cols :, :].astype(F32)
    for v, out in enumerate(vectors):
        at = v % 3 * 128
        out[...] = small[v // 3 : v // 3 + 1, at : at + cols]
    inner[...] = small[3:4, : inner.shape[1]]
    heads = limits.shape[1]
    value = jnp.full((1, half), NEG, F32)
    for r in range(devices // 8):
        line = jnp.broadcast_to(small[4 + r : 5 + r, :], (8, half))
        line = line + pltpu.roll(line, half - heads, 1) + pltpu.roll(line, half - 2 * heads, 1)
        value = jnp.maximum(value, line)
    step = half // 2
    while step >= 48:
        value = jnp.maximum(value, pltpu.roll(value, step, 1))
        step //= 2
    top = value[0:1, :heads]
    maxima[...] = top
    root = jnp.sqrt(limits[...] / jnp.maximum(top, limits[...]))
    column = lax.broadcasted_iota(jnp.int32, (cols, 1), 0) + shard * cols
    scale = jnp.zeros((cols, 1), F32)
    for h in range(heads):
        inside = (column >= h * head_dim) & (column < (h + 1) * head_dim)
        scale = jnp.where(inside, root[:, h : h + 1], scale)
    cut_q[...] = wq[...] * scale
    cut_k[...] = wk[...] * scale


def finish_rest_kernel(where, own, other, inner, output, outer, *, shards):
    half, cols, wide = own.shape[1], output.shape[0], inner.shape[1]
    core = where[shards]
    for ref, which in ((own, core), (other, 1 - core)):
        rows = ref[:wide, :]
        inner[pl.ds(pl.multiple_of(which * half, 128), half), :] = (
            rows.astype(F32) if wide == half else dot_nt(eye(half), rows)
        )
        output[:, lanes(which * half, half)] = ref[wide : wide + cols, :].astype(F32)
        count = outer.shape[1] // 2 // half
        for j in range(count):
            at = wide + cols * (1 + j)
            outer[:, lanes((which * count + j) * half, half)] = ref[at : at + cols, :].astype(F32)


def dense_kernel(
    where, early, late, early_other, late_other, att_own, att_other, tokens, cotangent, vec, bias_inner,
    layer_out, resid, grad_own, grad_other, keep, give, vec_grad, inner_bias_grad,
    inner_w, rest_w, att, low, normed, inverse, act, slope, acc, outer_grad, inner_g, rest_g, sem, out_sem,
    *, wide,
):
    shards, _, width = rest_w.shape
    rows, half = tokens.shape[0], width // 2
    cols = width // shards
    core = where[shards]
    natural = wide == half
    lead = wide if natural else 0
    rest_copies, inner_copies = [], []
    for side, pair in enumerate(((early, late), (early_other, late_other))):
        which = core if side == 0 else 1 - core
        at = 0
        for ref in pair:
            for i in range(ref.shape[0]):
                shard = where[at]
                rest_copies.append(
                    pltpu.make_async_copy(
                        ref.at[i, pl.ds(lead, ref.shape[1] - lead), :],
                        rest_w.at[shard, :, lanes(which * half, half)],
                        sem.at[0, side, at],
                    )
                )
                if natural:
                    inner_copies.append(
                        pltpu.make_async_copy(
                            ref.at[i, pl.ds(0, wide), :],
                            inner_w.at[pl.ds(pl.multiple_of(which * half, 128), half), lanes(shard * wide, wide)],
                            sem.at[1, side, at],
                        )
                    )
                at += 1
    for copy in rest_copies + inner_copies:
        copy.start()
    groups = act.shape[0]
    each = half // wide
    begin = 0 if natural else wide
    step = 128

    def inner_weights(g):
        if natural:
            return jnp.concatenate([inner_w[:, u * half : (u + 1) * half] for u in (g, g + groups)], axis=1)
        parts = [rest_w[u * each : (u + 1) * each, :wide, :].reshape(half, width) for u in (g, g + groups)]
        return jnp.concatenate(parts, axis=0)

    def outer_weights(g):
        at = begin + cols * (1 + g)
        return rest_w[:, at : at + cols, :].reshape(width, width)

    def output_weights():
        return rest_w[:, begin : begin + cols, :].reshape(width, width)

    sends = []

    def send(pairs):
        for source, target in pairs:
            copy = pltpu.make_async_copy(source, target, out_sem.at[len(sends)])
            copy.start()
            sends.append(copy)

    def send_rest(at, source_at, count, shard_from=0, shard_count=shards):
        which = pl.ds(shard_from, shard_count)
        send(
            (rest_g.at[which, pl.ds(source_at, count), here], target.at[which, pl.ds(at, count), :])
            for here, target in ((lanes(core * half, half), keep), (lanes((1 - core) * half, half), give))
        )

    att[:, lanes(core * half, half)] = att_own[...]
    att[:, lanes((1 - core) * half, half)] = att_other[...]
    for copy in rest_copies:
        copy.wait()
    acc[...] = dot_nt(att[...], output_weights())
    for r in range(0, rows, step):
        at = slice(r, r + step)
        n, inv = normalise(tokens[at, :] + (acc[at, :] + vec[2:3, :]))
        normed[at, :] = n
        inverse[at, :] = inv
        low[at, :] = (n * vec[4:5, :] + vec[5:6, :]).astype(LOW)
    for copy in inner_copies:
        copy.wait()

    for g in range(groups):
        product = (dot_nn if natural else dot_nt)(low[...], inner_weights(g))
        bias = jnp.concatenate([bias_inner[u : u + 1, :] for u in (g, g + groups)], axis=1)
        a, d = gelu_and_slope(product + bias)
        act[g] = a.astype(LOW)
        slope[g] = d.astype(LOW)
        product = dot_nt(act[g], outer_weights(g))
        acc[...] = product if g == 0 else acc[...] + product

    sums = [jnp.zeros((1, width), F32)] * 3
    for r in range(0, rows, step):
        at = slice(r, r + step)
        hidden = normed[at, :] * vec[4:5, :] + vec[5:6, :]
        n, inv = normalise(hidden + (acc[at, :] + vec[3:4, :]))
        layer_out[at, :] = n * vec[6:7, :] + vec[7:8, :]
        e = cotangent[at, :]
        dv = norm_backward(e, n, inv, vec[6:7, :])
        acc[at, :] = dv
        dl = dv.astype(LOW)
        outer_grad[at, :] = dl
        sums = [
            sums[0] + jnp.sum(dl.astype(F32), axis=0, keepdims=True),
            sums[1] + jnp.sum(e * n, axis=0, keepdims=True),
            sums[2] + jnp.sum(e, axis=0, keepdims=True),
        ]
    vec_grad[3:4, :] = sums[0]
    vec_grad[6:7, :] = sums[1]
    vec_grad[7:8, :] = sums[2]

    turned = outer_grad[...].T
    low_turned = low[...].T
    for g in range(groups):
        at = begin + cols * (1 + g)
        rest_g[:, at : at + cols, :] = dot_nn(turned, act[g]).astype(LOW).reshape(shards, cols, width)
        send_rest(at + lead, at, cols)
        inner_low = (dot_nn(outer_grad[...], outer_weights(g)) * slope[g].astype(F32)).astype(LOW)
        bias = jnp.sum(inner_low.astype(F32), axis=0, keepdims=True)
        inner_bias_grad[g : g + 1, :] = bias[:, :half]
        inner_bias_grad[g + groups : g + groups + 1, :] = bias[:, half:]
        acc[...] += (dot_nt if natural else dot_nn)(inner_low, inner_weights(g))
        if natural:
            part = dot_nn(low_turned, inner_low).astype(LOW)
            for i, u in enumerate((g, g + groups)):
                here = slice(i * half, (i + 1) * half)
                inner_g[0, u] = part[:half, here]
                inner_g[1, u] = part[half:, here]
                send(
                    (inner_g.at[which, u], target.at[u, pl.ds(0, wide), :])
                    for which, target in ((core, keep), (1 - core, give))
                )
        else:
            part = dot_nn(inner_low.T, low[...]).astype(LOW)
            for i, u in enumerate((g, g + groups)):
                block = part[i * half : (i + 1) * half].reshape(each, wide, width)
                rest_g[u * each : (u + 1) * each, :wide, :] = block
                send_rest(0, 0, wide, u * each, each)

    sums = [jnp.zeros((1, width), F32)] * 3
    for r in range(0, rows, step):
        at = slice(r, r + step)
        e, n = acc[at, :], normed[at, :]
        dv = norm_backward(e, n, inverse[at, :], vec[4:5, :])
        resid[at, :] = dv
        dl = dv.astype(LOW)
        outer_grad[at, :] = dl
        sums = [
            sums[0] + jnp.sum(dl.astype(F32), axis=0, keepdims=True),
            sums[1] + jnp.sum(e * n, axis=0, keepdims=True),
            sums[2] + jnp.sum(e, axis=0, keepdims=True),
        ]
    vec_grad[0:2, :] = jnp.zeros((2, width), F32)
    vec_grad[2:3, :] = sums[0]
    vec_grad[4:5, :] = sums[1]
    vec_grad[5:6, :] = sums[2]
    low[...] = dot_nn(outer_grad[...], output_weights()).astype(LOW)
    grad_own[...] = low[:, lanes(core * half, half)]
    grad_other[...] = low[:, lanes((1 - core) * half, half)]
    part = dot_nn(outer_grad[...].T, att[...]).astype(LOW).reshape(shards, cols, width)
    rest_g[:, begin : begin + cols, :] = part
    send_rest(begin + lead, begin, cols)
    for copy in sends:
        copy.wait()


def ring_kernel(where, *refs, counts, kind, cut):
    refs = list(refs)
    parts = []
    for count in counts:
        total = refs.pop(0)[0].astype(F32)
        for _ in range(count - 1):
            total = total + refs.pop(0)[0].astype(F32)
        parts.append(total)
    if kind == "first":
        up, down = refs
        up[...] = parts[0][:cut].astype(LOW)
        down[...] = parts[0][cut:].astype(LOW)
    elif kind == "second":
        above, below, up, down = refs
        up[:cut, :] = (parts[0][:cut] + above[...].astype(F32)).astype(LOW)
        up[cut:, :] = parts[0][cut:].astype(LOW)
        down[:cut, :] = parts[1][:cut].astype(LOW)
        down[cut:, :] = (parts[1][cut:] + below[...].astype(F32)).astype(LOW)
    elif kind == "later":
        above, below, up, down = refs
        up[...] = (parts[0] + above[...].astype(F32)).astype(LOW)
        down[...] = (parts[1] + below[...].astype(F32)).astype(LOW)
    else:
        above, below, out = refs
        out[...] = (parts[0] + above[...].astype(F32) + below[...].astype(F32)).astype(LOW)


def ring_step(where, arrays, slots, received, kind, cut):
    rows, half = arrays[0].shape[1:]
    specs = [
        pl.BlockSpec((1, rows, half), lambda i, where, slot=slot: (where[slot], 0, 0)) for slot in slots for _ in arrays
    ]
    specs += [pl.BlockSpec(a.shape, lambda i, where: (0, 0)) for a in received]
    shapes = [(rows, half)] if kind == "last" else [(rows, half)] * 2
    if kind == "first":
        shapes = [(cut, half), (rows - cut, half)]
    return pl.pallas_call(
        functools.partial(ring_kernel, counts=[len(arrays)] * len(slots), kind=kind, cut=cut),
        grid_spec=pltpu.PrefetchScalarGridSpec(
            num_scalar_prefetch=1,
            grid=(1,),
            in_specs=specs,
            out_specs=[pl.BlockSpec(s, lambda i, where: (0, 0)) for s in shapes],
        ),
        out_shape=[struct(s) for s in shapes],
        compiler_params=pltpu.CompilerParams(vmem_limit_bytes=32 << 20),
        cost_estimate=pl.CostEstimate(flops=10**9, bytes_accessed=3 << 20, transcendentals=0),
        name="ring_" + kind,
    )(where, *[a for _ in slots for a in arrays], *received)


class Moves:
    def __init__(self, ctx, wshard):
        self.ctx, self.wshard, self.chips = ctx, wshard, ctx // 2
        self.half = half = wshard // 2
        order = list(range(0, wshard, 2)) + list(range(wshard - 1, 0, -2))
        self.up_perm = [(order[i], order[(i + 1) % wshard]) for i in range(wshard)]
        self.down_perm = [(b, a) for a, b in self.up_perm]
        deltas = [0]
        for step in range(1, half):
            deltas += [-step, step]
        deltas.append(half)
        sums = [half]
        for step in range(half - 1, 0, -1):
            sums += [step, -step]
        sums.append(0)
        table = []
        for c in range(ctx):
            for w in range(wshard):
                at = order.index(w)
                goes = [order[(at + d) % wshard] for d in sums]
                placed = [(s // half != c % 2) * half + s % half for s in goes]
                table.append(
                    [order[(at + d) % wshard] for d in deltas] + [c % 2, c // 2, w, c * wshard + w] + goes + placed
                )
        self.sums, self.placed = wshard + 4, wshard + 4 + len(sums)
        here = lax.axis_index("ctx") * wshard + lax.axis_index("wshard")
        table = jnp.asarray(table, jnp.int32)
        self.where = lax.dynamic_slice(table, (here, 0), (1, table.shape[1]), allow_negative_indices=False)[0]

    def up(self, value):
        return lax.ppermute(value, "wshard", self.up_perm)

    def down(self, value):
        return lax.ppermute(value, "wshard", self.down_perm)

    def swap(self, value):
        return lax.ppermute(value, "ctx", [(c, c ^ 1) for c in range(self.ctx)])

    def chip_shift(self, value, j):
        return lax.ppermute(value, "ctx", [(c, (c + 2 * j) % self.ctx) for c in range(self.ctx)])

    def chip_flip(self, value, bit):
        return lax.ppermute(value, "ctx", [(c, c ^ (2 * bit)) for c in range(self.ctx)])

    def gather(self, piece, cut):
        above = below = piece
        pieces = [piece]
        for _ in range(1, self.half):
            above, below = self.up(above), self.down(below)
            pieces += [above, below]
            turn = yield pieces
            if turn is not None:
                above, below = after((above, below), turn)
        pieces.append(jnp.concatenate([self.up(above[:cut]), self.down(below[cut:])], axis=0))
        yield pieces

    def scatter(self, step, cut):
        up, down = step("first", [0], [])
        yield up
        for s in range(self.half - 1):
            above, below = self.up(up), self.down(down)
            up, down = step("second" if s == 0 else "later", [1 + 2 * s, 2 + 2 * s], [above, below])
            yield up
        above, below = self.up(up), self.down(down)
        [total] = step("last", [2 * self.half - 1], [above, below])
        yield total

    def chip_sum(self, value):
        bit = 1
        while bit < self.chips:
            other = self.chip_flip(value, bit)
            value = (value.astype(F32) + other.astype(F32)).astype(LOW)
            bit *= 2
        return value


def slot_lists(first, count, nblocks, glob, random_rows, heads):
    blocks = first + jnp.arange(count, dtype=jnp.int32)
    offsets = jnp.arange(-1, 2, dtype=jnp.int32)
    start = jnp.clip(blocks - 1, 0, nblocks - 3)
    window = start[:, None] + jnp.arange(3, dtype=jnp.int32)[None, :]
    near = jnp.abs(window - blocks[:, None]) <= 1
    slide = jnp.clip(blocks[:, None] + offsets[None, :], 0, nblocks - 1)
    spread = lambda a: jnp.broadcast_to(a[:, None, :], (count, heads, a.shape[-1]))
    rest = jnp.concatenate(
        [jnp.broadcast_to(glob[None, None, :], (count, heads, glob.shape[0])), random_rows], axis=2
    )
    lists = jnp.concatenate([spread(slide), rest], axis=2)
    slots = lists.shape[2]
    equal = lists[..., :, None] == lists[..., None, :]
    earlier = jnp.arange(slots)[:, None] < jnp.arange(slots)[None, :]
    fresh = jnp.logical_not(jnp.any(equal & earlier[None, None], axis=-2))
    on = jnp.concatenate([spread(near), fresh[..., 3:]], axis=2)
    index = jnp.concatenate([spread(window), rest], axis=2)
    return index, jnp.where(on, index, nblocks)


def struct(shape, dtype=LOW):
    return jax.ShapeDtypeStruct(tuple(shape), dtype)


def after(value, *others):
    return lax.optimization_barrier((value,) + others)[0]


def per_device(ctx, wshard, layer_input, segments, global_blocks, random_blocks, thresholds, w_query, w_key, w_value, w_output, w_inner, w_outer, query_bias, value_bias, output_bias, inner_bias, outer_bias, gain_attn, shift_attn, gain_mlp, shift_mlp, out_grad):
    m = Moves(ctx, wshard)
    chips, where, devices = m.chips, m.where, ctx * wshard
    tokens = layer_input[0]
    rows_here, width = tokens.shape
    seg_all = segments[0]
    length = seg_all.shape[0]
    glob = global_blocks[0]
    heads = thresholds.shape[0]
    head_dim = width // heads
    nblocks = length // BLK
    count = 2 * rows_here // BLK
    half = width // 2
    own_heads = heads // 2
    pairs = own_heads // 2
    cols, wide = w_query.shape[1], w_inner.shape[1]
    units = wide * wshard // half
    sizes = dict(shards=wshard, rows=rows_here, chips=chips)

    small_least = 4 + devices // 8
    head_rows = -(-(3 * cols + 4) // 16) * 16
    vectors = (query_bias, value_bias, output_bias, outer_bias, gain_attn, shift_attn, gain_mlp, shift_mlp, inner_bias)
    head_piece = simple_call(
        functools.partial(pack_heads_kernel, shards=wshard),
        struct((head_rows, half)),
        (w_query.T, w_key.T, w_value.T, jnp.concatenate(vectors)[None]),
        (where,),
        "pack_heads",
        1,
        scratch=[pltpu.VMEM((head_rows - 3 * cols, half), F32)],
    )
    inputs_low = tokens.astype(LOW)
    mine = jnp.concatenate([inputs_low] + [m.chip_shift(inputs_low, j) for j in range(1, chips)], axis=0)
    theirs = m.swap(mine)
    *_, head_pieces = m.gather(head_piece, head_rows // 2 // 16 * 16)
    got = jnp.stack(head_pieces)
    passed = m.swap(got)
    query, key, value, head_weights, vec, bias_inner = simple_call(
        functools.partial(project_kernel, rows=rows_here, chips=chips, cols=cols, wide=wide),
        [struct((length, half))] * 3
        + [struct((3 * half, width)), struct((8, width), F32), struct((units, half), F32)],
        (got, passed, mine, theirs),
        (where,),
        "project",
        10,
        scratch=[pltpu.VMEM((wshard, head_rows, width), LOW), pltpu.SemaphoreType.DMA((2, wshard))],
        anywhere=2,
        limit=40,
    )

    rest_rows = wide + 5 * cols
    rest_cut = rest_rows // 2 // 16 * 16
    rest_piece = simple_call(
        functools.partial(pack_rest_kernel, shards=wshard),
        struct((rest_rows, half)),
        (w_inner, w_output.T, w_outer.T),
        (where,),
        "pack_rest",
        1,
    )
    rest_piece = after(rest_piece, passed, theirs)
    gather = m.gather(rest_piece, rest_cut)
    gathered = next(gather)

    chip, core = where[wshard + 1], where[wshard]
    random_own = lax.dynamic_slice(
        random_blocks,
        (chip * count, core * own_heads, 0),
        (count, own_heads, random_blocks.shape[2]),
        allow_negative_indices=False,
    )
    index, active = slot_lists(chip * count, count, nblocks, glob, random_own, own_heads)
    seg_rep = seg_all.reshape(nblocks, BLK)
    seg_rep = jnp.concatenate([seg_rep, seg_rep], axis=1)
    seg_rep = jnp.concatenate([seg_rep, jnp.full((8, 2 * BLK), -1, jnp.int32)], axis=0)
    scalars = (index.reshape(-1), active.reshape(-1), glob, where)
    seg_args = (seg_all[:, None], seg_rep, seg_all[None, :])
    done = []
    for pair in range(pairs):
        q = after(query, gathered[2 * pair]) if 0 < 2 * pair < len(gathered) else query
        done.append(attend(*scalars, q, key, value, *seg_args, count, own_heads, pair, wshard))
        if len(gathered) < wshard:
            gathered = gather.send(done[-1][4])
    while len(gathered) < wshard:
        gathered = next(gather)
    early, late = jnp.stack(gathered[:-3]), jnp.stack(gathered[-3:])
    rest = (early, late, m.swap(early), m.swap(late))
    attended_glob = jnp.concatenate([d[2] for d in done], axis=1)
    glob_rows = [attended_glob] + [m.chip_shift(attended_glob, j) for j in range(1, chips)]
    att_own, att_give = simple_call(
        functools.partial(merge_kernel, **sizes),
        [struct((rows_here, half))] * 2,
        tuple(d[0] for d in done) + tuple(glob_rows),
        (where, glob),
        "merge",
        1,
    )
    att_other = m.swap(att_give)

    big = lambda *shape: pltpu.VMEM(shape, F32)
    low = lambda *shape: pltpu.VMEM(shape, LOW)
    layer_output, resid_one, grad_own, grad_other, keep, give, vec_grad, inner_bias_grad = (
        simple_call(
            functools.partial(dense_kernel, wide=wide),
            [struct((rows_here, width), F32)] * 2
            + [struct((rows_here, half))] * 2
            + [struct((wshard, rest_rows, half))] * 2
            + [struct((8, width), F32), struct((units, half), F32)],
            rest + (att_own, att_other, tokens, out_grad[0], vec, bias_inner),
            (where,),
            "dense",
            40,
            scratch=[
                low(width, wide * wshard) if wide == half else low(16, 128),
                low(wshard, rest_rows - wide if wide == half else rest_rows, width),
                low(rows_here, width),
                low(rows_here, width),
                big(rows_here, width),
                big(rows_here, 1),
                low(units // 2, rows_here, width),
                low(units // 2, rows_here, width),
                big(rows_here, width),
                low(rows_here, width),
                low(2, units, half, half) if wide == half else low(1, 1, 16, 128),
                low(wshard, rest_rows - wide if wide == half else rest_rows, width),
                pltpu.SemaphoreType.DMA((2, 2, wshard)),
                pltpu.SemaphoreType.DMA((2 * (units + units // 2 + 1),)),
            ],
            anywhere=4,
            away=(4, 5),
            limit=60,
        )
    )

    from_other = m.swap(grad_other)
    given = m.swap(after(give, from_other))
    heads_grad, *glob_sends = simple_call(
        functools.partial(spread_kernel, **sizes),
        [struct((2 * rows_here, half))] + [struct((BLK, half))] * chips,
        (grad_own, from_other),
        (where, glob),
        "spread",
        1,
    )
    glob_grads = [glob_sends[0]] + [m.chip_shift(glob_sends[j], j) for j in range(1, chips)]

    def ring_of(arrays, cut, base):
        def step(kind, slots, received):
            return ring_step(where, arrays, [base + s for s in slots], received, kind, cut)

        return m.scatter(step, cut)

    ring = ring_of([keep, given], rest_cut, m.sums)
    turn = (next(ring),)
    pulled = []
    for pair in range(pairs):
        q = after(query, *turn)
        pulled.append(
            pull(*scalars, q, key, value, heads_grad, glob_grads, done[pair][1], done[pair][3], own_heads, pair, wshard)
        )
        turn = (next(ring),)
    grads = tuple(pulled[pair][t] for t in range(3) for pair in range(pairs))
    small_rows = -(-(3 * cols + small_least) // 16) * 16 - 3 * cols
    lane = [i % 48 for i in range(half)]
    layout = jnp.asarray(
        [[i % heads if i < 3 * heads else -1 for i in lane], [i // heads for i in lane], [i // 48 for i in range(half)]],
        jnp.int32,
    )
    layout = jnp.concatenate([layout, jnp.zeros((5, half), jnp.int32)], axis=0)
    head_keep, head_give, small_parts, part_mine, part_theirs = simple_call(
        functools.partial(head_grads_kernel, pairs=pairs, cols=cols, wide=wide, devices=devices, **sizes),
        [struct((wshard // 2, 3 * cols, half))] * 2
        + [struct((wshard, small_rows, half), F32)]
        + [struct((chips * rows_here, width))] * 2,
        after(grads, *turn) + tuple(d[4] for d in done) + (mine, theirs, head_weights, vec_grad, inner_bias_grad, layout),
        (where,),
        "head_grads",
        12,
        scratch=[big(8, width), low(wshard // 2, cols, width)],
        limit=48,
    )
    *_, total = ring
    head_give, part_theirs = after((head_give, part_theirs), total)
    head_given = m.swap(head_give)
    passed_theirs = m.swap(part_theirs)
    summed = part_mine.astype(F32) + passed_theirs.astype(F32)
    summed = summed.reshape(chips, rows_here, width)
    sent = [summed[j].astype(LOW) for j in range(1, chips)]
    input_grad = resid_one + summed[0]
    for j in range(1, chips):
        input_grad = input_grad + m.chip_shift(sent[j - 1], chips - j).astype(F32)

    head_parts = jnp.concatenate([head_keep, head_given], axis=0)
    head_parts = [after(head_parts, total, *sent)]

    def head_step(kind, slots, received):
        return head_ring_step(where, head_parts[0], small_parts, m, slots, received, kind)

    head_ring = m.scatter(head_step, None)
    for _ in range(3):
        next(head_ring)
    head_parts[0] = after(head_parts[0], input_grad)
    *_, head_tail = head_ring
    rest_tail = m.chip_sum(total)
    grad_inner, grad_output, grad_outer = simple_call(
        functools.partial(finish_rest_kernel, shards=wshard),
        [struct(w_inner.shape, F32), struct(w_output.shape[::-1], F32), struct(w_outer.shape[::-1], F32)],
        (rest_tail, m.swap(rest_tail)),
        (where,),
        "finish_rest",
        2,
    )
    head_tail = m.chip_sum(head_tail)
    vector, turned = struct((1, cols), F32), struct((cols, width), F32)
    finished = simple_call(
        functools.partial(finish_heads_kernel, shards=wshard, devices=devices, head_dim=head_dim),
        [turned] * 3 + [vector] * 8 + [struct((1, wide), F32), struct((1, heads), F32), turned, turned],
        (head_tail, m.swap(head_tail), thresholds[None], w_query.T, w_key.T),
        (where,),
        "finish_heads",
        2,
    )
    grad_query, grad_key, grad_value = finished[:3]
    vector_out = [v[0] for v in finished[3:11]]
    inner_out, maxima, clipped_query, clipped_key = finished[11][0], finished[12][0], finished[13], finished[14]

    return (
        layer_output[None],
        input_grad[None],
        grad_query.T,
        grad_key.T,
        grad_value.T,
        grad_output.T,
        grad_inner,
        grad_outer.T,
        vector_out[0],
        vector_out[1],
        vector_out[2],
        inner_out,
        vector_out[3],
        vector_out[4],
        vector_out[5],
        vector_out[6],
        vector_out[7],
        clipped_query.T,
        clipped_key.T,
        maxima,
    )


def head_ring_kernel(where, *refs, kind, targets, cut):
    refs = list(refs)
    parts = []
    for _ in range(targets):
        part, small = refs.pop(0), refs.pop(0)
        parts.append(jnp.concatenate([part[0].astype(F32), small[0]], axis=0))
    if kind == "first":
        up, down = refs
        up[...] = parts[0][:cut].astype(LOW)
        down[...] = parts[0][cut:].astype(LOW)
    elif kind == "second":
        above, below, up, down = refs
        up[:cut, :] = (parts[0][:cut] + above[...].astype(F32)).astype(LOW)
        up[cut:, :] = parts[0][cut:].astype(LOW)
        down[:cut, :] = parts[1][:cut].astype(LOW)
        down[cut:, :] = (parts[1][cut:] + below[...].astype(F32)).astype(LOW)
    elif kind == "later":
        above, below, up, down = refs
        up[...] = (parts[0] + above[...].astype(F32)).astype(LOW)
        down[...] = (parts[1] + below[...].astype(F32)).astype(LOW)
    else:
        above, below, out = refs
        out[...] = (parts[0] + above[...].astype(F32) + below[...].astype(F32)).astype(LOW)


def head_ring_step(where, parts, small, m, slots, received, kind):
    half = parts.shape[2]
    rows = parts.shape[1] + small.shape[1]
    cut = rows // 2 // 16 * 16
    specs, args = [], []
    for slot in slots:
        specs.append(
            pl.BlockSpec((1,) + parts.shape[1:], lambda i, where, at=m.placed + slot: (where[at], 0, 0))
        )
        specs.append(pl.BlockSpec((1,) + small.shape[1:], lambda i, where, at=m.sums + slot: (where[at], 0, 0)))
        args += [parts, small]
    specs += [pl.BlockSpec(a.shape, lambda i, where: (0, 0)) for a in received]
    shapes = [(rows, half)] if kind == "last" else [(rows, half)] * 2
    if kind == "first":
        shapes = [(cut, half), (rows - cut, half)]
    return pl.pallas_call(
        functools.partial(head_ring_kernel, kind=kind, targets=len(slots), cut=cut),
        grid_spec=pltpu.PrefetchScalarGridSpec(
            num_scalar_prefetch=1,
            grid=(1,),
            in_specs=specs,
            out_specs=[pl.BlockSpec(s, lambda i, where: (0, 0)) for s in shapes],
        ),
        out_shape=[struct(s) for s in shapes],
        compiler_params=pltpu.CompilerParams(vmem_limit_bytes=32 << 20),
        cost_estimate=pl.CostEstimate(flops=10**9, bytes_accessed=3 << 20, transcendentals=0),
        name="head_ring_" + kind,
    )(where, *args, *received)


def solution(mesh):
    tokens = P("wshard", "ctx", None)
    sequence = P("wshard", None)
    matrix = P(None, "wshard")
    vector = P("wshard")
    in_specs = (tokens, sequence, sequence, P(), P()) + (matrix,) * 6 + (vector,) * 9 + (tokens,)
    out_specs = (tokens, tokens) + (matrix,) * 6 + (vector,) * 9 + (matrix, matrix, P())
    return jax.shard_map(
        functools.partial(per_device, mesh.shape["ctx"], mesh.shape["wshard"]),
        mesh=mesh,
        in_specs=in_specs,
        out_specs=out_specs,
        check_vma=False,
    )
```

```python
import functools

import jax
import jax.numpy as jnp
from jax import lax
from jax.experimental import pallas as pl
from jax.experimental.pallas import tpu as pltpu
from jax.sharding import PartitionSpec as P

BLK = 64
EPSILON = 1e-05
NEG = -1e30
UNROLL = 8
LOW = jnp.bfloat16
F32 = jnp.float32


def dot_nn(left, right):
    return lax.dot_general(left, right, (((1,), (0,)), ((), ())), preferred_element_type=F32)


def dot_tn(left, right):
    return lax.dot_general(left, right, (((0,), (0,)), ((), ())), preferred_element_type=F32)


def dot_nt(left, right):
    return lax.dot_general(left, right, (((1,), (1,)), ((), ())), preferred_element_type=F32)


def normalise(values):
    centre = values - jnp.mean(values, axis=-1, keepdims=True)
    inverse = lax.rsqrt(jnp.mean(centre * centre, axis=-1, keepdims=True) + EPSILON)
    return centre * inverse, inverse


def norm_backward(upstream, normed, inverse, gain):
    scaled = upstream * gain
    mean_one = jnp.mean(scaled, axis=-1, keepdims=True)
    mean_two = jnp.mean(scaled * normed, axis=-1, keepdims=True)
    return inverse * (scaled - mean_one - normed * mean_two)


def gelu_and_slope(v):
    c = 0.7978845608028654
    k = c * 0.044715
    square = v * v
    t = jnp.tanh(v * (c + k * square))
    half = 0.5 + 0.5 * t
    return v * half, half + (half - half * t) * (v * (c + 3 * k * square))


def global_of(glob, number):
    block = glob[jnp.minimum(number, glob.shape[0] - 1)]
    on = number < glob.shape[0]
    for i in range(glob.shape[0]):
        on = on & ((i >= number) | (glob[i] != block))
    return block, on


def in_global(glob, place):
    found = glob[0] == place
    for i in range(1, glob.shape[0]):
        found = found | (glob[i] == place)
    return found


def halves():
    lane = lax.broadcasted_iota(jnp.int32, (BLK, 2 * BLK), 1)
    return lane < BLK


def stack_pair(tile):
    low = jnp.where(halves(), 1.0, 0.0).astype(tile.dtype)
    high = jnp.where(halves(), 0.0, 1.0).astype(tile.dtype)
    return jnp.concatenate([tile * low, tile * high], axis=0)


def unstack_pair(rows):
    return jnp.where(halves(), rows[:BLK], rows[BLK:])


def rows_of(ref, block, count=1):
    return ref[pl.ds(pl.multiple_of(block * BLK, BLK), count * BLK), :]


def shared_rows(ref, index, base):
    return jnp.concatenate([rows_of(ref, index[base], 3), rows_of(ref, index[base + 3])], axis=0)


def own_rows(ref, index, base):
    return jnp.concatenate([rows_of(ref, index[base + j]) for j in range(4, 8)], axis=0)


def attend_kernel(index, active, glob, where, q_ref, k_ref, v_ref, seg_q, seg_k, seg_row, o_ref, p_ref, og_ref, pg_ref, top_ref, score, *, heads, pair, shards, blocks):
    chip = where[shards + 1]
    my_glob, my_on = global_of(glob, chip)
    step = pl.program_id(0)
    wide = lax.broadcasted_iota(jnp.int32, (1, 2 * BLK), 1) < BLK
    length = k_ref.shape[0]

    @pl.when(step == 0)
    def _():
        top_ref[...] = jnp.full(top_ref.shape, NEG, F32)

        @pl.when(jnp.logical_not(my_on))
        def _():
            og_ref[...] = jnp.zeros(og_ref.shape, og_ref.dtype)
            pg_ref[...] = jnp.zeros(pg_ref.shape, pg_ref.dtype)

        @pl.when(my_on)
        def _():
            place = my_glob
            q2 = stack_pair(rows_of(q_ref, place))
            sq = rows_of(seg_q, place)
            sq = jnp.concatenate([sq, sq], axis=0)
            top = jnp.full((2 * BLK, 1), NEG, F32)
            cut = 512
            for j in range(length // cut):
                raw = dot_nt(q2, k_ref[j * cut : (j + 1) * cut, :])
                raw = jnp.where(seg_row[:, j * cut : (j + 1) * cut] == sq, raw, NEG)
                score[:, j * cut : (j + 1) * cut] = raw
                top = jnp.maximum(top, jnp.max(raw, axis=1, keepdims=True))
            total = jnp.zeros((2 * BLK, 1), F32)
            for j in range(length // cut):
                power = jnp.exp(score[:, j * cut : (j + 1) * cut] - top)
                score[:, j * cut : (j + 1) * cut] = power
                total = total + jnp.sum(power, axis=1, keepdims=True)
            scale = 1.0 / total
            acc = jnp.zeros((2 * BLK, 2 * BLK), F32)
            for j in range(length // cut):
                prob = (score[:, j * cut : (j + 1) * cut] * scale).astype(LOW)
                pg_ref[:, j * cut : (j + 1) * cut] = prob
                acc = acc + dot_nn(prob, v_ref[j * cut : (j + 1) * cut, :])
            og_ref[...] = unstack_pair(acc).astype(LOW)
            top_ref[...] = jnp.maximum(top_ref[...], jnp.broadcast_to(top, top_ref.shape))

    for u in range(UNROLL):
        b = step * UNROLL + u
        place = chip * blocks + b
        q2 = stack_pair(rows_of(q_ref, place))
        sq = rows_of(seg_q, place)
        sq = jnp.concatenate([sq, sq], axis=0)
        base = (b * heads + 2 * pair) * 8
        shared = dot_nt(q2, shared_rows(k_ref, index, base))
        own = jnp.concatenate(
            [dot_nt(q2[h * BLK : (h + 1) * BLK], own_rows(k_ref, index, base + 8 * h)) for h in range(2)],
            axis=0,
        )

        def seg_of(at, j):
            first = seg_k[pl.ds(active[at + j], 1), :]
            second = seg_k[pl.ds(active[at + j + 1], 1), :]
            return jnp.where(wide, first, second)

        raw_s = jnp.where(jnp.concatenate([seg_of(base, 0), seg_of(base, 2)], axis=1) == sq, shared, NEG)
        seg_own = [
            jnp.broadcast_to(
                jnp.concatenate([seg_of(base + 8 * h, 4), seg_of(base + 8 * h, 6)], axis=1), (BLK, 4 * BLK)
            )
            for h in range(2)
        ]
        raw_o = jnp.where(jnp.concatenate(seg_own, axis=0) == sq, own, NEG)
        top = jnp.maximum(jnp.max(raw_s, axis=1, keepdims=True), jnp.max(raw_o, axis=1, keepdims=True))
        power_s = jnp.exp(raw_s - top)
        power_o = jnp.exp(raw_o - top)
        scale = 1.0 / (jnp.sum(power_s, axis=1, keepdims=True) + jnp.sum(power_o, axis=1, keepdims=True))
        prob_s = (power_s * scale).astype(LOW)
        prob_o = (power_o * scale).astype(LOW)
        p_ref[u, :, : 4 * BLK] = prob_s
        p_ref[u, :, 4 * BLK :] = prob_o
        out = dot_nn(prob_s, shared_rows(v_ref, index, base))
        out = out + jnp.concatenate(
            [
                dot_nn(prob_o[h * BLK : (h + 1) * BLK], own_rows(v_ref, index, base + 8 * h))
                for h in range(2)
            ],
            axis=0,
        )
        o_ref[u * BLK : (u + 1) * BLK, :] = unstack_pair(out).astype(LOW)
        used = jnp.where(in_global(glob, place), jnp.full_like(top, NEG), top)
        top_ref[...] = jnp.maximum(top_ref[...], jnp.broadcast_to(used, top_ref.shape))


def pull_kernel(index, active, glob, where, q_ref, k_ref, v_ref, do_ref, p_ref, pg_ref, *refs, heads, pair, shards, blocks):
    *dog_refs, dq_ref, dk_ref, dv_ref, dk, dv, score = refs
    chip = where[shards + 1]
    my_glob, my_on = global_of(glob, chip)
    del active
    step = pl.program_id(0)
    steps = pl.num_programs(0)
    length = k_ref.shape[0]

    @pl.when(step == 0)
    def _():
        dk[...] = jnp.zeros(dk.shape, F32)
        dv[...] = jnp.zeros(dv.shape, F32)
        dq_ref[...] = jnp.zeros(dq_ref.shape, dq_ref.dtype)

    def add(ref, block, value):
        at = pl.ds(pl.multiple_of(block * BLK, BLK), value.shape[0])
        ref[at, :] += value

    for u in range(UNROLL):
        b = step * UNROLL + u
        place = chip * blocks + b
        q2 = stack_pair(rows_of(q_ref, place))
        keep = jnp.where(in_global(glob, place), 0.0, 1.0).astype(LOW)
        do2 = stack_pair(do_ref[u * BLK : (u + 1) * BLK, :] * keep)
        base = (b * heads + 2 * pair) * 8
        ks = shared_rows(k_ref, index, base)
        ko = [own_rows(k_ref, index, base + 8 * h) for h in range(2)]
        vs = shared_rows(v_ref, index, base)
        vo = [own_rows(v_ref, index, base + 8 * h) for h in range(2)]
        prob_s = p_ref[u, :, : 4 * BLK]
        prob_o = p_ref[u, :, 4 * BLK :]
        dp_s = dot_nt(do2, vs)
        dp_o = jnp.concatenate([dot_nt(do2[h * BLK : (h + 1) * BLK], vo[h]) for h in range(2)], axis=0)
        ps = prob_s.astype(F32)
        po = prob_o.astype(F32)
        ts = ps * dp_s
        to = po * dp_o
        total = jnp.sum(ts, axis=1, keepdims=True) + jnp.sum(to, axis=1, keepdims=True)
        ds_s = (ts - ps * total).astype(LOW)
        ds_o = (to - po * total).astype(LOW)
        dq = dot_nn(ds_s, ks) + jnp.concatenate(
            [dot_nn(ds_o[h * BLK : (h + 1) * BLK], ko[h]) for h in range(2)], axis=0
        )
        at = pl.ds(pl.multiple_of(place * BLK, BLK), BLK)
        dq_ref[at, :] = (unstack_pair(dq) * 0.125).astype(LOW)
        dks = dot_tn(ds_s, q2)
        dvs = dot_tn(prob_s, do2)
        add(dk, index[base], dks[: 3 * BLK])
        add(dk, index[base + 3], dks[3 * BLK :])
        add(dv, index[base], dvs[: 3 * BLK])
        add(dv, index[base + 3], dvs[3 * BLK :])
        for h in range(2):
            part = slice(h * BLK, (h + 1) * BLK)
            dko = dot_tn(ds_o[part], q2[part])
            dvo = dot_tn(prob_o[part], do2[part])
            for j in range(4):
                add(dk, index[base + 8 * h + 4 + j], dko[j * BLK : (j + 1) * BLK])
                add(dv, index[base + 8 * h + 4 + j], dvo[j * BLK : (j + 1) * BLK])

    @pl.when((step == steps - 1) & my_on)
    def _():
        place = my_glob
        q2 = stack_pair(rows_of(q_ref, place))
        dog = dog_refs[0][...].astype(F32)
        for ref in dog_refs[1:]:
            dog = dog + ref[...].astype(F32)
        do2 = stack_pair(dog.astype(LOW))
        cut = 512
        total = jnp.zeros((2 * BLK, 1), F32)
        for j in range(length // cut):
            part = slice(j * cut, (j + 1) * cut)
            dp = dot_nt(do2, v_ref[part, :])
            score[:, part] = dp
            total = total + jnp.sum(pg_ref[:, part].astype(F32) * dp, axis=1, keepdims=True)
        acc = jnp.zeros((2 * BLK, 2 * BLK), F32)
        for j in range(length // cut):
            part = slice(j * cut, (j + 1) * cut)
            prob = pg_ref[:, part]
            ds = (prob.astype(F32) * (score[:, part] - total)).astype(LOW)
            acc = acc + dot_nn(ds, k_ref[part, :])
            dk[part, :] += dot_tn(ds, q2)
            dv[part, :] += dot_tn(prob, do2)
        at = pl.ds(pl.multiple_of(place * BLK, BLK), BLK)
        dq_ref[at, :] = (unstack_pair(acc) * 0.125).astype(LOW)

    @pl.when(step == steps - 1)
    def _():
        dk_ref[...] = dk[...].astype(LOW)
        dv_ref[...] = dv[...].astype(LOW)


def attend(index, active, glob, where, query, key, value, seg_col, seg_rep, seg_row, blocks, heads, pair, shards):
    length = key.shape[0]
    column = pl.BlockSpec((length, 2 * BLK), lambda s, *_: (0, pair))
    whole = lambda shape: pl.BlockSpec(shape, lambda s, *_: (0,) * len(shape))
    grid = pltpu.PrefetchScalarGridSpec(
        num_scalar_prefetch=4,
        grid=(blocks // UNROLL,),
        in_specs=[column, column, column, whole(seg_col.shape), whole(seg_rep.shape), whole(seg_row.shape)],
        out_specs=[
            pl.BlockSpec((UNROLL * BLK, 2 * BLK), lambda s, *_: (s, 0)),
            pl.BlockSpec((UNROLL, 2 * BLK, 8 * BLK), lambda s, *_: (s, 0, 0)),
            whole((BLK, 2 * BLK)),
            whole((2 * BLK, length)),
            whole((2 * BLK, 2 * BLK)),
        ],
        scratch_shapes=[pltpu.VMEM((2 * BLK, length), F32)],
    )
    work = (blocks * 8 + length // BLK) * 2 * BLK * BLK
    return pl.pallas_call(
        functools.partial(attend_kernel, heads=heads, pair=pair, shards=shards, blocks=blocks),
        grid_spec=grid,
        out_shape=[
            jax.ShapeDtypeStruct((blocks * BLK, 2 * BLK), LOW),
            jax.ShapeDtypeStruct((blocks, 2 * BLK, 8 * BLK), LOW),
            jax.ShapeDtypeStruct((BLK, 2 * BLK), LOW),
            jax.ShapeDtypeStruct((2 * BLK, length), LOW),
            jax.ShapeDtypeStruct((2 * BLK, 2 * BLK), F32),
        ],
        compiler_params=pltpu.CompilerParams(vmem_limit_bytes=32 << 20),
        cost_estimate=pl.CostEstimate(flops=work * 8192, bytes_accessed=27 << 20, transcendentals=0),
        name="attend",
    )(index, active, glob, where, query, key, value, seg_col, seg_rep, seg_row)


def pull(index, active, glob, where, query, key, value, grad, grad_glob, probs, probs_glob, heads, pair, shards):
    length = key.shape[0]
    blocks = grad.shape[0] // BLK
    column = pl.BlockSpec((length, 2 * BLK), lambda s, *_: (0, pair))
    whole = lambda shape: pl.BlockSpec(shape, lambda s, *_: (0,) * len(shape))
    grid = pltpu.PrefetchScalarGridSpec(
        num_scalar_prefetch=4,
        grid=(blocks // UNROLL,),
        in_specs=[
            column,
            column,
            column,
            pl.BlockSpec((UNROLL * BLK, 2 * BLK), lambda s, *_: (s, pair)),
            pl.BlockSpec((UNROLL, 2 * BLK, 8 * BLK), lambda s, *_: (s, 0, 0)),
            whole((2 * BLK, length)),
        ]
        + [pl.BlockSpec((BLK, 2 * BLK), lambda s, *_: (0, pair))] * len(grad_glob),
        out_specs=[whole((length, 2 * BLK))] * 3,
        scratch_shapes=[
            pltpu.VMEM((length, 2 * BLK), F32),
            pltpu.VMEM((length, 2 * BLK), F32),
            pltpu.VMEM((2 * BLK, length), F32),
        ],
    )
    work = (blocks * 8 + length // BLK) * 2 * BLK * BLK
    return pl.pallas_call(
        functools.partial(pull_kernel, heads=heads, pair=pair, shards=shards, blocks=blocks),
        grid_spec=grid,
        out_shape=[jax.ShapeDtypeStruct((length, 2 * BLK), LOW)] * 3,
        compiler_params=pltpu.CompilerParams(vmem_limit_bytes=32 << 20),
        cost_estimate=pl.CostEstimate(flops=work * 8192, bytes_accessed=30 << 20, transcendentals=0),
        name="pull",
    )(index, active, glob, where, query, key, value, grad, probs, probs_glob, *grad_glob)


def eye(size):
    row = lax.broadcasted_iota(jnp.int32, (size, size), 0)
    column = lax.broadcasted_iota(jnp.int32, (size, size), 1)
    return jnp.where(row == column, 1.0, 0.0).astype(LOW)


def lanes(start, size):
    return pl.ds(pl.multiple_of(start, 128), size)


def simple_call(kernel, out_shape, args, scalars, name, cost, scratch=(), anywhere=0, limit=32, away=()):
    many = isinstance(out_shape, list)
    smem = pl.BlockSpec(memory_space=pltpu.SMEM)
    vmem = pl.BlockSpec(memory_space=pltpu.VMEM)
    free = pl.BlockSpec(memory_space=pl.ANY)
    specs = [smem] * len(scalars) + [free] * anywhere + [vmem] * (len(args) - anywhere)
    return pl.pallas_call(
        kernel,
        in_specs=specs,
        out_specs=[free if i in away else vmem for i in range(len(out_shape))] if many else vmem,
        out_shape=out_shape,
        scratch_shapes=list(scratch),
        compiler_params=pltpu.CompilerParams(vmem_limit_bytes=limit << 20),
        cost_estimate=pl.CostEstimate(flops=cost * 10**9, bytes_accessed=cost * 3 << 20, transcendentals=0),
        name=name,
    )(*scalars, *args)


def pack_heads_kernel(where, wq, wk, wv, *refs, shards):
    vectors, out, rows_ref = refs
    half, cols = wq.shape[1] // 2, wq.shape[0]
    here = lanes(where[shards] * half, half)
    for i, ref in enumerate((wq, wk, wv)):
        out[i * cols : (i + 1) * cols, :] = ref[:, here].astype(LOW)
    rows_ref[...] = jnp.zeros(rows_ref.shape, F32)
    for v in range(8):
        at = v % 3 * 128
        rows_ref[v // 3 : v // 3 + 1, at : at + cols] = vectors[:, v * cols : (v + 1) * cols]
    rows_ref[3:4, : vectors.shape[1] - 8 * cols] = vectors[:, 8 * cols :]
    out[3 * cols :, :] = rows_ref[...].astype(LOW)


def pack_rest_kernel(where, inner, output, outer, out, *, shards):
    half, cols = output.shape[1] // 2, output.shape[0]
    core = where[shards]
    rows = inner[pl.ds(pl.multiple_of(core * half, 128), half), :].astype(LOW)
    wide = inner.shape[1]
    out[:wide, :] = rows if wide == half else dot_nt(eye(wide), rows).astype(LOW)
    out[wide : wide + cols, :] = output[:, lanes(core * half, half)].astype(LOW)
    count = outer.shape[1] // 2 // half
    for j in range(count):
        at = wide + cols * (1 + j)
        out[at : at + cols, :] = outer[:, lanes((core * count + j) * half, half)].astype(LOW)


def project_kernel(
    where, got, passed, mine, theirs, q_ref, k_ref, v_ref, wh, vec, bias_inner, pieces, sem, *, rows, chips, cols, wide
):
    shards, width = pieces.shape[0], pieces.shape[2]
    half = width // 2
    core, chip = where[shards], where[shards + 1]
    copies = []
    for side, ref in enumerate((got, passed)):
        at = lanes((core if side == 0 else 1 - core) * half, half)
        for i in range(shards):
            copies.append(pltpu.make_async_copy(ref.at[i], pieces.at[where[i], :, at], sem.at[side, i]))
    for copy in copies:
        copy.start()
    for copy in copies:
        copy.wait()
    for t in range(3):
        part = pieces[pl.ds(core * (shards // 2), shards // 2), t * cols : (t + 1) * cols, :]
        wh[t * half : (t + 1) * half, :] = part.reshape(half, width)
    for i in range(shards):
        small = pieces[i, 3 * cols :, :half].astype(F32)
        for v in range(8):
            at = v % 3 * 128
            vec[v : v + 1, i * cols : (i + 1) * cols] = small[v // 3 : v // 3 + 1, at : at + cols]
        unit, at = i * wide // half, i * wide % half
        bias_inner[unit : unit + 1, at : at + wide] = small[3:4, :wide]
    own_lanes = lanes(core * half, half)
    bias_query, bias_value = vec[0:1, own_lanes], vec[1:2, own_lanes]
    for j in range(chips):
        source = lax.rem(chip - j + chips, chips)
        for side, ref in enumerate((mine, theirs)):
            place = (2 * source + (core if side == 0 else 1 - core)) * rows
            at = pl.ds(pl.multiple_of(place, rows), rows)
            value = dot_nt(ref[j * rows : (j + 1) * rows, :], wh[...])
            query = (value[:, :half] + bias_query).astype(LOW).astype(F32) * 0.125
            q_ref[at, :] = query.astype(LOW)
            k_ref[at, :] = value[:, half : 2 * half].astype(LOW)
            v_ref[at, :] = (value[:, 2 * half :] + bias_value).astype(LOW)


def merge_kernel(where, glob, *refs, shards, chips, rows):
    outs = refs[-2:]
    parts, globs = refs[: -2 - chips], refs[-2 - chips : -2]
    core, chip = where[shards], where[shards + 1]
    full = jnp.concatenate
    for side, out in enumerate(outs):
        start = (core if side == 0 else 1 - core) * rows
        out[...] = full([p[pl.ds(pl.multiple_of(start, rows), rows), :] for p in parts], axis=1)
    per = 2 * rows // BLK
    for j in range(chips):
        number = lax.rem(chip - j + chips, chips)
        block, on = global_of(glob, number)
        local = block - chip * per
        for side, out in enumerate(outs):
            start = local - (core if side == 0 else 1 - core) * (per // 2)

            @pl.when(on & (start >= 0) & (start < per // 2))
            def _(out=out, start=start, j=j):
                out[pl.ds(pl.multiple_of(start * BLK, BLK), BLK), :] = globs[j][...]


def spread_kernel(where, glob, own, other, heads_grad, *sends, shards, chips, rows):
    core, chip = where[shards], where[shards + 1]
    heads_grad[pl.ds(pl.multiple_of(core * rows, rows), rows), :] = own[...]
    heads_grad[pl.ds(pl.multiple_of((1 - core) * rows, rows), rows), :] = other[...]
    per = 2 * rows // BLK
    for j, send in enumerate(sends):
        number = lax.rem(chip + j, chips)
        block, on = global_of(glob, number)
        local = block - chip * per
        send[...] = jnp.zeros(send.shape, send.dtype)

        @pl.when(on & (local >= 0) & (local < per))
        def _(send=send, local=local):
            send[...] = heads_grad[pl.ds(pl.multiple_of(local * BLK, BLK), BLK), :]


def head_grads_kernel(
    where, *refs, rows, chips, pairs, cols, wide, shards, devices
):
    grads = refs[: 3 * pairs]
    tops = refs[3 * pairs : 4 * pairs]
    mine, theirs, wh, vec_grad, inner_bias, layout, keep, give, small, part_mine, part_theirs, vec, both = refs[4 * pairs :]
    core, chip = where[shards], where[shards + 1]
    half = mine.shape[1] // 2
    for j in range(chips):
        source = lax.rem(chip - j + chips, chips)
        for side, out in enumerate((part_mine, part_theirs)):
            place = (2 * source + (core if side == 0 else 1 - core)) * rows
            at = pl.ds(pl.multiple_of(place, rows), rows)
            part = jnp.concatenate([g[at, :] for g in grads], axis=1)
            out[j * rows : (j + 1) * rows, :] = dot_nn(part, wh[...]).astype(LOW)
    vec[...] = vec_grad[...]
    vec[0:2, :] = jnp.zeros((2, vec.shape[1]), F32)
    for t in range(3):
        whole = None
        total = jnp.zeros((1, half), F32)
        for j in range(chips):
            source = lax.rem(chip - j + chips, chips)
            for side, ref in enumerate((mine, theirs)):
                place = (2 * source + (core if side == 0 else 1 - core)) * rows
                at = pl.ds(pl.multiple_of(place, rows), rows)
                part = jnp.concatenate([g[at, :] for g in grads[t * pairs : (t + 1) * pairs]], axis=1)
                if t != 1:
                    total = total + jnp.sum(part.astype(F32), axis=0, keepdims=True)
                product = dot_tn(part, ref[j * rows : (j + 1) * rows, :])
                whole = product if whole is None else whole + product
        here = slice(t * cols, (t + 1) * cols)
        both[...] = whole.astype(LOW).reshape(shards // 2, cols, 2 * half)
        keep[:, here, :] = both[:, :, lanes(core * half, half)]
        give[:, here, :] = both[:, :, lanes((1 - core) * half, half)]
        if t != 1:
            vec[t // 2 : t // 2 + 1, lanes(core * half, half)] = total
    head, part, slot = layout[0:1, :], layout[1:2, :], layout[2:3, :]
    value = jnp.full((1, half), NEG, F32)
    for p in range(pairs):
        for i in range(2):
            top = jnp.max(tops[p][i * BLK : (i + 1) * BLK, :], axis=0, keepdims=True)
            value = jnp.where(head == core * 2 * pairs + 2 * p + i, top[:, 0:1], value)
    first = value.astype(LOW).astype(F32)
    second = (value - first).astype(LOW).astype(F32)
    third = value - first - second
    value = jnp.where(part == 0, first, jnp.where(part == 1, second, jnp.where(part == 2, third, 0.0)))
    small[...] = jnp.zeros(small.shape, F32)
    device = where[shards + 3]
    value = jnp.where(slot == lax.rem(device, 8), value, 0.0)
    for r in range(devices // 8):
        line = jnp.where(device // 8 == r, value, 0.0)
        for i in range(shards):
            small[i, 4 + r : 5 + r, :] = line
    for i in range(shards):
        for v in range(8):
            at = v % 3 * 128
            small[i, v // 3 : v // 3 + 1, at : at + cols] = vec[v : v + 1, i * cols : (i + 1) * cols]
        unit, at = i * wide // half, i * wide % half
        small[i, 3:4, :wide] = inner_bias[unit : unit + 1, at : at + wide]


def finish_heads_kernel(where, own, other, limits, wq, wk, *outs, shards, devices, head_dim):
    grads, vectors, (inner, maxima, cut_q, cut_k) = outs[:3], outs[3:11], outs[11:]
    core, shard = where[shards], where[shards + 2]
    half, cols = own.shape[1], wq.shape[0]
    for t, out in enumerate(grads):
        for ref, which in ((own, core), (other, 1 - core)):
            out[:, lanes(which * half, half)] = ref[t * cols : (t + 1) * cols, :].astype(F32)
    small = own[3 * cols :, :].astype(F32) + other[3 * cols :, :].astype(F32)
    for v, out in enumerate(vectors):
        at = v % 3 * 128
        out[...] = small[v // 3 : v // 3 + 1, at : at + cols]
    inner[...] = small[3:4, : inner.shape[1]]
    heads = limits.shape[1]
    value = jnp.full((1, half), NEG, F32)
    for r in range(devices // 8):
        line = jnp.broadcast_to(small[4 + r : 5 + r, :], (8, half))
        line = line + pltpu.roll(line, half - heads, 1) + pltpu.roll(line, half - 2 * heads, 1)
        value = jnp.maximum(value, line)
    step = half // 2
    while step >= 48:
        value = jnp.maximum(value, pltpu.roll(value, step, 1))
        step //= 2
    top = value[0:1, :heads]
    maxima[...] = top
    root = jnp.sqrt(limits[...] / jnp.maximum(top, limits[...]))
    column = lax.broadcasted_iota(jnp.int32, (cols, 1), 0) + shard * cols
    scale = jnp.zeros((cols, 1), F32)
    for h in range(heads):
        inside = (column >= h * head_dim) & (column < (h + 1) * head_dim)
        scale = jnp.where(inside, root[:, h : h + 1], scale)
    cut_q[...] = wq[...] * scale
    cut_k[...] = wk[...] * scale


def finish_rest_kernel(where, own, other, inner, output, outer, *, shards):
    half, cols, wide = own.shape[1], output.shape[0], inner.shape[1]
    core = where[shards]
    for ref, which in ((own, core), (other, 1 - core)):
        rows = ref[:wide, :]
        inner[pl.ds(pl.multiple_of(which * half, 128), half), :] = (
            rows.astype(F32) if wide == half else dot_nt(eye(half), rows)
        )
        output[:, lanes(which * half, half)] = ref[wide : wide + cols, :].astype(F32)
        count = outer.shape[1] // 2 // half
        for j in range(count):
            at = wide + cols * (1 + j)
            outer[:, lanes((which * count + j) * half, half)] = ref[at : at + cols, :].astype(F32)


def dense_kernel(
    where, early, late, early_other, late_other, att_own, att_other, tokens, cotangent, vec, bias_inner,
    layer_out, resid, grad_own, grad_other, keep, give, vec_grad, inner_bias_grad,
    inner_w, rest_w, att, low, normed, inverse, act, slope, acc, outer_grad, inner_g, rest_g, sem, out_sem,
    *, wide,
):
    shards, _, width = rest_w.shape
    rows, half = tokens.shape[0], width // 2
    cols = width // shards
    core = where[shards]
    natural = wide == half
    lead = wide if natural else 0
    rest_copies, inner_copies = [], []
    for side, pair in enumerate(((early, late), (early_other, late_other))):
        which = core if side == 0 else 1 - core
        at = 0
        for ref in pair:
            for i in range(ref.shape[0]):
                shard = where[at]
                rest_copies.append(
                    pltpu.make_async_copy(
                        ref.at[i, pl.ds(lead, ref.shape[1] - lead), :],
                        rest_w.at[shard, :, lanes(which * half, half)],
                        sem.at[0, side, at],
                    )
                )
                if natural:
                    inner_copies.append(
                        pltpu.make_async_copy(
                            ref.at[i, pl.ds(0, wide), :],
                            inner_w.at[pl.ds(pl.multiple_of(which * half, 128), half), lanes(shard * wide, wide)],
                            sem.at[1, side, at],
                        )
                    )
                at += 1
    for copy in rest_copies + inner_copies:
        copy.start()
    groups = act.shape[0]
    each = half // wide
    begin = 0 if natural else wide
    step = 128

    def inner_weights(g):
        if natural:
            return jnp.concatenate([inner_w[:, u * half : (u + 1) * half] for u in (g, g + groups)], axis=1)
        parts = [rest_w[u * each : (u + 1) * each, :wide, :].reshape(half, width) for u in (g, g + groups)]
        return jnp.concatenate(parts, axis=0)

    def outer_weights(g):
        at = begin + cols * (1 + g)
        return rest_w[:, at : at + cols, :].reshape(width, width)

    def output_weights():
        return rest_w[:, begin : begin + cols, :].reshape(width, width)

    sends = []

    def send(pairs):
        for source, target in pairs:
            copy = pltpu.make_async_copy(source, target, out_sem.at[len(sends)])
            copy.start()
            sends.append(copy)

    def send_rest(at, source_at, count, shard_from=0, shard_count=shards):
        which = pl.ds(shard_from, shard_count)
        send(
            (rest_g.at[which, pl.ds(source_at, count), here], target.at[which, pl.ds(at, count), :])
            for here, target in ((lanes(core * half, half), keep), (lanes((1 - core) * half, half), give))
        )

    att[:, lanes(core * half, half)] = att_own[...]
    att[:, lanes((1 - core) * half, half)] = att_other[...]
    for copy in rest_copies:
        copy.wait()
    acc[...] = dot_nt(att[...], output_weights())
    for r in range(0, rows, step):
        at = slice(r, r + step)
        n, inv = normalise(tokens[at, :] + (acc[at, :] + vec[2:3, :]))
        normed[at, :] = n
        inverse[at, :] = inv
        low[at, :] = (n * vec[4:5, :] + vec[5:6, :]).astype(LOW)
    for copy in inner_copies:
        copy.wait()

    for g in range(groups):
        product = (dot_nn if natural else dot_nt)(low[...], inner_weights(g))
        bias = jnp.concatenate([bias_inner[u : u + 1, :] for u in (g, g + groups)], axis=1)
        a, d = gelu_and_slope(product + bias)
        act[g] = a.astype(LOW)
        slope[g] = d.astype(LOW)
        product = dot_nt(act[g], outer_weights(g))
        acc[...] = product if g == 0 else acc[...] + product

    sums = [jnp.zeros((1, width), F32)] * 3
    for r in range(0, rows, step):
        at = slice(r, r + step)
        hidden = normed[at, :] * vec[4:5, :] + vec[5:6, :]
        n, inv = normalise(hidden + (acc[at, :] + vec[3:4, :]))
        layer_out[at, :] = n * vec[6:7, :] + vec[7:8, :]
        e = cotangent[at, :]
        dv = norm_backward(e, n, inv, vec[6:7, :])
        acc[at, :] = dv
        dl = dv.astype(LOW)
        outer_grad[at, :] = dl
        sums = [
            sums[0] + jnp.sum(dl.astype(F32), axis=0, keepdims=True),
            sums[1] + jnp.sum(e * n, axis=0, keepdims=True),
            sums[2] + jnp.sum(e, axis=0, keepdims=True),
        ]
    vec_grad[3:4, :] = sums[0]
    vec_grad[6:7, :] = sums[1]
    vec_grad[7:8, :] = sums[2]

    turned = outer_grad[...].T
    low_turned = low[...].T
    for g in range(groups):
        at = begin + cols * (1 + g)
        rest_g[:, at : at + cols, :] = dot_nn(turned, act[g]).astype(LOW).reshape(shards, cols, width)
        send_rest(at + lead, at, cols)
        inner_low = (dot_nn(outer_grad[...], outer_weights(g)) * slope[g].astype(F32)).astype(LOW)
        bias = jnp.sum(inner_low.astype(F32), axis=0, keepdims=True)
        inner_bias_grad[g : g + 1, :] = bias[:, :half]
        inner_bias_grad[g + groups : g + groups + 1, :] = bias[:, half:]
        acc[...] += (dot_nt if natural else dot_nn)(inner_low, inner_weights(g))
        if natural:
            part = dot_nn(low_turned, inner_low).astype(LOW)
            for i, u in enumerate((g, g + groups)):
                here = slice(i * half, (i + 1) * half)
                inner_g[0, u] = part[:half, here]
                inner_g[1, u] = part[half:, here]
                send(
                    (inner_g.at[which, u], target.at[u, pl.ds(0, wide), :])
                    for which, target in ((core, keep), (1 - core, give))
                )
        else:
            part = dot_nn(inner_low.T, low[...]).astype(LOW)
            for i, u in enumerate((g, g + groups)):
                block = part[i * half : (i + 1) * half].reshape(each, wide, width)
                rest_g[u * each : (u + 1) * each, :wide, :] = block
                send_rest(0, 0, wide, u * each, each)

    sums = [jnp.zeros((1, width), F32)] * 3
    for r in range(0, rows, step):
        at = slice(r, r + step)
        e, n = acc[at, :], normed[at, :]
        dv = norm_backward(e, n, inverse[at, :], vec[4:5, :])
        resid[at, :] = dv
        dl = dv.astype(LOW)
        outer_grad[at, :] = dl
        sums = [
            sums[0] + jnp.sum(dl.astype(F32), axis=0, keepdims=True),
            sums[1] + jnp.sum(e * n, axis=0, keepdims=True),
            sums[2] + jnp.sum(e, axis=0, keepdims=True),
        ]
    vec_grad[0:2, :] = jnp.zeros((2, width), F32)
    vec_grad[2:3, :] = sums[0]
    vec_grad[4:5, :] = sums[1]
    vec_grad[5:6, :] = sums[2]
    low[...] = dot_nn(outer_grad[...], output_weights()).astype(LOW)
    grad_own[...] = low[:, lanes(core * half, half)]
    grad_other[...] = low[:, lanes((1 - core) * half, half)]
    part = dot_nn(outer_grad[...].T, att[...]).astype(LOW).reshape(shards, cols, width)
    rest_g[:, begin : begin + cols, :] = part
    send_rest(begin + lead, begin, cols)
    for copy in sends:
        copy.wait()


def ring_kernel(where, *refs, counts, kind, cut):
    refs = list(refs)
    parts = []
    for count in counts:
        total = refs.pop(0)[0].astype(F32)
        for _ in range(count - 1):
            total = total + refs.pop(0)[0].astype(F32)
        parts.append(total)
    if kind == "first":
        up, down = refs
        up[...] = parts[0][:cut].astype(LOW)
        down[...] = parts[0][cut:].astype(LOW)
    elif kind == "second":
        above, below, up, down = refs
        up[:cut, :] = (parts[0][:cut] + above[...].astype(F32)).astype(LOW)
        up[cut:, :] = parts[0][cut:].astype(LOW)
        down[:cut, :] = parts[1][:cut].astype(LOW)
        down[cut:, :] = (parts[1][cut:] + below[...].astype(F32)).astype(LOW)
    elif kind == "later":
        above, below, up, down = refs
        up[...] = (parts[0] + above[...].astype(F32)).astype(LOW)
        down[...] = (parts[1] + below[...].astype(F32)).astype(LOW)
    else:
        above, below, out = refs
        out[...] = (parts[0] + above[...].astype(F32) + below[...].astype(F32)).astype(LOW)


def ring_step(where, arrays, slots, received, kind, cut):
    rows, half = arrays[0].shape[1:]
    specs = [
        pl.BlockSpec((1, rows, half), lambda i, where, slot=slot: (where[slot], 0, 0)) for slot in slots for _ in arrays
    ]
    specs += [pl.BlockSpec(a.shape, lambda i, where: (0, 0)) for a in received]
    shapes = [(rows, half)] if kind == "last" else [(rows, half)] * 2
    if kind == "first":
        shapes = [(cut, half), (rows - cut, half)]
    return pl.pallas_call(
        functools.partial(ring_kernel, counts=[len(arrays)] * len(slots), kind=kind, cut=cut),
        grid_spec=pltpu.PrefetchScalarGridSpec(
            num_scalar_prefetch=1,
            grid=(1,),
            in_specs=specs,
            out_specs=[pl.BlockSpec(s, lambda i, where: (0, 0)) for s in shapes],
        ),
        out_shape=[struct(s) for s in shapes],
        compiler_params=pltpu.CompilerParams(vmem_limit_bytes=32 << 20),
        cost_estimate=pl.CostEstimate(flops=10**9, bytes_accessed=3 << 20, transcendentals=0),
        name="ring_" + kind,
    )(where, *[a for _ in slots for a in arrays], *received)


class Moves:
    def __init__(self, ctx, wshard):
        self.ctx, self.wshard, self.chips = ctx, wshard, ctx // 2
        self.half = half = wshard // 2
        order = list(range(0, wshard, 2)) + list(range(wshard - 1, 0, -2))
        self.up_perm = [(order[i], order[(i + 1) % wshard]) for i in range(wshard)]
        self.down_perm = [(b, a) for a, b in self.up_perm]
        deltas = [0]
        for step in range(1, half):
            deltas += [-step, step]
        deltas.append(half)
        sums = [half]
        for step in range(half - 1, 0, -1):
            sums += [step, -step]
        sums.append(0)
        table = []
        for c in range(ctx):
            for w in range(wshard):
                at = order.index(w)
                goes = [order[(at + d) % wshard] for d in sums]
                placed = [(s // half != c % 2) * half + s % half for s in goes]
                table.append(
                    [order[(at + d) % wshard] for d in deltas] + [c % 2, c // 2, w, c * wshard + w] + goes + placed
                )
        self.sums, self.placed = wshard + 4, wshard + 4 + len(sums)
        here = lax.axis_index("ctx") * wshard + lax.axis_index("wshard")
        table = jnp.asarray(table, jnp.int32)
        self.where = lax.dynamic_slice(table, (here, 0), (1, table.shape[1]), allow_negative_indices=False)[0]

    def up(self, value):
        return lax.ppermute(value, "wshard", self.up_perm)

    def down(self, value):
        return lax.ppermute(value, "wshard", self.down_perm)

    def swap(self, value):
        return lax.ppermute(value, "ctx", [(c, c ^ 1) for c in range(self.ctx)])

    def chip_shift(self, value, j):
        return lax.ppermute(value, "ctx", [(c, (c + 2 * j) % self.ctx) for c in range(self.ctx)])

    def chip_flip(self, value, bit):
        return lax.ppermute(value, "ctx", [(c, c ^ (2 * bit)) for c in range(self.ctx)])

    def gather(self, piece, cut):
        above = below = piece
        pieces = [piece]
        for _ in range(1, self.half):
            above, below = self.up(above), self.down(below)
            pieces += [above, below]
            turn = yield pieces
            if turn is not None:
                above, below = after((above, below), turn)
        pieces.append(jnp.concatenate([self.up(above[:cut]), self.down(below[cut:])], axis=0))
        yield pieces

    def scatter(self, step, cut):
        up, down = step("first", [0], [])
        yield up
        for s in range(self.half - 1):
            above, below = self.up(up), self.down(down)
            up, down = step("second" if s == 0 else "later", [1 + 2 * s, 2 + 2 * s], [above, below])
            yield up
        above, below = self.up(up), self.down(down)
        [total] = step("last", [2 * self.half - 1], [above, below])
        yield total

    def chip_sum(self, value):
        bit = 1
        while bit < self.chips:
            other = self.chip_flip(value, bit)
            value = (value.astype(F32) + other.astype(F32)).astype(LOW)
            bit *= 2
        return value


def slot_lists(first, count, nblocks, glob, random_rows, heads):
    blocks = first + jnp.arange(count, dtype=jnp.int32)
    offsets = jnp.arange(-1, 2, dtype=jnp.int32)
    start = jnp.clip(blocks - 1, 0, nblocks - 3)
    window = start[:, None] + jnp.arange(3, dtype=jnp.int32)[None, :]
    near = jnp.abs(window - blocks[:, None]) <= 1
    slide = jnp.clip(blocks[:, None] + offsets[None, :], 0, nblocks - 1)
    spread = lambda a: jnp.broadcast_to(a[:, None, :], (count, heads, a.shape[-1]))
    rest = jnp.concatenate(
        [jnp.broadcast_to(glob[None, None, :], (count, heads, glob.shape[0])), random_rows], axis=2
    )
    lists = jnp.concatenate([spread(slide), rest], axis=2)
    slots = lists.shape[2]
    equal = lists[..., :, None] == lists[..., None, :]
    earlier = jnp.arange(slots)[:, None] < jnp.arange(slots)[None, :]
    fresh = jnp.logical_not(jnp.any(equal & earlier[None, None], axis=-2))
    on = jnp.concatenate([spread(near), fresh[..., 3:]], axis=2)
    index = jnp.concatenate([spread(window), rest], axis=2)
    return index, jnp.where(on, index, nblocks)


def struct(shape, dtype=LOW):
    return jax.ShapeDtypeStruct(tuple(shape), dtype)


def after(value, *others):
    return lax.optimization_barrier((value,) + others)[0]


def per_device(ctx, wshard, layer_input, segments, global_blocks, random_blocks, thresholds, w_query, w_key, w_value, w_output, w_inner, w_outer, query_bias, value_bias, output_bias, inner_bias, outer_bias, gain_attn, shift_attn, gain_mlp, shift_mlp, out_grad):
    m = Moves(ctx, wshard)
    chips, where, devices = m.chips, m.where, ctx * wshard
    tokens = layer_input[0]
    rows_here, width = tokens.shape
    seg_all = segments[0]
    length = seg_all.shape[0]
    glob = global_blocks[0]
    heads = thresholds.shape[0]
    head_dim = width // heads
    nblocks = length // BLK
    count = 2 * rows_here // BLK
    half = width // 2
    own_heads = heads // 2
    pairs = own_heads // 2
    cols, wide = w_query.shape[1], w_inner.shape[1]
    units = wide * wshard // half
    sizes = dict(shards=wshard, rows=rows_here, chips=chips)

    small_least = 4 + devices // 8
    head_rows = -(-(3 * cols + 4) // 16) * 16
    vectors = (query_bias, value_bias, output_bias, outer_bias, gain_attn, shift_attn, gain_mlp, shift_mlp, inner_bias)
    head_piece = simple_call(
        functools.partial(pack_heads_kernel, shards=wshard),
        struct((head_rows, half)),
        (w_query.T, w_key.T, w_value.T, jnp.concatenate(vectors)[None]),
        (where,),
        "pack_heads",
        1,
        scratch=[pltpu.VMEM((head_rows - 3 * cols, half), F32)],
    )
    inputs_low = tokens.astype(LOW)
    mine = jnp.concatenate([inputs_low] + [m.chip_shift(inputs_low, j) for j in range(1, chips)], axis=0)
    theirs = m.swap(mine)
    *_, head_pieces = m.gather(head_piece, head_rows // 2 // 16 * 16)
    got = jnp.stack(head_pieces)
    passed = m.swap(got)
    query, key, value, head_weights, vec, bias_inner = simple_call(
        functools.partial(project_kernel, rows=rows_here, chips=chips, cols=cols, wide=wide),
        [struct((length, half))] * 3
        + [struct((3 * half, width)), struct((8, width), F32), struct((units, half), F32)],
        (got, passed, mine, theirs),
        (where,),
        "project",
        10,
        scratch=[pltpu.VMEM((wshard, head_rows, width), LOW), pltpu.SemaphoreType.DMA((2, wshard))],
        anywhere=2,
        limit=40,
    )

    rest_rows = wide + 5 * cols
    rest_cut = rest_rows // 2 // 16 * 16
    rest_piece = simple_call(
        functools.partial(pack_rest_kernel, shards=wshard),
        struct((rest_rows, half)),
        (w_inner, w_output.T, w_outer.T),
        (where,),
        "pack_rest",
        1,
    )
    rest_piece = after(rest_piece, passed, theirs)
    gather = m.gather(rest_piece, rest_cut)
    gathered = next(gather)

    chip, core = where[wshard + 1], where[wshard]
    random_own = lax.dynamic_slice(
        random_blocks,
        (chip * count, core * own_heads, 0),
        (count, own_heads, random_blocks.shape[2]),
        allow_negative_indices=False,
    )
    index, active = slot_lists(chip * count, count, nblocks, glob, random_own, own_heads)
    seg_rep = seg_all.reshape(nblocks, BLK)
    seg_rep = jnp.concatenate([seg_rep, seg_rep], axis=1)
    seg_rep = jnp.concatenate([seg_rep, jnp.full((8, 2 * BLK), -1, jnp.int32)], axis=0)
    scalars = (index.reshape(-1), active.reshape(-1), glob, where)
    seg_args = (seg_all[:, None], seg_rep, seg_all[None, :])
    done = []
    for pair in range(pairs):
        q = after(query, gathered[2 * pair]) if 0 < 2 * pair < len(gathered) else query
        done.append(attend(*scalars, q, key, value, *seg_args, count, own_heads, pair, wshard))
        if len(gathered) < wshard:
            gathered = gather.send(done[-1][4])
    while len(gathered) < wshard:
        gathered = next(gather)
    early, late = jnp.stack(gathered[:-3]), jnp.stack(gathered[-3:])
    rest = (early, late, m.swap(early), m.swap(late))
    attended_glob = jnp.concatenate([d[2] for d in done], axis=1)
    glob_rows = [attended_glob] + [m.chip_shift(attended_glob, j) for j in range(1, chips)]
    att_own, att_give = simple_call(
        functools.partial(merge_kernel, **sizes),
        [struct((rows_here, half))] * 2,
        tuple(d[0] for d in done) + tuple(glob_rows),
        (where, glob),
        "merge",
        1,
    )
    att_other = m.swap(att_give)

    big = lambda *shape: pltpu.VMEM(shape, F32)
    low = lambda *shape: pltpu.VMEM(shape, LOW)
    layer_output, resid_one, grad_own, grad_other, keep, give, vec_grad, inner_bias_grad = (
        simple_call(
            functools.partial(dense_kernel, wide=wide),
            [struct((rows_here, width), F32)] * 2
            + [struct((rows_here, half))] * 2
            + [struct((wshard, rest_rows, half))] * 2
            + [struct((8, width), F32), struct((units, half), F32)],
            rest + (att_own, att_other, tokens, out_grad[0], vec, bias_inner),
            (where,),
            "dense",
            40,
            scratch=[
                low(width, wide * wshard) if wide == half else low(16, 128),
                low(wshard, rest_rows - wide if wide == half else rest_rows, width),
                low(rows_here, width),
                low(rows_here, width),
                big(rows_here, width),
                big(rows_here, 1),
                low(units // 2, rows_here, width),
                low(units // 2, rows_here, width),
                big(rows_here, width),
                low(rows_here, width),
                low(2, units, half, half) if wide == half else low(1, 1, 16, 128),
                low(wshard, rest_rows - wide if wide == half else rest_rows, width),
                pltpu.SemaphoreType.DMA((2, 2, wshard)),
                pltpu.SemaphoreType.DMA((2 * (units + units // 2 + 1),)),
            ],
            anywhere=4,
            away=(4, 5),
            limit=60,
        )
    )

    from_other = m.swap(grad_other)
    given = m.swap(after(give, from_other))
    heads_grad, *glob_sends = simple_call(
        functools.partial(spread_kernel, **sizes),
        [struct((2 * rows_here, half))] + [struct((BLK, half))] * chips,
        (grad_own, from_other),
        (where, glob),
        "spread",
        1,
    )
    glob_grads = [glob_sends[0]] + [m.chip_shift(glob_sends[j], j) for j in range(1, chips)]

    def ring_of(arrays, cut, base):
        def step(kind, slots, received):
            return ring_step(where, arrays, [base + s for s in slots], received, kind, cut)

        return m.scatter(step, cut)

    ring = ring_of([keep, given], rest_cut, m.sums)
    turn = (next(ring),)
    pulled = []
    for pair in range(pairs):
        q = after(query, *turn)
        pulled.append(
            pull(*scalars, q, key, value, heads_grad, glob_grads, done[pair][1], done[pair][3], own_heads, pair, wshard)
        )
        turn = (next(ring),)
    grads = tuple(pulled[pair][t] for t in range(3) for pair in range(pairs))
    small_rows = -(-(3 * cols + small_least) // 16) * 16 - 3 * cols
    lane = [i % 48 for i in range(half)]
    layout = jnp.asarray(
        [[i % heads if i < 3 * heads else -1 for i in lane], [i // heads for i in lane], [i // 48 for i in range(half)]],
        jnp.int32,
    )
    layout = jnp.concatenate([layout, jnp.zeros((5, half), jnp.int32)], axis=0)
    head_keep, head_give, small_parts, part_mine, part_theirs = simple_call(
        functools.partial(head_grads_kernel, pairs=pairs, cols=cols, wide=wide, devices=devices, **sizes),
        [struct((wshard // 2, 3 * cols, half))] * 2
        + [struct((wshard, small_rows, half), F32)]
        + [struct((chips * rows_here, width))] * 2,
        after(grads, *turn) + tuple(d[4] for d in done) + (mine, theirs, head_weights, vec_grad, inner_bias_grad, layout),
        (where,),
        "head_grads",
        12,
        scratch=[big(8, width), low(wshard // 2, cols, width)],
        limit=48,
    )
    *_, total = ring
    head_give, part_theirs = after((head_give, part_theirs), total)
    head_given = m.swap(head_give)
    passed_theirs = m.swap(part_theirs)
    summed = part_mine.astype(F32) + passed_theirs.astype(F32)
    summed = summed.reshape(chips, rows_here, width)
    sent = [summed[j].astype(LOW) for j in range(1, chips)]
    input_grad = resid_one + summed[0]
    for j in range(1, chips):
        input_grad = input_grad + m.chip_shift(sent[j - 1], chips - j).astype(F32)

    head_parts = jnp.concatenate([head_keep, head_given], axis=0)
    head_parts = [after(head_parts, total, *sent)]

    def head_step(kind, slots, received):
        return head_ring_step(where, head_parts[0], small_parts, m, slots, received, kind)

    head_ring = m.scatter(head_step, None)
    for _ in range(3):
        next(head_ring)
    head_parts[0] = after(head_parts[0], input_grad)
    *_, head_tail = head_ring
    rest_tail = m.chip_sum(total)
    grad_inner, grad_output, grad_outer = simple_call(
        functools.partial(finish_rest_kernel, shards=wshard),
        [struct(w_inner.shape, F32), struct(w_output.shape[::-1], F32), struct(w_outer.shape[::-1], F32)],
        (rest_tail, m.swap(rest_tail)),
        (where,),
        "finish_rest",
        2,
    )
    head_tail = m.chip_sum(head_tail)
    vector, turned = struct((1, cols), F32), struct((cols, width), F32)
    finished = simple_call(
        functools.partial(finish_heads_kernel, shards=wshard, devices=devices, head_dim=head_dim),
        [turned] * 3 + [vector] * 8 + [struct((1, wide), F32), struct((1, heads), F32), turned, turned],
        (head_tail, m.swap(head_tail), thresholds[None], w_query.T, w_key.T),
        (where,),
        "finish_heads",
        2,
    )
    grad_query, grad_key, grad_value = finished[:3]
    vector_out = [v[0] for v in finished[3:11]]
    inner_out, maxima, clipped_query, clipped_key = finished[11][0], finished[12][0], finished[13], finished[14]

    return (
        layer_output[None],
        input_grad[None],
        grad_query.T,
        grad_key.T,
        grad_value.T,
        grad_output.T,
        grad_inner,
        grad_outer.T,
        vector_out[0],
        vector_out[1],
        vector_out[2],
        inner_out,
        vector_out[3],
        vector_out[4],
        vector_out[5],
        vector_out[6],
        vector_out[7],
        clipped_query.T,
        clipped_key.T,
        maxima,
    )


def head_ring_kernel(where, *refs, kind, targets, cut):
    refs = list(refs)
    parts = []
    for _ in range(targets):
        part, small = refs.pop(0), refs.pop(0)
        parts.append(jnp.concatenate([part[0].astype(F32), small[0]], axis=0))
    if kind == "first":
        up, down = refs
        up[...] = parts[0][:cut].astype(LOW)
        down[...] = parts[0][cut:].astype(LOW)
    elif kind == "second":
        above, below, up, down = refs
        up[:cut, :] = (parts[0][:cut] + above[...].astype(F32)).astype(LOW)
        up[cut:, :] = parts[0][cut:].astype(LOW)
        down[:cut, :] = parts[1][:cut].astype(LOW)
        down[cut:, :] = (parts[1][cut:] + below[...].astype(F32)).astype(LOW)
    elif kind == "later":
        above, below, up, down = refs
        up[...] = (parts[0] + above[...].astype(F32)).astype(LOW)
        down[...] = (parts[1] + below[...].astype(F32)).astype(LOW)
    else:
        above, below, out = refs
        out[...] = (parts[0] + above[...].astype(F32) + below[...].astype(F32)).astype(LOW)


def head_ring_step(where, parts, small, m, slots, received, kind):
    half = parts.shape[2]
    rows = parts.shape[1] + small.shape[1]
    cut = rows // 2 // 16 * 16
    specs, args = [], []
    for slot in slots:
        specs.append(
            pl.BlockSpec((1,) + parts.shape[1:], lambda i, where, at=m.placed + slot: (where[at], 0, 0))
        )
        specs.append(pl.BlockSpec((1,) + small.shape[1:], lambda i, where, at=m.sums + slot: (where[at], 0, 0)))
        args += [parts, small]
    specs += [pl.BlockSpec(a.shape, lambda i, where: (0, 0)) for a in received]
    shapes = [(rows, half)] if kind == "last" else [(rows, half)] * 2
    if kind == "first":
        shapes = [(cut, half), (rows - cut, half)]
    return pl.pallas_call(
        functools.partial(head_ring_kernel, kind=kind, targets=len(slots), cut=cut),
        grid_spec=pltpu.PrefetchScalarGridSpec(
            num_scalar_prefetch=1,
            grid=(1,),
            in_specs=specs,
            out_specs=[pl.BlockSpec(s, lambda i, where: (0, 0)) for s in shapes],
        ),
        out_shape=[struct(s) for s in shapes],
        compiler_params=pltpu.CompilerParams(vmem_limit_bytes=32 << 20),
        cost_estimate=pl.CostEstimate(flops=10**9, bytes_accessed=3 << 20, transcendentals=0),
        name="head_ring_" + kind,
    )(where, *args, *received)


def solution(mesh):
    tokens = P("wshard", "ctx", None)
    sequence = P("wshard", None)
    matrix = P(None, "wshard")
    vector = P("wshard")
    in_specs = (tokens, sequence, sequence, P(), P()) + (matrix,) * 6 + (vector,) * 9 + (tokens,)
    out_specs = (tokens, tokens) + (matrix,) * 6 + (vector,) * 9 + (matrix, matrix, P())
    return jax.shard_map(
        functools.partial(per_device, mesh.shape["ctx"], mesh.shape["wshard"]),
        mesh=mesh,
        in_specs=in_specs,
        out_specs=out_specs,
        check_vma=False,
    )
```
